32 devices in a mesh: ctx: 8 (over z, x), cls: 4 (over y, core).
Axes of the slice: x: 2, y: 2, z: 4, core: 2. Of those that a mesh axis runs over, the one named last changes fastest.
Arguments:
- tokens: bfloat16 [24576, 8192], P(('ctx', 'cls')), may hold values from -80 to 80
- doc_length: int32 [1], replicated, may hold values from 12288 to 24576
- queries: bfloat16 [64, 8192], P('cls', 'ctx'), may hold values from -0.046875 to 0.046875
- norm_gain: float32 [8192], P('ctx'), may hold values from 0.1 to 1.9
- head_weight: bfloat16 [8192, 4096], P('ctx', 'cls'), may hold values from -0.0625 to 0.0625
- head_bias: float32 [4096], P('cls'), may hold values from -20 to 20
- labels: int32 [4096], P('cls'), may hold values 0 or 1
Outputs:
- mean_loss: float32 [], replicated
- query_grad: float32 [64, 8192], P('cls', 'ctx')
- head_grad: float32 [8192, 4096], P('ctx', 'cls')
- bias_grad: float32 [4096], P('cls')
The draws below stay inside these ranges and needn't reach their ends.
All inputs are finite; a program needn't handle non-finite values. No bound on the sum of `labels` on one device may be relied on, other than what follows from the above.
Results may differ from the reference program's by a relative error of at most 0.017.
Values may be sent and summed in bfloat16 or wider, within the bound.
No kernel may reach another device: no remote copies, remote signals or barrier semaphores. Data moves between devices by JAX's collectives and lax.ppermute only.
A program may use at most 64 MiB of HBM per device.

```python
import math
import jax
import jax.numpy as jnp
from jax import lax

D = 8192
H = 64
A = 4096
AQ = 64
TOKENS = 24576
N_CTX = 8


def draw_tokens(key, part):
    row_key, col_key, noise_key = jax.random.split(jax.random.fold_in(key, 5), 3)
    row_scale = jnp.exp(jax.random.uniform(row_key, (TOKENS, 1), jnp.float32, math.log(0.3), math.log(3.0)))
    col_noise = jnp.exp(jax.random.uniform(col_key, (1, D), jnp.float32, math.log(0.5), math.log(1.5)))
    column_pos = jnp.arange(D, dtype=jnp.float32)[None, :] / D
    col_scale = col_noise * jnp.exp(math.log(3.0) * column_pos)
    base_noise = jnp.clip(jax.random.normal(noise_key, (TOKENS, D), jnp.float32), -5.0, 5.0)
    values = base_noise * row_scale * col_scale
    return values.astype(jnp.bfloat16)


def draw_queries(key, part):
    noise_key = jax.random.fold_in(key, 17)
    spread = 0.25 / math.sqrt(D)
    values = jnp.clip(jax.random.normal(noise_key, (H, D), jnp.float32), -5.0, 5.0) * spread
    return values.astype(jnp.bfloat16)


def draw_head_bias(key, part):
    noise_key = jax.random.fold_in(key, 29)
    position = jnp.arange(A, dtype=jnp.float32) / A
    scale = 0.4 * jnp.exp(math.log(10.0) * position)
    values = jnp.clip(jax.random.normal(noise_key, (A,), jnp.float32), -4.0, 4.0) * scale
    return values.astype(jnp.float32)


def with_ends(values, own_key, smallest, top_value):
    extent = values.shape
    place = [jax.random.randint(jax.random.fold_in(own_key, axis), (), 0, extent[axis]) for axis in range(len(extent))]
    values = values.at[tuple(place)].set(smallest)
    longest = extent.index(max(extent))
    place[longest] = (place[longest] + 1) % extent[longest]
    return values.at[tuple(place)].set(top_value)


def block_scale(rng, dims, shards, smallest, largest):
    level, own = 1.0, jax.random.fold_in(rng, 6)
    for axis_at, blocks in shards:
        draws = jnp.exp(jax.random.uniform(jax.random.fold_in(own, axis_at), (blocks,), jnp.float32, smallest / len(shards), largest / len(shards)))
        level = level * jnp.repeat(draws, dims[axis_at] // blocks).reshape([-1 if axis == axis_at else 1 for axis in range(len(dims))])
    return level


def gaussian(own_key, extent, scale, reach, pieces=(), held_as=jnp.bfloat16):
    entries = scale * jax.random.normal(own_key, extent, jnp.float32)
    if pieces:
        entries = entries * block_scale(own_key, extent, pieces, -0.22, 0.18)
    return jnp.clip(entries, -reach, reach).astype(held_as)


def setup_inputs(seed: int = 0) -> dict:
    arg_keys = jax.random.split(jax.random.key(seed), 8)
    tokens = draw_tokens(jax.random.fold_in(arg_keys[7], 71), 0)
    doc_length = jax.random.randint(arg_keys[1], (1,), TOKENS // 2, TOKENS + 1).astype(jnp.int32)
    queries = draw_queries(jax.random.fold_in(arg_keys[7], 71), 0)
    norm_gain = jnp.clip(1.0 + 0.18 * jax.random.normal(arg_keys[3], (D,), jnp.float32), 0.1, 1.9)
    head_weight = gaussian(arg_keys[4], (D, A), D ** -0.5, 0.0625, ((0, 8), (1, 4)))
    head_bias = draw_head_bias(jax.random.fold_in(arg_keys[7], 71), 0)
    labels = with_ends((jax.random.randint(arg_keys[6], (A,), 0, 2) < 1).astype(jnp.int32), jax.random.fold_in(arg_keys[6], 1), 0, 1)
    return dict(tokens=tokens, doc_length=doc_length, queries=queries, norm_gain=norm_gain, head_weight=head_weight, head_bias=head_bias, labels=labels)


def reference(tokens, doc_length, queries, norm_gain, head_weight, head_bias, labels):
    block_count = N_CTX
    block_rows = TOKENS // block_count
    token_blocks = tokens.reshape(block_count, block_rows, D)

    def score_block(carry, block):
        return (carry, jnp.dot(queries, block.T, preferred_element_type=jnp.float32))
    _, scores = lax.scan(score_block, 0, token_blocks)
    position = (jnp.arange(block_count, dtype=jnp.int32)[:, None] * block_rows + jnp.arange(block_rows, dtype=jnp.int32)[None, :]).astype(jnp.int32)
    valid_mask = (position < doc_length[0])[:, None, :]
    peak = lax.optimization_barrier(jnp.max(jnp.where(valid_mask, scores, -1e+30), axis=(0, 2)))
    weights = jnp.exp(jnp.where(valid_mask, scores - peak[None, :, None], -1e+30))
    weights_b = weights.astype(jnp.bfloat16)

    def pool_block(running, pair):
        return (running + jnp.dot(pair[0], pair[1], preferred_element_type=jnp.float32), 0)
    pooled, _ = lax.scan(pool_block, jnp.zeros((H, D), jnp.float32), (weights_b, token_blocks))
    inverse_rms = lax.rsqrt(lax.optimization_barrier(jnp.sum(pooled * pooled, axis=1)) / D + 1e-05)
    scaled_b = (pooled * norm_gain[None, :]).astype(jnp.bfloat16)
    head_blocks = head_weight.reshape(D, H, AQ).astype(jnp.float32)
    logit_raw = jnp.einsum('hd,dha->ha', scaled_b.astype(jnp.float32), head_blocks, precision=lax.Precision.HIGHEST)
    logits = inverse_rms[:, None] * logit_raw + head_bias.reshape(H, AQ)
    target = labels.reshape(H, AQ).astype(jnp.float32)
    mean_loss = jnp.sum(jax.nn.softplus(logits) - target * logits) / A
    logit_grad = jax.nn.sigmoid(logits) - target
    normed = pooled * inverse_rms[:, None] * norm_gain[None, :]
    head_grad = jnp.einsum('hd,ha->dha', normed, logit_grad, precision=lax.Precision.HIGHEST).reshape(D, A)
    normed_grad = jnp.einsum('dha,ha->hd', head_blocks, logit_grad, precision=lax.Precision.HIGHEST) * norm_gain[None, :]
    unit_pooled = pooled * inverse_rms[:, None]
    inner_mean = lax.optimization_barrier(jnp.sum(unit_pooled * normed_grad, axis=1)) / D
    pooled_grad = (inverse_rms[:, None] * (normed_grad - unit_pooled * inner_mean[:, None])).astype(jnp.bfloat16)

    def grad_block(running, pair):
        projected = jnp.dot(pooled_grad, pair[1].T, preferred_element_type=jnp.float32)
        score_grad = (pair[0] * projected).astype(jnp.bfloat16)
        return (running + jnp.dot(score_grad, pair[1], preferred_element_type=jnp.float32), 0)
    query_grad, _ = lax.scan(grad_block, jnp.zeros((H, D), jnp.float32), (weights, token_blocks))
    return (mean_loss, query_grad, head_grad, logit_grad.reshape(A))
```

```python
import functools

import jax
import jax.numpy as jnp
from jax import lax
from jax.experimental import pallas as pl
from jax.experimental.pallas import tpu as pltpu
from jax.sharding import PartitionSpec as P

F32 = jnp.float32
BF16 = jnp.bfloat16
LANES = 128
MASKED = -1e30
VMEM_LIMIT = 48 * 1024 * 1024


def bits(count):
    return [1 << b for b in reversed(range(count.bit_length() - 1))]


def swap(x, axis, bit):
    count = lax.axis_size(axis)
    return lax.ppermute(x, axis, [(i, i ^ bit) for i in range(count)])


def gather(block):
    held = block[None]
    for bit in bits(lax.axis_size("ctx")):
        held = jnp.concatenate([held, swap(held, "ctx", bit)], axis=0)
    for bit in bits(lax.axis_size("cls")):
        held = jnp.concatenate([held, swap(held, "cls", bit)], axis=1)
    return held


def relative_blocks(count):
    order = [0]
    for bit in bits(count):
        order = order + [o ^ bit for o in order]
    return order


def vmem_call(kernel, outs, name, scratch=(), any_args=(), smem_args=(), flops=0, count=0):
    def spec(i):
        if i in any_args:
            return pl.BlockSpec(memory_space=pl.ANY)
        if i in smem_args:
            return pl.BlockSpec(memory_space=pltpu.SMEM)
        return pl.BlockSpec(memory_space=pltpu.VMEM)

    return pl.pallas_call(
        kernel,
        out_shape=[jax.ShapeDtypeStruct(s, d) for s, d in outs],
        in_specs=[spec(i) for i in range(count)],
        out_specs=[pl.BlockSpec(memory_space=pltpu.VMEM)] * len(outs),
        scratch_shapes=list(scratch),
        compiler_params=pltpu.CompilerParams(vmem_limit_bytes=VMEM_LIMIT),
        name=name,
    )


def start_tokens(order_ref, tokens_ref, held, sems, width):
    copies = []
    for p in range(held.shape[0]):
        at = pl.multiple_of(order_ref[p] * width, LANES)
        copy = pltpu.make_async_copy(tokens_ref.at[:, pl.ds(at, width)], held.at[p], sems.at[p])
        copy.start()
        copies.append(copy)
    return copies


def project(copies, block_ref, held):
    total = None
    for p, copy in enumerate(copies):
        copy.wait()
        part = lax.dot_general(
            block_ref[p], held[p], (((1,), (1,)), ((), ())), preferred_element_type=F32
        )
        total = part if total is None else total + part
    return total


def spread(left, held, keep_ref, send_ref):
    half = keep_ref.shape[1]
    for p in range(held.shape[0]):
        part = jnp.dot(left, held[p], preferred_element_type=F32)
        keep_ref[p] = part[:half]
        send_ref[p] = part[half:].astype(send_ref.dtype)


def pool_kernel(order_ref, count_ref, q_ref, tokens_ref, keep_ref, send_ref, peak_ref, w_ref, held, sems):
    copies = start_tokens(order_ref, tokens_ref, held, sems, q_ref.shape[2])
    scores = project(copies, q_ref, held)
    valid = lax.broadcasted_iota(jnp.int32, scores.shape, 1) < count_ref[0]
    peak = jnp.max(jnp.where(valid, scores, MASKED), axis=1, keepdims=True)
    weights = jnp.where(valid, jnp.exp(scores - peak), 0.0)
    w_ref[...] = weights
    peak_ref[...] = jnp.broadcast_to(peak, peak_ref.shape)
    spread(weights.astype(BF16), held, keep_ref, send_ref)


def grad_kernel(order_ref, g_ref, tokens_ref, w_ref, peak_ref, top_ref, keep_ref, send_ref, held, sems):
    copies = start_tokens(order_ref, tokens_ref, held, sems, g_ref.shape[2])
    projected = project(copies, g_ref, held)
    weights = w_ref[...] * jnp.exp(peak_ref[:, :1] - top_ref[:, :1])
    spread((weights * projected).astype(BF16), held, keep_ref, send_ref)


def combine_peaks_kernel(axis, keep_ref, recv_ref, mine_ref, other_ref, *outs):
    mine, other = mine_ref[...], other_ref[...]
    top = jnp.maximum(mine, other)
    scale_mine = jnp.exp(mine - top)[:, :1]
    scale_other = jnp.exp(other - top)[:, :1]
    outs[-1][...] = top
    for p in range(keep_ref.shape[0]):
        total = keep_ref[p] * scale_mine + recv_ref[p].astype(F32) * scale_other
        store_half(axis, p, total, outs[:-1])


def combine_kernel(axis, keep_ref, recv_ref, *outs):
    for p in range(keep_ref.shape[0]):
        store_half(axis, p, keep_ref[p] + recv_ref[p].astype(F32), outs)


def store_half(axis, p, total, outs):
    keep_ref = outs[0]
    if len(outs) == 1:
        keep_ref[p] = total
    elif axis == "cls":
        half = keep_ref.shape[1]
        keep_ref[p] = total[:half]
        outs[1][p] = total[half:].astype(BF16)
    elif p < keep_ref.shape[0]:
        keep_ref[p] = total
    else:
        outs[1][p - keep_ref.shape[0]] = total.astype(BF16)


def scatter_sum(keep, send, peak):
    steps = [("ctx", b) for b in bits(lax.axis_size("ctx"))] + [("cls", b) for b in bits(lax.axis_size("cls"))]
    steps = steps[::-1]
    for i, (axis, bit) in enumerate(steps):
        recv = swap(send, axis, bit)
        blocks, rows, width = keep.shape
        following = steps[i + 1][0] if i + 1 < len(steps) else None
        if following is None:
            outs = [((blocks, rows, width), F32)]
        else:
            shape = (blocks, rows // 2, width) if following == "cls" else (blocks // 2, rows, width)
            outs = [(shape, F32), (shape, BF16)]
        if peak is None:
            out = vmem_call(functools.partial(combine_kernel, following), outs, "combine", count=2)(keep, recv)
        else:
            if axis == "cls":
                mine, other = peak[:rows], swap(peak[rows:], axis, bit)
            else:
                mine, other = peak, swap(peak, axis, bit)
            *out, peak = vmem_call(
                functools.partial(combine_peaks_kernel, following), outs + [(mine.shape, F32)], "combine_peaks", count=4
            )(keep, recv, mine, other)
        keep, send = out if following is not None else (out[0], None)
    return keep[0], peak


def head_mask(shape, attributes):
    row = lax.broadcasted_iota(jnp.int32, shape, 0)
    column = lax.broadcasted_iota(jnp.int32, shape, 1)
    return column // attributes == row


def head_sums_kernel(pooled_ref, gain_ref, weight_ref, sums_ref):
    pooled = pooled_ref[...]
    scaled_b = (pooled * gain_ref[...]).astype(BF16)
    product = jnp.dot(scaled_b, weight_ref[...], preferred_element_type=F32)
    mask = head_mask(product.shape, product.shape[1] // product.shape[0])
    squares = jnp.sum(pooled * pooled, axis=1, keepdims=True)
    sums_ref[0:1, :] = jnp.sum(jnp.where(mask, product, 0.0), axis=0, keepdims=True)
    sums_ref[1:2, :] = jnp.sum(jnp.where(mask, squares, 0.0), axis=0, keepdims=True)


def head_grads_kernel(
    full_width, sums_ref, pooled_ref, gain_ref, weight_ref, bias_ref, label_ref, bias_grad_ref, loss_ref, grad_ref, normed_ref
):
    pooled, gain = pooled_ref[...], gain_ref[...]
    heads, columns = pooled.shape[0], sums_ref.shape[1]
    mask = head_mask((heads, columns), columns // heads)
    inverse_flat = lax.rsqrt(sums_ref[1:2, :] / full_width + 1e-05)
    inverse_rms = jnp.max(jnp.where(mask, inverse_flat, 0.0), axis=1, keepdims=True)
    product = inverse_flat * sums_ref[0:1, :]
    logits = product + bias_ref[...]
    target = label_ref[...].astype(F32)
    loss = jnp.maximum(logits, 0.0) + jnp.log1p(jnp.exp(-jnp.abs(logits))) - target * logits
    loss_ref[...] = jnp.broadcast_to(jnp.sum(loss, axis=1, keepdims=True), loss_ref.shape)
    bias_grad = jax.nn.sigmoid(logits) - target
    bias_grad_ref[...] = bias_grad
    by_head = jnp.where(mask, bias_grad, 0.0)
    high = by_head.astype(BF16)
    low = (by_head - high.astype(F32)).astype(BF16)
    both = jnp.concatenate([high, low], axis=0)
    back = lax.dot_general(both, weight_ref[...], (((1,), (1,)), ((), ())), preferred_element_type=F32)
    normed_grad = (back[:heads] + back[heads:]) * gain
    inner = jnp.sum(by_head * product, axis=1, keepdims=True) / full_width
    unit = pooled * inverse_rms
    grad_ref[...] = (inverse_rms * (normed_grad - unit * inner)).astype(BF16)
    normed_ref[...] = unit * gain


def shards(tokens, doc_length, queries, norm_gain, head_weight, head_bias, labels):
    context_count = lax.axis_size("ctx")
    class_count = lax.axis_size("cls")
    context_index = lax.axis_index("ctx")
    class_index = lax.axis_index("cls")
    token_count = tokens.shape[0]
    rows, width = queries.shape
    full_width = width * context_count
    heads = rows * class_count
    columns = labels.shape[0]
    order = context_index ^ jnp.array(relative_blocks(context_count), jnp.int32)
    offset = (context_index * class_count + class_index) * token_count
    valid_count = jnp.clip(doc_length - offset, 0, token_count)
    half = ((context_count, heads // 2, width), F32), ((context_count, heads // 2, width), BF16)
    tokens_scratch = (pltpu.VMEM((context_count, token_count, width), BF16), pltpu.SemaphoreType.DMA((context_count,)))

    query_blocks = gather(queries)
    keep, send, own_peak, weights = vmem_call(
        pool_kernel,
        [*half, ((heads, LANES), F32), ((heads, token_count), F32)],
        "pool",
        tokens_scratch,
        any_args=(3,),
        smem_args=(0, 1),
        count=4,
    )(order, valid_count, query_blocks, tokens)
    pooled, peak = scatter_sum(keep, send, own_peak)
    top = peak
    for bit in bits(class_count):
        top = jnp.concatenate([top, swap(top, "cls", bit)], axis=0)

    gain = norm_gain[None, :]
    (sums,) = vmem_call(head_sums_kernel, [((2, columns), F32)], "head_sums", count=3)(pooled, gain, head_weight)
    for bit in bits(context_count):
        sums = sums + swap(sums, "ctx", bit)
    bias_grad, loss, pooled_grad, normed = vmem_call(
        functools.partial(head_grads_kernel, full_width),
        [((1, columns), F32), ((1, LANES), F32), ((rows, width), BF16), ((rows, width), F32)],
        "head_grads",
        count=6,
    )(sums, pooled, gain, head_weight, head_bias[None, :], labels[None, :])

    grad_blocks = gather(pooled_grad)
    keep, send = vmem_call(
        grad_kernel, half, "grad", tokens_scratch, any_args=(2,), smem_args=(0,), count=6
    )(order, grad_blocks, tokens, weights, own_peak, top)
    query_grad, _ = scatter_sum(keep, send, None)

    for bit in bits(class_count):
        loss = loss + swap(loss, "cls", bit)
    mean_loss = loss[0, 0] / (columns * class_count)
    bias_rows = bias_grad.reshape(rows, -1)
    head_grad = (normed.T[:, :, None] * bias_rows[None]).reshape(width, columns)
    return (mean_loss, query_grad, head_grad, bias_grad.reshape(-1))


def solution(mesh):
    return jax.shard_map(
        shards,
        mesh=mesh,
        in_specs=(
            P(("ctx", "cls"), None),
            P(),
            P("cls", "ctx"),
            P("ctx"),
            P("ctx", "cls"),
            P("cls"),
            P("cls"),
        ),
        out_specs=(P(), P("cls", "ctx"), P("ctx", "cls"), P("cls")),
        check_vma=False,
    )
```

```python
import functools

import jax
import jax.numpy as jnp
from jax import lax
from jax.experimental import pallas as pl
from jax.experimental.pallas import tpu as pltpu
from jax.sharding import PartitionSpec as P

F32 = jnp.float32
BF16 = jnp.bfloat16
LANES = 128
MASKED = -1e30
MIB = 1024 * 1024


def swap(x, ctx_bits, cls_bits):
    contexts, classes = lax.axis_size("ctx"), lax.axis_size("cls")
    pairs = [
        (c * classes + k, (c ^ ctx_bits) * classes + (k ^ cls_bits)) for c in range(contexts) for k in range(classes)
    ]
    return lax.ppermute(x, ("ctx", "cls"), pairs)


def far_steps():
    return [(2 * j, 0) for j in range(1, lax.axis_size("ctx") // 2)]


def near_steps():
    return [(i, 2 * k) for i in range(2) for k in range(lax.axis_size("cls") // 2) if i or k]


def relative_blocks(contexts):
    return [i ^ (2 * j) for i in range(2) for j in range(contexts // 2)]


def call(kernel, outs, name, args, scratch=(), any_args=(), smem_args=(), limit=16, cost=None):
    def spec(i):
        if i in any_args:
            return pl.BlockSpec(memory_space=pl.ANY)
        if i in smem_args:
            return pl.BlockSpec(memory_space=pltpu.SMEM)
        return pl.BlockSpec(memory_space=pltpu.VMEM)

    run = pl.pallas_call(
        kernel,
        out_shape=[jax.ShapeDtypeStruct(s, d) for s, d in outs],
        in_specs=[spec(i) for i in range(len(args))],
        out_specs=[pl.BlockSpec(memory_space=pltpu.VMEM)] * len(outs),
        scratch_shapes=list(scratch),
        compiler_params=pltpu.CompilerParams(vmem_limit_bytes=limit * MIB),
        cost_estimate=cost,
        name=name,
    )
    return list(run(*args))


def stack_kernel(axis, *refs):
    out_ref, at = refs[-1], 0
    for ref in refs[:-1]:
        size = ref.shape[axis]
        if axis == 0:
            out_ref[at : at + size] = ref[...]
        else:
            out_ref[:, at : at + size] = ref[...]
        at += size


def stack(parts, axis):
    shape = list(parts[0].shape)
    shape[axis] = sum(p.shape[axis] for p in parts)
    (out,) = call(functools.partial(stack_kernel, axis), [(tuple(shape), parts[0].dtype)], "stack", parts)
    return out


def near_kernel(*refs):
    out_ref, parts = refs[-1], refs[:-1]
    blocks, rows, _ = parts[0].shape
    across = len(parts) // 2
    for i in range(2):
        for k in range(across):
            out_ref[i * blocks : (i + 1) * blocks, k * rows : (k + 1) * rows] = parts[i * across + k][...]


def gather(block):
    block = block[None]
    held = stack([block] + [swap(block, *step) for step in far_steps()], 0)
    parts = [held] + [swap(held, *step) for step in near_steps()]
    blocks, rows, width = held.shape
    (held,) = call(near_kernel, [((2 * blocks, len(parts) // 2 * rows, width), held.dtype)], "near", parts)
    return held, swap(held, 0, 1)


def pieces(x):
    high = x.astype(BF16)
    rest = x - high.astype(F32)
    middle = rest.astype(BF16)
    return high, middle, (rest - middle.astype(F32)).astype(BF16)


def into_lanes(columns, rows):
    lane = lax.broadcasted_iota(jnp.int32, (rows, LANES), 1)
    out = jnp.zeros((rows, LANES), F32)
    for i, column in enumerate(columns):
        for j, piece in enumerate(pieces(column)):
            out = jnp.where(lane == 3 * i + j, piece.astype(F32), out)
    return out.astype(BF16)


def from_lanes(block, width, i):
    at = width + 3 * i
    block = block.astype(F32)
    return block[:, at : at + 1] + (block[:, at + 1 : at + 2] + block[:, at + 2 : at + 3])


def columns_of(context_ref, contexts, p, width):
    return pl.ds(pl.multiple_of((context_ref[0] ^ relative_blocks(contexts)[p]) * width, LANES), width)


def project(context_ref, own_ref, other_ref, tokens_ref, width):
    contexts = own_ref.shape[0]
    total = None
    for p in range(contexts):
        both = jnp.concatenate([own_ref[p], other_ref[p]], axis=0)[:, :width]
        block = tokens_ref[:, columns_of(context_ref, contexts, p, width)]
        part = lax.dot_general(block, both, (((1,), (1,)), ((), ())), preferred_element_type=F32)
        total = part if total is None else total + part
    return total.T


def spread(context_ref, left, tokens_ref, keep_ref, send_ref, extra):
    contexts, half, width = keep_ref.shape
    for p in range(contexts):
        block = tokens_ref[:, columns_of(context_ref, contexts, p, width)]
        part = jnp.dot(left, block, preferred_element_type=F32)
        keep_ref[p] = part[:half]
        send_ref[p, :, :width] = part[half:].astype(BF16)
        if extra is not None:
            send_ref[p, :, width:] = extra


def pool_kernel(context_ref, count_ref, own_ref, other_ref, tokens_ref, keep_ref, send_ref, peak_ref, w_ref):
    scores = project(context_ref, own_ref, other_ref, tokens_ref, keep_ref.shape[2])
    valid = lax.broadcasted_iota(jnp.int32, scores.shape, 1) < count_ref[0]
    peak = jnp.max(jnp.where(valid, scores, MASKED), axis=1, keepdims=True)
    weights = jnp.where(valid, jnp.exp(scores - peak), 0.0)
    w_ref[...] = weights
    peak_ref[...] = jnp.broadcast_to(peak, peak_ref.shape)
    half = keep_ref.shape[1]
    spread(context_ref, weights.astype(BF16), tokens_ref, keep_ref, send_ref, into_lanes([peak[half:]], half))


def grad_kernel(scale, context_ref, own_ref, other_ref, tokens_ref, w_ref, peak_ref, keep_ref, send_ref, loss_ref):
    width = keep_ref.shape[2]
    projected = project(context_ref, own_ref, other_ref, tokens_ref, width)
    own, other = own_ref[0], other_ref[0]
    top = jnp.concatenate([from_lanes(own, width, 0), from_lanes(other, width, 0)], axis=0)
    weights = w_ref[...] * jnp.exp(peak_ref[:, :1] - top)
    spread(context_ref, (weights * projected).astype(BF16), tokens_ref, keep_ref, send_ref, None)
    rows = loss_ref.shape[0] // 2
    each = own.shape[0] // rows
    sums = []
    for block in (own, other):
        column = from_lanes(block, width, 1)
        level = [column[i * each : i * each + 1] for i in range(rows)]
        while len(level) > 1:
            level = [a + b for a, b in zip(level[::2], level[1::2])]
        sums.append(level[0])
    loss_ref[...] = jnp.broadcast_to((sums[0] + sums[1]) * scale, loss_ref.shape)


def total_of(keep, peak, received, width):
    if peak is None:
        for block in received:
            keep = keep + block.astype(F32)
        return keep, None
    others = [from_lanes(block, width, 0) for block in received]
    top = peak
    for other in others:
        top = jnp.maximum(top, other)
    keep = keep * jnp.exp(peak - top)
    for block, other in zip(received, others):
        keep = keep + block[:, :width].astype(F32) * jnp.exp(other - top)
    return keep, top


def put(ref, p, total, top, width):
    ref[p, :, :width] = total.astype(BF16)
    if top is not None:
        ref[p, :, width:] = into_lanes([top], total.shape[0])


def core_kernel(peaks, across, *refs):
    keep_ref, recv_ref, *refs = refs
    peak = refs.pop(0)[: keep_ref.shape[1], :1] if peaks else None
    top_ref = refs.pop() if peaks else None
    width = keep_ref.shape[2]
    blocks, rows = refs[0].shape[:2]
    for i in range(2):
        for b in range(blocks):
            p = i * blocks + b
            total, top = total_of(keep_ref[p], peak, [recv_ref[p]], width)
            for k in range(across):
                part = total[k * rows : (k + 1) * rows]
                part_top = top[k * rows : (k + 1) * rows] if peaks else None
                if i == 0 and k == 0:
                    refs[0][b] = part
                else:
                    put(refs[i * across + k], b, part, part_top, width)
    if peaks:
        top_ref[...] = jnp.broadcast_to(top[:rows], top_ref.shape)


def near_sum_kernel(peaks, count, *refs):
    keep_ref, *refs = refs
    received, refs = refs[:count], list(refs[count:])
    peak = refs.pop(0)[:, :1] if peaks else None
    top_ref = refs.pop() if peaks else None
    width = keep_ref.shape[2]
    for p in range(keep_ref.shape[0]):
        total, top = total_of(keep_ref[p], peak, [ref[p] for ref in received], width)
        if p == 0:
            refs[0][0] = total
        else:
            put(refs[p], 0, total, top, width)
    if peaks:
        top_ref[...] = jnp.broadcast_to(top, top_ref.shape)


def scatter_sum(keep, send, peak):
    peaks = peak is not None
    contexts, half, width = keep.shape
    lanes = send.shape[2]
    near, far = near_steps(), far_steps()
    across = (len(near) + 1) // 2
    blocks, rows = contexts // 2, half // across
    top_out = [((rows, LANES), F32)] if peaks else []
    outs = [((blocks, rows, width), F32)] + [((blocks, rows, lanes), BF16)] * len(near) + top_out
    args = [keep, swap(send, 0, 1)] + ([peak] if peaks else [])
    out = call(functools.partial(core_kernel, peaks, across), outs, "core_sum", args)
    received = [swap(s, *step) for s, step in zip(out[1:], near)]
    outs = [((1, rows, width), F32)] + [((1, rows, lanes), BF16)] * len(far) + top_out
    args = [out[0], *received] + (out[-1:] if peaks else [])
    out = call(functools.partial(near_sum_kernel, peaks, len(received)), outs, "near_sum", args)
    received = [swap(s, *step) for s, step in zip(out[1:], far)]
    return [out[0], *received] + (out[-1:] if peaks else [])


def far_sum_kernel(*refs):
    keep_ref, *received, out_ref = refs
    out_ref[...] = total_of(keep_ref[0], None, [ref[0] for ref in received], keep_ref.shape[2])[0]


def head_mask(shape, attributes):
    row = lax.broadcasted_iota(jnp.int32, shape, 0)
    column = lax.broadcasted_iota(jnp.int32, shape, 1)
    return column // attributes == row


def head_sums_kernel(*refs):
    keep_ref, *received, peak_ref, gain_ref, weight_ref, sums_ref, pooled_ref, top_ref = refs
    pooled, top = total_of(keep_ref[0], peak_ref[:, :1], [ref[0] for ref in received], keep_ref.shape[2])
    pooled_ref[...] = pooled
    top_ref[...] = jnp.broadcast_to(top, top_ref.shape)
    scaled_b = (pooled * gain_ref[...]).astype(BF16)
    product = jnp.dot(scaled_b, weight_ref[...], preferred_element_type=F32)
    mask = head_mask(product.shape, product.shape[1] // product.shape[0])
    squares = jnp.sum(pooled * pooled, axis=1, keepdims=True)
    product_flat = jnp.sum(jnp.where(mask, product, 0.0), axis=0, keepdims=True)
    squares_flat = jnp.sum(jnp.where(mask, squares, 0.0), axis=0, keepdims=True)
    for p in range(sums_ref.shape[0]):
        sums_ref[p, 0:1, :] = product_flat
        sums_ref[p, 1:2, :] = squares_flat


def head_grads_kernel(
    full_width, sums_ref, pooled_ref, top_ref, gain_ref, weight_ref, bias_ref, label_ref, bias_grad_ref, grad_ref, normed_ref
):
    pooled, gain = pooled_ref[...], gain_ref[...]
    heads, width = pooled.shape
    columns = sums_ref.shape[2]
    sums = sums_ref[0]
    for p in range(1, sums_ref.shape[0]):
        sums = sums + sums_ref[p]
    mask = head_mask((heads, columns), columns // heads)
    inverse_flat = lax.rsqrt(sums[1:2] / full_width + 1e-05)
    inverse_rms = jnp.max(jnp.where(mask, inverse_flat, 0.0), axis=1, keepdims=True)
    product = inverse_flat * sums[0:1]
    logits = product + bias_ref[...]
    target = label_ref[...].astype(F32)
    losses = jnp.maximum(logits, 0.0) + jnp.log1p(jnp.exp(-jnp.abs(logits))) - target * logits
    loss = jnp.sum(losses, axis=1, keepdims=True)
    bias_grad = jax.nn.sigmoid(logits) - target
    bias_grad_ref[...] = bias_grad
    by_head = jnp.where(mask, bias_grad, 0.0)
    high = by_head.astype(BF16)
    low = (by_head - high.astype(F32)).astype(BF16)
    both = jnp.concatenate([high, low], axis=0)
    back = lax.dot_general(both, weight_ref[...], (((1,), (1,)), ((), ())), preferred_element_type=F32)
    normed_grad = (back[:heads] + back[heads:]) * gain
    inner = jnp.sum(by_head * product, axis=1, keepdims=True) / full_width
    unit = pooled * inverse_rms
    grad_ref[:, :width] = (inverse_rms * (normed_grad - unit * inner)).astype(BF16)
    grad_ref[:, width:] = into_lanes([top_ref[:, :1], jnp.broadcast_to(loss, (heads, 1))], heads)
    normed_ref[...] = unit * gain


def head_weight_grad_kernel(attributes, normed_ref, bias_grad_ref, out_ref):
    heads = normed_ref.shape[0]
    columns = out_ref.shape[1]
    parts = jnp.concatenate(pieces(normed_ref[...]), axis=0)
    row = lax.broadcasted_iota(jnp.int32, (3 * heads, columns), 0) % heads
    column = pl.program_id(0) * columns + lax.broadcasted_iota(jnp.int32, (3 * heads, columns), 1)
    ones = jnp.where(column // attributes == row, 1.0, 0.0).astype(BF16)
    normed = lax.dot_general(parts, ones, (((0,), (0,)), ((), ())), preferred_element_type=F32)
    out_ref[...] = normed * bias_grad_ref[...]


def head_weight_grad(normed, bias_grad):
    rows, width = normed.shape
    columns = bias_grad.shape[1]
    block = columns // 4
    return pl.pallas_call(
        functools.partial(head_weight_grad_kernel, columns // rows),
        out_shape=jax.ShapeDtypeStruct((width, columns), F32),
        grid=(columns // block,),
        in_specs=[
            pl.BlockSpec((rows, width), lambda i: (0, 0)),
            pl.BlockSpec((1, block), lambda i: (0, i)),
        ],
        out_specs=pl.BlockSpec((width, block), lambda i: (0, i)),
        compiler_params=pltpu.CompilerParams(vmem_limit_bytes=16 * MIB),
        cost_estimate=pl.CostEstimate(flops=6 * rows * width * columns, bytes_accessed=4 * width * columns, transcendentals=0),
        name="head_weight_grad",
    )(normed, bias_grad)


def shards(tokens, doc_length, queries, norm_gain, head_weight, head_bias, labels):
    contexts, classes = lax.axis_size("ctx"), lax.axis_size("cls")
    context_index, class_index = lax.axis_index("ctx"), lax.axis_index("cls")
    token_count = tokens.shape[0]
    rows, width = queries.shape
    full_width = width * contexts
    heads = rows * classes
    half = heads // 2
    columns = labels.shape[0]
    offset = (context_index * classes + class_index) * token_count
    valid_count = jnp.clip(doc_length - offset, 0, token_count)

    context = context_index.astype(jnp.int32)[None]
    own, other = gather(queries)
    keep, send, own_peak, weights = call(
        pool_kernel,
        [
            ((contexts, half, width), F32),
            ((contexts, half, width + LANES), BF16),
            ((heads, LANES), F32),
            ((heads, token_count), F32),
        ],
        "pool",
        [context, valid_count, own, other, tokens],
        smem_args=(0, 1),
        limit=32,
    )
    parts = scatter_sum(keep, send, own_peak)
    gain = norm_gain[None, :]
    sums, pooled, top = call(
        head_sums_kernel,
        [((contexts, 2, columns), F32), ((rows, width), F32), ((rows, LANES), F32)],
        "head_sums",
        [*parts, gain, head_weight],
    )
    sums = lax.all_to_all(sums, "ctx", 0, 0)
    bias_grad, pooled_grad, normed = call(
        functools.partial(head_grads_kernel, full_width),
        [((1, columns), F32), ((rows, width + LANES), BF16), ((rows, width), F32)],
        "head_grads",
        [sums, pooled, top, gain, head_weight, head_bias[None, :], labels[None, :]],
    )
    head_grad = head_weight_grad(normed, bias_grad)
    own, other = gather(pooled_grad)
    keep, send, loss = call(
        functools.partial(grad_kernel, 1.0 / (columns * classes)),
        [((contexts, half, width), F32), ((contexts, half, width), BF16), ((classes, LANES), F32)],
        "grad",
        [context, own, other, tokens, weights, own_peak],
        smem_args=(0,),
        limit=32,
    )
    (query_grad,) = call(far_sum_kernel, [((rows, width), F32)], "far_sum", scatter_sum(keep, send, None))
    return (loss[0, 0], query_grad, head_grad, bias_grad.reshape(-1))


def solution(mesh):
    return jax.shard_map(
        shards,
        mesh=mesh,
        in_specs=(
            P(("ctx", "cls"), None),
            P(),
            P("cls", "ctx"),
            P("ctx"),
            P("ctx", "cls"),
            P("cls"),
            P("cls"),
        ),
        out_specs=(P(), P("cls", "ctx"), P("ctx", "cls"), P("cls")),
        check_vma=False,
    )
```

```python
import functools

import jax
import jax.numpy as jnp
from jax import lax
from jax.experimental import pallas as pl
from jax.experimental.pallas import tpu as pltpu
from jax.sharding import PartitionSpec as P

F32 = jnp.float32
BF16 = jnp.bfloat16
LANES = 128
MASKED = -1e30
MIB = 1024 * 1024


def swap(x, ctx_bits, cls_bits):
    contexts, classes = lax.axis_size("ctx"), lax.axis_size("cls")
    pairs = [
        (c * classes + k, (c ^ ctx_bits) * classes + (k ^ cls_bits)) for c in range(contexts) for k in range(classes)
    ]
    return lax.ppermute(x, ("ctx", "cls"), pairs)


def far_steps():
    return [(2 * j, 0) for j in range(1, lax.axis_size("ctx") // 2)]


def near_steps():
    return [(i, 2 * k) for i in range(2) for k in range(lax.axis_size("cls") // 2) if i or k]


def relative_blocks(contexts):
    return [i ^ (2 * j) for i in range(2) for j in range(contexts // 2)]


def call(kernel, outs, name, args, scratch=(), hbm_args=(), smem_args=(), limit=16, cost=None):
    def spec(i):
        if i in hbm_args:
            return pl.BlockSpec(memory_space=pltpu.HBM)
        if i in smem_args:
            return pl.BlockSpec(memory_space=pltpu.SMEM)
        return pl.BlockSpec(memory_space=pltpu.VMEM)

    run = pl.pallas_call(
        kernel,
        out_shape=[jax.ShapeDtypeStruct(s, d) for s, d in outs],
        in_specs=[spec(i) for i in range(len(args))],
        out_specs=[pl.BlockSpec(memory_space=pltpu.VMEM)] * len(outs),
        scratch_shapes=list(scratch),
        compiler_params=pltpu.CompilerParams(vmem_limit_bytes=limit * MIB),
        cost_estimate=cost,
        name=name,
    )
    return list(run(*args))


def stack_kernel(*refs):
    out_ref = refs[-1]
    for at, ref in enumerate(refs[:-1]):
        out_ref[at] = ref[...].reshape(out_ref.shape[1:])


def near_kernel(count, *refs):
    out_ref, parts = refs[-1], refs[:count]
    blocks, rows, _ = parts[0].shape
    across = len(parts) // 2
    for i in range(2):
        for k in range(across):
            out_ref[i * blocks : (i + 1) * blocks, k * rows : (k + 1) * rows] = parts[i * across + k][...]


def gather(block, local=None, after=()):
    far = [swap(block, *step) for step in far_steps()]
    rows, width = block.shape
    (held,) = call(
        stack_kernel, [((len(far) + 1, rows, width), block.dtype)], "stack", [block if local is None else local, *far]
    )
    parts = [held] + [swap(held, *step) for step in near_steps()]
    shape = (2 * held.shape[0], len(parts) // 2 * rows, width)
    (held,) = call(functools.partial(near_kernel, len(parts)), [(shape, held.dtype)], "near", [*parts, *after])
    return held, swap(held, 0, 1)


def pieces(x):
    high = x.astype(BF16)
    rest = x - high.astype(F32)
    middle = rest.astype(BF16)
    return high, middle, (rest - middle.astype(F32)).astype(BF16)


def into_lanes(columns, rows):
    lane = lax.broadcasted_iota(jnp.int32, (rows, LANES), 1)
    out = jnp.zeros((rows, LANES), F32)
    for i, column in enumerate(columns):
        for j, piece in enumerate(pieces(column)):
            out = jnp.where(lane == 3 * i + j, piece.astype(F32), out)
    return out.astype(BF16)


def from_lanes(block, width, i):
    at = width + 3 * i
    block = block.astype(F32)
    return block[:, at : at + 1] + (block[:, at + 1 : at + 2] + block[:, at + 2 : at + 3])


def first_kernel(tokens_ref, queries_ref, out_ref):
    out_ref[...] = queries_ref[...]


def columns_of(context_ref, contexts, p, width):
    return pl.ds(pl.multiple_of((context_ref[0] ^ relative_blocks(contexts)[p]) * width, LANES), width)


def project(context_ref, own_ref, other_ref, tokens_ref, width):
    contexts = own_ref.shape[0]
    total = None
    for p in range(contexts):
        both = jnp.concatenate([own_ref[p], other_ref[p]], axis=0)[:, :width]
        block = tokens_ref[:, columns_of(context_ref, contexts, p, width)]
        part = lax.dot_general(block, both, (((1,), (1,)), ((), ())), preferred_element_type=F32)
        total = part if total is None else total + part
    return total.T


def spread(context_ref, left, tokens_ref, keep_ref, send_ref, extra):
    contexts, half, width = keep_ref.shape
    for p in range(contexts):
        block = tokens_ref[:, columns_of(context_ref, contexts, p, width)]
        part = jnp.dot(left, block, preferred_element_type=F32)
        keep_ref[p] = part[:half]
        send_ref[p, :, :width] = part[half:].astype(BF16)
        if extra is not None:
            send_ref[p, :, width:] = extra


def pool_kernel(context_ref, count_ref, own_ref, other_ref, tokens_ref, keep_ref, send_ref, peak_ref, w_ref):
    scores = project(context_ref, own_ref, other_ref, tokens_ref, keep_ref.shape[2])
    valid = lax.broadcasted_iota(jnp.int32, scores.shape, 1) < count_ref[0]
    peak = jnp.max(jnp.where(valid, scores, MASKED), axis=1, keepdims=True)
    weights = jnp.where(valid, jnp.exp(scores - peak), 0.0)
    w_ref[...] = weights
    peak_ref[...] = jnp.broadcast_to(peak, peak_ref.shape)
    half = keep_ref.shape[1]
    spread(context_ref, weights.astype(BF16), tokens_ref, keep_ref, send_ref, into_lanes([peak[half:]], half))


def grad_kernel(scale, classes, context_ref, own_ref, other_ref, tokens_ref, w_ref, peak_ref, keep_ref, send_ref, loss_ref):
    width = keep_ref.shape[2]
    projected = project(context_ref, own_ref, other_ref, tokens_ref, width)
    own, other = own_ref[0], other_ref[0]
    top = jnp.concatenate([from_lanes(own, width, 0), from_lanes(other, width, 0)], axis=0)
    weights = w_ref[...] * jnp.exp(peak_ref[:, :1] - top)
    spread(context_ref, (weights * projected).astype(BF16), tokens_ref, keep_ref, send_ref, None)
    rows = classes // 2
    each = own.shape[0] // rows
    sums = []
    for block in (own, other):
        column = from_lanes(block, width, 1)
        level = [column[i * each : i * each + 1] for i in range(rows)]
        while len(level) > 1:
            level = [a + b for a, b in zip(level[::2], level[1::2])]
        sums.append(level[0])
    loss_ref[...] = (sums[0] + sums[1]) * scale


def total_of(keep, peak, received, width):
    if peak is None:
        for block in received:
            keep = keep + block.astype(F32)
        return keep, None
    others = [from_lanes(block, width, 0) for block in received]
    top = peak
    for other in others:
        top = jnp.maximum(top, other)
    keep = keep * jnp.exp(peak - top)
    for block, other in zip(received, others):
        keep = keep + block[:, :width].astype(F32) * jnp.exp(other - top)
    return keep, top


def put(ref, p, total, top, width):
    ref[p, :, :width] = total.astype(BF16)
    if top is not None:
        ref[p, :, width:] = into_lanes([top], total.shape[0])


def core_kernel(peaks, across, *refs):
    keep_ref, recv_ref, *refs = refs
    peak = refs.pop(0)[: keep_ref.shape[1], :1] if peaks else None
    top_ref = refs.pop() if peaks else None
    width = keep_ref.shape[2]
    blocks, rows = refs[0].shape[:2]
    for i in range(2):
        for b in range(blocks):
            p = i * blocks + b
            total, top = total_of(keep_ref[p], peak, [recv_ref[p]], width)
            for k in range(across):
                part = total[k * rows : (k + 1) * rows]
                part_top = top[k * rows : (k + 1) * rows] if peaks else None
                if i == 0 and k == 0:
                    refs[0][b] = part
                else:
                    put(refs[i * across + k], b, part, part_top, width)
    if peaks:
        top_ref[...] = jnp.broadcast_to(top[:rows], top_ref.shape)


def near_sum_kernel(peaks, count, *refs):
    keep_ref, *refs = refs
    received, refs = refs[:count], list(refs[count:])
    peak = refs.pop(0)[:, :1] if peaks else None
    top_ref = refs.pop() if peaks else None
    width = keep_ref.shape[2]
    for p in range(keep_ref.shape[0]):
        total, top = total_of(keep_ref[p], peak, [ref[p] for ref in received], width)
        if p == 0:
            refs[0][0] = total
        else:
            put(refs[p], 0, total, top, width)
    if peaks:
        top_ref[...] = jnp.broadcast_to(top, top_ref.shape)


def scatter_sum(keep, send, peak):
    peaks = peak is not None
    contexts, half, width = keep.shape
    lanes = send.shape[2]
    near, far = near_steps(), far_steps()
    across = (len(near) + 1) // 2
    blocks, rows = contexts // 2, half // across
    top_out = [((rows, LANES), F32)] if peaks else []
    outs = [((blocks, rows, width), F32)] + [((blocks, rows, lanes), BF16)] * len(near) + top_out
    args = [keep, swap(send, 0, 1)] + ([peak] if peaks else [])
    out = call(functools.partial(core_kernel, peaks, across), outs, "core_sum", args)
    received = [swap(s, *step) for s, step in zip(out[1:], near)]
    outs = [((1, rows, width), F32)] + [((1, rows, lanes), BF16)] * len(far) + top_out
    args = [out[0], *received] + (out[-1:] if peaks else [])
    out = call(functools.partial(near_sum_kernel, peaks, len(received)), outs, "near_sum", args)
    received = [swap(s, *step) for s, step in zip(out[1:], far)]
    return [out[0], *received] + (out[-1:] if peaks else [])


def far_sum_kernel(*refs):
    keep_ref, *received, out_ref = refs
    out_ref[...] = total_of(keep_ref[0], None, [ref[0] for ref in received], keep_ref.shape[2])[0]


def head_mask(shape, attributes):
    row = lax.broadcasted_iota(jnp.int32, shape, 0)
    column = lax.broadcasted_iota(jnp.int32, shape, 1)
    return column // attributes == row


def head_sums_kernel(*refs):
    keep_ref, *received, peak_ref, gain_ref, weight_ref, sums_ref, pooled_ref, top_ref = refs
    pooled, top = total_of(keep_ref[0], peak_ref[:, :1], [ref[0] for ref in received], keep_ref.shape[2])
    pooled_ref[...] = pooled
    top_ref[...] = jnp.broadcast_to(top, top_ref.shape)
    scaled_b = (pooled * gain_ref[...]).astype(BF16)
    product = jnp.dot(scaled_b, weight_ref[...], preferred_element_type=F32)
    mask = head_mask(product.shape, product.shape[1] // product.shape[0])
    squares = jnp.sum(pooled * pooled, axis=1, keepdims=True)
    product_flat = jnp.sum(jnp.where(mask, product, 0.0), axis=0, keepdims=True)
    squares_flat = jnp.sum(jnp.where(mask, squares, 0.0), axis=0, keepdims=True)
    sums_ref[0:1, :] = product_flat
    sums_ref[1:2, :] = squares_flat


def tree_sum_kernel(*refs):
    level = [ref[...] for ref in refs[:-1]]
    while len(level) > 1:
        level = [a + b for a, b in zip(level[::2], level[1::2])]
    refs[-1][...] = level[0]


def head_grads_kernel(
    full_width, sums_ref, other_sums_ref, pooled_ref, top_ref, gain_ref, weight_ref, bias_ref, label_ref, bias_grad_ref, grad_ref, normed_ref
):
    pooled, gain = pooled_ref[...], gain_ref[...]
    heads, width = pooled.shape
    columns = sums_ref.shape[1]
    sums = sums_ref[...] + other_sums_ref[...]
    mask = head_mask((heads, columns), columns // heads)
    inverse_flat = lax.rsqrt(sums[1:2] / full_width + 1e-05)
    inverse_rms = jnp.max(jnp.where(mask, inverse_flat, 0.0), axis=1, keepdims=True)
    product = inverse_flat * sums[0:1]
    logits = product + bias_ref[...]
    target = label_ref[...].astype(F32)
    losses = jnp.maximum(logits, 0.0) + jnp.log1p(jnp.exp(-jnp.abs(logits))) - target * logits
    loss = jnp.sum(losses, axis=1, keepdims=True)
    bias_grad = jax.nn.sigmoid(logits) - target
    bias_grad_ref[...] = bias_grad
    by_head = jnp.where(mask, bias_grad, 0.0)
    high = by_head.astype(BF16)
    low = (by_head - high.astype(F32)).astype(BF16)
    both = jnp.concatenate([high, low], axis=0)
    back = lax.dot_general(both, weight_ref[...], (((1,), (1,)), ((), ())), preferred_element_type=F32)
    normed_grad = (back[:heads] + back[heads:]) * gain
    inner = jnp.sum(by_head * product, axis=1, keepdims=True) / full_width
    unit = pooled * inverse_rms
    grad_ref[:, :width] = (inverse_rms * (normed_grad - unit * inner)).astype(BF16)
    grad_ref[:, width:] = into_lanes([top_ref[:, :1], jnp.broadcast_to(loss, (heads, 1))], heads)
    normed_ref[...] = unit * gain


def head_weight_grad_kernel(attributes, normed_ref, bias_grad_ref, out_ref, done_ref):
    heads = normed_ref.shape[0]
    columns = out_ref.shape[1]
    parts = jnp.concatenate(pieces(normed_ref[...]), axis=0)
    row = lax.broadcasted_iota(jnp.int32, (3 * heads, columns), 0) % heads
    column = pl.program_id(0) * columns + lax.broadcasted_iota(jnp.int32, (3 * heads, columns), 1)
    ones = jnp.where(column // attributes == row, 1.0, 0.0).astype(BF16)
    normed = lax.dot_general(parts, ones, (((0,), (0,)), ((), ())), preferred_element_type=F32)
    out_ref[...] = normed * bias_grad_ref[...]
    done_ref[...] = jnp.zeros_like(done_ref)


def head_weight_grad(normed, bias_grad):
    rows, width = normed.shape
    columns = bias_grad.shape[1]
    block = columns // 4
    return pl.pallas_call(
        functools.partial(head_weight_grad_kernel, columns // rows),
        out_shape=[jax.ShapeDtypeStruct((width, columns), F32), jax.ShapeDtypeStruct((8, LANES), F32)],
        grid=(columns // block,),
        in_specs=[
            pl.BlockSpec((rows, width), lambda i: (0, 0)),
            pl.BlockSpec((1, block), lambda i: (0, i)),
        ],
        out_specs=[pl.BlockSpec((width, block), lambda i: (0, i)), pl.BlockSpec((8, LANES), lambda i: (0, 0))],
        compiler_params=pltpu.CompilerParams(vmem_limit_bytes=16 * MIB),
        cost_estimate=pl.CostEstimate(flops=6 * rows * width * columns, bytes_accessed=4 * width * columns, transcendentals=0),
        name="head_weight_grad",
    )(normed, bias_grad)


def shards(tokens, doc_length, queries, norm_gain, head_weight, head_bias, labels):
    contexts, classes = lax.axis_size("ctx"), lax.axis_size("cls")
    context_index, class_index = lax.axis_index("ctx"), lax.axis_index("cls")
    token_count = tokens.shape[0]
    rows, width = queries.shape
    full_width = width * contexts
    heads = rows * classes
    half = heads // 2
    columns = labels.shape[0]
    offset = (context_index * classes + class_index) * token_count
    valid_count = jnp.clip(doc_length - offset, 0, token_count)

    context = context_index.astype(jnp.int32)[None]
    (queries_here,) = call(
        first_kernel,
        [(queries.shape, BF16)],
        "first",
        [tokens, queries],
        limit=32,
        cost=pl.CostEstimate(flops=0, bytes_accessed=2 * token_count * full_width, transcendentals=0),
    )
    own, other = gather(queries, queries_here)
    keep, send, own_peak, weights = call(
        pool_kernel,
        [
            ((contexts, half, width), F32),
            ((contexts, half, width + LANES), BF16),
            ((heads, LANES), F32),
            ((heads, token_count), F32),
        ],
        "pool",
        [context, valid_count, own, other, tokens],
        smem_args=(0, 1),
        limit=32,
    )
    parts = scatter_sum(keep, send, own_peak)
    gain = norm_gain[None, :]
    sums, pooled, top = call(
        head_sums_kernel,
        [((2, columns), F32), ((rows, width), F32), ((rows, LANES), F32)],
        "head_sums",
        [*parts, gain, head_weight],
    )
    far_sums = [swap(sums, *step) for step in far_steps()]
    (sums,) = call(tree_sum_kernel, [((2, columns), F32)], "tree_sum", [sums, *far_sums])
    bias_grad, pooled_grad, normed = call(
        functools.partial(head_grads_kernel, full_width),
        [((1, columns), F32), ((rows, width + LANES), BF16), ((rows, width), F32)],
        "head_grads",
        [sums, swap(sums, 1, 0), pooled, top, gain, head_weight, head_bias[None, :], labels[None, :]],
    )
    head_grad, done = head_weight_grad(normed, bias_grad)
    own, other = gather(pooled_grad, after=(done,))
    keep, send, loss = call(
        functools.partial(grad_kernel, 1.0 / (columns * classes), classes),
        [((contexts, half, width), F32), ((contexts, half, width), BF16), ((1, 1), F32)],
        "grad",
        [context, own, other, tokens, weights, own_peak],
        smem_args=(0,),
        limit=32,
    )
    (query_grad,) = call(far_sum_kernel, [((rows, width), F32)], "far_sum", scatter_sum(keep, send, None))
    return (loss.reshape(()), query_grad, head_grad, bias_grad.reshape(-1))


def solution(mesh):
    return jax.shard_map(
        shards,
        mesh=mesh,
        in_specs=(
            P(("ctx", "cls"), None),
            P(),
            P("cls", "ctx"),
            P("ctx"),
            P("ctx", "cls"),
            P("cls"),
            P("cls"),
        ),
        out_specs=(P(), P("cls", "ctx"), P("ctx", "cls"), P("cls")),
        check_vma=False,
    )
```

```python
import functools

import jax
import jax.numpy as jnp
from jax import lax
from jax.experimental import pallas as pl
from jax.experimental.pallas import tpu as pltpu
from jax.sharding import PartitionSpec as P

F32 = jnp.float32
BF16 = jnp.bfloat16
LANES = 128
MASKED = -1e30
MIB = 1024 * 1024


def swap(x, ctx_bits, cls_bits):
    contexts, classes = lax.axis_size("ctx"), lax.axis_size("cls")
    pairs = [
        (c * classes + k, (c ^ ctx_bits) * classes + (k ^ cls_bits)) for c in range(contexts) for k in range(classes)
    ]
    return lax.ppermute(x, ("ctx", "cls"), pairs)


def far_steps():
    return [(2 * j, 0) for j in reversed(range(1, lax.axis_size("ctx") // 2))]


def near_steps():
    steps = [(i, 2 * k) for i in range(2) for k in range(lax.axis_size("cls") // 2) if i or k]
    return sorted(steps, key=lambda step: not (step[0] and step[1]))


def relative_blocks(contexts):
    return [i ^ (2 * j) for i in range(2) for j in range(contexts // 2)]


def call(kernel, outs, name, args, scratch=(), hbm_args=(), smem_args=(), limit=16, cost=None):
    def spec(i):
        if i in hbm_args:
            return pl.BlockSpec(memory_space=pltpu.HBM)
        if i in smem_args:
            return pl.BlockSpec(memory_space=pltpu.SMEM)
        return pl.BlockSpec(memory_space=pltpu.VMEM)

    run = pl.pallas_call(
        kernel,
        out_shape=[jax.ShapeDtypeStruct(s, d) for s, d in outs],
        in_specs=[spec(i) for i in range(len(args))],
        out_specs=[pl.BlockSpec(memory_space=pltpu.VMEM)] * len(outs),
        scratch_shapes=list(scratch),
        compiler_params=pltpu.CompilerParams(vmem_limit_bytes=limit * MIB),
        cost_estimate=cost,
        name=name,
    )
    return list(run(*args))


def stack_kernel(*refs):
    out_ref = refs[-1]
    for at, ref in enumerate(refs[:-1]):
        out_ref[at] = ref[...].reshape(out_ref.shape[1:])


def near_kernel(steps, *refs):
    out_ref = refs[-1]
    blocks, rows, _ = refs[0].shape
    for (i, k), ref in zip(steps, refs):
        at = k // 2 * rows
        out_ref[i * blocks : (i + 1) * blocks, at : at + rows] = ref[...]


def gather(block, local=None, after=()):
    far = [swap(block, *step) for step in far_steps()[::-1]]
    rows, width = block.shape
    (held,) = call(
        stack_kernel, [((len(far) + 1, rows, width), block.dtype)], "stack", [block if local is None else local, *far]
    )
    steps = near_steps()[::-1]
    parts = [held] + [swap(held, *step) for step in steps]
    steps = [(0, 0)] + steps
    shape = (2 * held.shape[0], len(parts) // 2 * rows, width)
    (held,) = call(functools.partial(near_kernel, steps), [(shape, held.dtype)], "near", [*parts, *after])
    return held, swap(held, 0, 1)


def pieces(x):
    high = x.astype(BF16)
    rest = x - high.astype(F32)
    middle = rest.astype(BF16)
    return high, middle, (rest - middle.astype(F32)).astype(BF16)


def into_lanes(columns, rows):
    lane = lax.broadcasted_iota(jnp.int32, (rows, LANES), 1)
    out = jnp.zeros((rows, LANES), F32)
    for i, column in enumerate(columns):
        for j, piece in enumerate(pieces(column)):
            out = jnp.where(lane == 3 * i + j, piece.astype(F32), out)
    return out.astype(BF16)


def from_lanes(block, width, i):
    at = width + 3 * i
    block = block.astype(F32)
    return block[:, at : at + 1] + (block[:, at + 1 : at + 2] + block[:, at + 2 : at + 3])


def load_kernel(tokens_ref, queries_ref, held_ref, own_ref, sems):
    chunks = sems.shape[0] - 1
    rows = held_ref.shape[0] // chunks
    copies = [pltpu.make_async_copy(queries_ref, own_ref, sems.at[chunks])]
    for i in range(chunks):
        part = pl.ds(i * rows, rows)
        copies.append(pltpu.make_async_copy(tokens_ref.at[part], held_ref.at[part], sems.at[i]))
    for copy in copies:
        copy.start()
    for copy in copies:
        copy.wait()


def load(*arrays):
    chunks = 8
    return pl.pallas_call(
        load_kernel,
        out_shape=[pltpu.VMEM(x.shape, x.dtype) for x in arrays],
        in_specs=[pl.BlockSpec(memory_space=pltpu.HBM)] * len(arrays),
        out_specs=[pl.BlockSpec(memory_space=pltpu.VMEM)] * len(arrays),
        scratch_shapes=[pltpu.SemaphoreType.DMA((chunks + 1,))],
        compiler_params=pltpu.CompilerParams(vmem_limit_bytes=16 * MIB),
        name="load",
    )(*[pltpu.with_memory_space_constraint(x, pltpu.HBM) for x in arrays])


def columns_of(context_ref, contexts, p, width, at=0, size=None):
    start = pl.multiple_of((context_ref[0] ^ relative_blocks(contexts)[p]) * width, LANES)
    return pl.ds(start + at, size or width)


def project(context_ref, own_ref, other_ref, tokens_ref, width, tile=256):
    contexts = own_ref.shape[0]
    tiles = []
    for at in range(0, tokens_ref.shape[0], tile):
        total = None
        for p in range(contexts):
            both = jnp.concatenate([own_ref[p], other_ref[p]], axis=0)[:, :width]
            block = tokens_ref[at : at + tile, columns_of(context_ref, contexts, p, width)]
            part = lax.dot_general(block, both, (((1,), (1,)), ((), ())), preferred_element_type=F32)
            total = part if total is None else total + part
        tiles.append(total.T)
    return jnp.concatenate(tiles, axis=1)


def project_grad(context_ref, own_ref, other_ref, tokens_ref, width):
    contexts = own_ref.shape[0]
    total = None
    for p in range(contexts):
        both = jnp.concatenate([own_ref[p], other_ref[p]], axis=0)[:, :width]
        block = tokens_ref[:, columns_of(context_ref, contexts, p, width)]
        part = lax.dot_general(both, block, (((1,), (1,)), ((), ())), preferred_element_type=F32)
        total = part if total is None else total + part
    return total


def spread(context_ref, left, tokens_ref, keep_ref, send_ref, extra, tile):
    contexts, half, width = keep_ref.shape
    for p in range(contexts):
        for at in range(0, width, tile):
            block = tokens_ref[:, columns_of(context_ref, contexts, p, width, at, tile)]
            part = jnp.dot(left, block, preferred_element_type=F32)
            keep_ref[p, :, at : at + tile] = part[:half]
            send_ref[p, :, at : at + tile] = part[half:].astype(BF16)
        if extra is not None:
            send_ref[p, :, width:] = extra


def pool_kernel(context_ref, count_ref, own_ref, other_ref, tokens_ref, keep_ref, send_ref, peak_ref, w_ref):
    scores = project(context_ref, own_ref, other_ref, tokens_ref, keep_ref.shape[2])
    valid = lax.broadcasted_iota(jnp.int32, scores.shape, 1) < count_ref[0]
    peak = jnp.max(jnp.where(valid, scores, MASKED), axis=1, keepdims=True)
    weights = jnp.where(valid, jnp.exp(scores - peak), 0.0)
    w_ref[...] = weights
    peak_ref[...] = jnp.broadcast_to(peak, peak_ref.shape)
    half = keep_ref.shape[1]
    spread(context_ref, weights.astype(BF16), tokens_ref, keep_ref, send_ref, into_lanes([peak[half:]], half), 256)


def grad_kernel(scale, classes, context_ref, own_ref, other_ref, tokens_ref, w_ref, peak_ref, keep_ref, send_ref, loss_ref):
    width = keep_ref.shape[2]
    projected = project_grad(context_ref, own_ref, other_ref, tokens_ref, width)
    own, other = own_ref[0], other_ref[0]
    top = jnp.concatenate([from_lanes(own, width, 0), from_lanes(other, width, 0)], axis=0)
    weights = w_ref[...] * jnp.exp(peak_ref[:, :1] - top)
    spread(context_ref, (weights * projected).astype(BF16), tokens_ref, keep_ref, send_ref, None, width)
    rows = classes // 2
    each = own.shape[0] // rows
    sums = []
    for block in (own, other):
        column = from_lanes(block, width, 1)
        level = [column[i * each : i * each + 1] for i in range(rows)]
        while len(level) > 1:
            level = [a + b for a, b in zip(level[::2], level[1::2])]
        sums.append(level[0])
    loss_ref[...] = (sums[0] + sums[1]) * scale


def total_of(keep, peak, received, width):
    if peak is None:
        for block in received:
            keep = keep + block.astype(F32)
        return keep, None
    others = [from_lanes(block, width, 0) for block in received]
    top = peak
    for other in others:
        top = jnp.maximum(top, other)
    keep = keep * jnp.exp(peak - top)
    for block, other in zip(received, others):
        keep = keep + block[:, :width].astype(F32) * jnp.exp(other - top)
    return keep, top


def put(ref, p, total, top, width):
    ref[p, :, :width] = total.astype(BF16)
    if top is not None:
        ref[p, :, width:] = into_lanes([top], total.shape[0])


def core_kernel(peaks, steps, *refs):
    keep_ref, recv_ref, *refs = refs
    peak = refs.pop(0)[: keep_ref.shape[1], :1] if peaks else None
    top_ref = refs.pop() if peaks else None
    width = keep_ref.shape[2]
    blocks, rows = refs[0].shape[:2]
    for i in range(2):
        for b in range(blocks):
            p = i * blocks + b
            total, top = total_of(keep_ref[p], peak, [recv_ref[p]], width)
            for ref, (_, k) in [(r, step) for r, step in zip(refs, steps) if step[0] == i]:
                at = k // 2 * rows
                part = total[at : at + rows]
                if ref is refs[0]:
                    ref[b] = part
                else:
                    put(ref, b, part, top[at : at + rows] if peaks else None, width)
    if peaks:
        top_ref[...] = jnp.broadcast_to(top[:rows], top_ref.shape)


def near_sum_kernel(peaks, count, steps, *refs):
    keep_ref, *refs = refs
    received, refs = refs[:count], list(refs[count:])
    peak = refs.pop(0)[:, :1] if peaks else None
    top_ref = refs.pop() if peaks else None
    width = keep_ref.shape[2]
    for p in range(keep_ref.shape[0]):
        total, top = total_of(keep_ref[p], peak, [ref[p] for ref in received], width)
        if p == 0:
            refs[0][0] = total
        else:
            put(refs[steps.index((2 * p, 0)) + 1], 0, total, top, width)
    if peaks:
        top_ref[...] = jnp.broadcast_to(top, top_ref.shape)


def scatter_sum(keep, send, peak):
    peaks = peak is not None
    contexts, half, width = keep.shape
    lanes = send.shape[2]
    near, far = near_steps(), far_steps()
    across = (len(near) + 1) // 2
    blocks, rows = contexts // 2, half // across
    top_out = [((rows, LANES), F32)] if peaks else []
    outs = [((blocks, rows, width), F32)] + [((blocks, rows, lanes), BF16)] * len(near) + top_out
    args = [keep, swap(send, 0, 1)] + ([peak] if peaks else [])
    out = call(functools.partial(core_kernel, peaks, [(0, 0)] + near), outs, "core_sum", args)
    received = [swap(s, *step) for s, step in zip(out[1:], near)]
    outs = [((1, rows, width), F32)] + [((1, rows, lanes), BF16)] * len(far) + top_out
    args = [out[0], *received] + (out[-1:] if peaks else [])
    out = call(functools.partial(near_sum_kernel, peaks, len(received), far), outs, "near_sum", args)
    received = [swap(s, *step) for s, step in zip(out[1:], far)]
    return [out[0], *received] + (out[-1:] if peaks else [])


def far_sum_kernel(*refs):
    keep_ref, *received, out_ref = refs
    out_ref[...] = total_of(keep_ref[0], None, [ref[0] for ref in received], keep_ref.shape[2])[0]


def head_mask(shape, attributes):
    row = lax.broadcasted_iota(jnp.int32, shape, 0)
    column = lax.broadcasted_iota(jnp.int32, shape, 1)
    return column // attributes == row


def head_sums_kernel(*refs):
    keep_ref, *received, peak_ref, gain_ref, weight_ref, sums_ref, pooled_ref, top_ref = refs
    pooled, top = total_of(keep_ref[0], peak_ref[:, :1], [ref[0] for ref in received], keep_ref.shape[2])
    pooled_ref[...] = pooled
    top_ref[...] = jnp.broadcast_to(top, top_ref.shape)
    scaled_b = (pooled * gain_ref[...]).astype(BF16)
    product = jnp.dot(scaled_b, weight_ref[...], preferred_element_type=F32)
    mask = head_mask(product.shape, product.shape[1] // product.shape[0])
    squares = jnp.sum(pooled * pooled, axis=1, keepdims=True)
    product_flat = jnp.sum(jnp.where(mask, product, 0.0), axis=0, keepdims=True)
    squares_flat = jnp.sum(jnp.where(mask, squares, 0.0), axis=0, keepdims=True)
    sums_ref[0:1, :] = product_flat
    sums_ref[1:2, :] = squares_flat


def tree_sum_kernel(*refs):
    level = [ref[...] for ref in refs[:-1]]
    while len(level) > 1:
        level = [a + b for a, b in zip(level[::2], level[1::2])]
    refs[-1][...] = level[0]


def head_grads_kernel(
    full_width, sums_ref, other_sums_ref, pooled_ref, top_ref, gain_ref, weight_ref, bias_ref, label_ref, bias_grad_ref, grad_ref, normed_ref
):
    pooled, gain = pooled_ref[...], gain_ref[...]
    heads, width = pooled.shape
    columns = sums_ref.shape[1]
    sums = sums_ref[...] + other_sums_ref[...]
    mask = head_mask((heads, columns), columns // heads)
    inverse_flat = lax.rsqrt(sums[1:2] / full_width + 1e-05)
    inverse_rms = jnp.max(jnp.where(mask, inverse_flat, 0.0), axis=1, keepdims=True)
    product = inverse_flat * sums[0:1]
    logits = product + bias_ref[...]
    target = label_ref[...].astype(F32)
    losses = jnp.maximum(logits, 0.0) + jnp.log1p(jnp.exp(-jnp.abs(logits))) - target * logits
    loss = jnp.sum(losses, axis=1, keepdims=True)
    bias_grad = jax.nn.sigmoid(logits) - target
    bias_grad_ref[...] = bias_grad
    by_head = jnp.where(mask, bias_grad, 0.0)
    high = by_head.astype(BF16)
    low = (by_head - high.astype(F32)).astype(BF16)
    both = jnp.concatenate([high, low], axis=0)
    back = lax.dot_general(both, weight_ref[...], (((1,), (1,)), ((), ())), preferred_element_type=F32)
    normed_grad = (back[:heads] + back[heads:]) * gain
    inner = jnp.sum(by_head * product, axis=1, keepdims=True) / full_width
    unit = pooled * inverse_rms
    grad_ref[:, :width] = (inverse_rms * (normed_grad - unit * inner)).astype(BF16)
    grad_ref[:, width:] = into_lanes([top_ref[:, :1], jnp.broadcast_to(loss, (heads, 1))], heads)
    normed_ref[...] = unit * gain


def head_weight_grad_kernel(attributes, normed_ref, bias_grad_ref, out_ref, done_ref):
    heads = normed_ref.shape[0]
    columns = out_ref.shape[1]
    parts = jnp.concatenate(pieces(normed_ref[...]), axis=0)
    row = lax.broadcasted_iota(jnp.int32, (3 * heads, columns), 0) % heads
    column = pl.program_id(0) * columns + lax.broadcasted_iota(jnp.int32, (3 * heads, columns), 1)
    ones = jnp.where(column // attributes == row, 1.0, 0.0).astype(BF16)
    normed = lax.dot_general(parts, ones, (((0,), (0,)), ((), ())), preferred_element_type=F32)
    out_ref[...] = normed * bias_grad_ref[...]
    done_ref[...] = jnp.zeros_like(done_ref)


def head_weight_grad(normed, bias_grad):
    rows, width = normed.shape
    columns = bias_grad.shape[1]
    block = columns // 4
    return pl.pallas_call(
        functools.partial(head_weight_grad_kernel, columns // rows),
        out_shape=[jax.ShapeDtypeStruct((width, columns), F32), jax.ShapeDtypeStruct((8, LANES), F32)],
        grid=(columns // block,),
        in_specs=[
            pl.BlockSpec((rows, width), lambda i: (0, 0)),
            pl.BlockSpec((1, block), lambda i: (0, i)),
        ],
        out_specs=[pl.BlockSpec((width, block), lambda i: (0, i)), pl.BlockSpec((8, LANES), lambda i: (0, 0))],
        compiler_params=pltpu.CompilerParams(vmem_limit_bytes=16 * MIB),
        cost_estimate=pl.CostEstimate(flops=6 * rows * width * columns, bytes_accessed=4 * width * columns, transcendentals=0),
        name="head_weight_grad",
    )(normed, bias_grad)


def shards(tokens, doc_length, queries, norm_gain, head_weight, head_bias, labels):
    contexts, classes = lax.axis_size("ctx"), lax.axis_size("cls")
    context_index, class_index = lax.axis_index("ctx"), lax.axis_index("cls")
    token_count = tokens.shape[0]
    rows, width = queries.shape
    full_width = width * contexts
    heads = rows * classes
    half = heads // 2
    columns = labels.shape[0]
    offset = (context_index * classes + class_index) * token_count
    valid_count = jnp.clip(doc_length - offset, 0, token_count)

    context = context_index.astype(jnp.int32)[None]
    held, queries_here = load(tokens, queries)
    own, other = gather(queries, queries_here)
    keep, send, own_peak, weights = call(
        pool_kernel,
        [
            ((contexts, half, width), F32),
            ((contexts, half, width + LANES), BF16),
            ((heads, LANES), F32),
            ((heads, token_count), F32),
        ],
        "pool",
        [context, valid_count, own, other, held],
        smem_args=(0, 1),
        limit=16,
    )
    parts = scatter_sum(keep, send, own_peak)
    gain = norm_gain[None, :]
    sums, pooled, top = call(
        head_sums_kernel,
        [((2, columns), F32), ((rows, width), F32), ((rows, LANES), F32)],
        "head_sums",
        [*parts, gain, head_weight],
    )
    far_sums = [swap(sums, *step) for step in far_steps()[::-1]]
    (sums,) = call(tree_sum_kernel, [((2, columns), F32)], "tree_sum", [sums, *far_sums])
    bias_grad, pooled_grad, normed = call(
        functools.partial(head_grads_kernel, full_width),
        [((1, columns), F32), ((rows, width + LANES), BF16), ((rows, width), F32)],
        "head_grads",
        [sums, swap(sums, 1, 0), pooled, top, gain, head_weight, head_bias[None, :], labels[None, :]],
    )
    head_grad, done = head_weight_grad(normed, bias_grad)
    own, other = gather(pooled_grad, after=(done,))
    keep, send, loss = call(
        functools.partial(grad_kernel, 1.0 / (columns * classes), classes),
        [((contexts, half, width), F32), ((contexts, half, width), BF16), ((1, 1), F32)],
        "grad",
        [context, own, other, held, weights, own_peak],
        smem_args=(0,),
        limit=16,
    )
    (query_grad,) = call(far_sum_kernel, [((rows, width), F32)], "far_sum", scatter_sum(keep, send, None))
    return (loss.reshape(()), query_grad, head_grad, bias_grad.reshape(-1))


def solution(mesh):
    return jax.shard_map(
        shards,
        mesh=mesh,
        in_specs=(
            P(("ctx", "cls"), None),
            P(),
            P("cls", "ctx"),
            P("ctx"),
            P("ctx", "cls"),
            P("cls"),
            P("cls"),
        ),
        out_specs=(P(), P("cls", "ctx"), P("ctx", "cls"), P("cls")),
        check_vma=False,
    )
```

```python
import functools

import jax
import jax.numpy as jnp
from jax import lax
from jax.experimental import pallas as pl
from jax.experimental.pallas import tpu as pltpu
from jax.sharding import PartitionSpec as P

F32 = jnp.float32
BF16 = jnp.bfloat16
LANES = 128
MASKED = -1e30
MIB = 1024 * 1024


def swap(x, ctx_bits, cls_bits):
    contexts, classes = lax.axis_size("ctx"), lax.axis_size("cls")
    pairs = [
        (c * classes + k, (c ^ ctx_bits) * classes + (k ^ cls_bits)) for c in range(contexts) for k in range(classes)
    ]
    return lax.ppermute(x, ("ctx", "cls"), pairs)


def far_steps():
    return [(2 * j, 0) for j in reversed(range(1, lax.axis_size("ctx") // 2))]


def near_steps():
    steps = [(i, 2 * k) for i in range(2) for k in range(lax.axis_size("cls") // 2) if i or k]
    return sorted(steps, key=lambda step: not (step[0] and step[1]))


def relative_blocks(contexts):
    return [i ^ (2 * j) for i in range(2) for j in range(contexts // 2)]


def call(kernel, outs, name, args, scratch=(), hbm_args=(), smem_args=(), limit=16, cost=None):
    def spec(i):
        if i in hbm_args:
            return pl.BlockSpec(memory_space=pltpu.HBM)
        if i in smem_args:
            return pl.BlockSpec(memory_space=pltpu.SMEM)
        return pl.BlockSpec(memory_space=pltpu.VMEM)

    run = pl.pallas_call(
        kernel,
        out_shape=[jax.ShapeDtypeStruct(s, d) for s, d in outs],
        in_specs=[spec(i) for i in range(len(args))],
        out_specs=[pl.BlockSpec(memory_space=pltpu.VMEM)] * len(outs),
        scratch_shapes=list(scratch),
        compiler_params=pltpu.CompilerParams(vmem_limit_bytes=limit * MIB),
        cost_estimate=cost,
        name=name,
    )
    return list(run(*args))


def stack_kernel(*refs):
    out_ref = refs[-1]
    for at, ref in enumerate(refs[:-1]):
        out_ref[at] = ref[...].reshape(out_ref.shape[1:])


def near_kernel(steps, *refs):
    out_ref = refs[-1]
    blocks, rows, _ = refs[0].shape
    for (i, k), ref in zip(steps, refs):
        at = k // 2 * rows
        out_ref[i * blocks : (i + 1) * blocks, at : at + rows] = ref[...]


def gather(block, local=None, after=()):
    far = [swap(block, *step) for step in far_steps()[::-1]]
    rows, width = block.shape
    (held,) = call(
        stack_kernel, [((len(far) + 1, rows, width), block.dtype)], "stack", [block if local is None else local, *far]
    )
    steps = near_steps()[::-1]
    parts = [held] + [swap(held, *step) for step in steps]
    steps = [(0, 0)] + steps
    shape = (2 * held.shape[0], len(parts) // 2 * rows, width)
    (held,) = call(functools.partial(near_kernel, steps), [(shape, held.dtype)], "near", [*parts, *after])
    return held, swap(held, 0, 1)


def pieces(x):
    high = x.astype(BF16)
    rest = x - high.astype(F32)
    middle = rest.astype(BF16)
    return high, middle, (rest - middle.astype(F32)).astype(BF16)


def into_lanes(columns, rows):
    lane = lax.broadcasted_iota(jnp.int32, (rows, LANES), 1)
    out = jnp.zeros((rows, LANES), F32)
    for i, column in enumerate(columns):
        for j, piece in enumerate(pieces(column)):
            out = jnp.where(lane == 3 * i + j, piece.astype(F32), out)
    return out.astype(BF16)


def from_lanes(block, width, i):
    at = width + 3 * i
    block = block.astype(F32)
    return block[:, at : at + 1] + (block[:, at + 1 : at + 2] + block[:, at + 2 : at + 3])


def load_kernel(tokens_ref, queries_ref, held_ref, own_ref, sems):
    chunks = sems.shape[0] - 1
    rows = held_ref.shape[0] // chunks
    copies = [pltpu.make_async_copy(queries_ref, own_ref, sems.at[chunks])]
    for i in range(chunks):
        part = pl.ds(i * rows, rows)
        copies.append(pltpu.make_async_copy(tokens_ref.at[part], held_ref.at[part], sems.at[i]))
    for copy in copies:
        copy.start()
    for copy in copies:
        copy.wait()


def load(*arrays):
    chunks = 8
    return pl.pallas_call(
        load_kernel,
        out_shape=[pltpu.VMEM(x.shape, x.dtype) for x in arrays],
        in_specs=[pl.BlockSpec(memory_space=pltpu.HBM)] * len(arrays),
        out_specs=[pl.BlockSpec(memory_space=pltpu.VMEM)] * len(arrays),
        scratch_shapes=[pltpu.SemaphoreType.DMA((chunks + 1,))],
        compiler_params=pltpu.CompilerParams(vmem_limit_bytes=16 * MIB),
        name="load",
    )(*[pltpu.with_memory_space_constraint(x, pltpu.HBM) for x in arrays])


def columns_of(contexts, p, width, at=0, size=None):
    start = pl.multiple_of((lax.axis_index("ctx") ^ relative_blocks(contexts)[p]) * width, LANES)
    return pl.ds(start + at, size or width)


def project(own_ref, other_ref, tokens_ref, width, tile=256):
    contexts = own_ref.shape[0]
    tiles = []
    for at in range(0, tokens_ref.shape[0], tile):
        total = None
        for p in range(contexts):
            both = jnp.concatenate([own_ref[p], other_ref[p]], axis=0)[:, :width]
            block = tokens_ref[at : at + tile, columns_of(contexts, p, width)]
            part = lax.dot_general(both, block, (((1,), (1,)), ((), ())), preferred_element_type=F32)
            total = part if total is None else total + part
        tiles.append(total)
    return jnp.concatenate(tiles, axis=1)


def spread(left, tokens_ref, keep_ref, send_ref, extra, tile=256):
    contexts, half, width = keep_ref.shape
    for p in range(contexts):
        for at in range(0, width, tile):
            block = tokens_ref[:, columns_of(contexts, p, width, at, tile)]
            part = jnp.dot(left, block, preferred_element_type=F32)
            keep_ref[p, :, at : at + tile] = part[:half]
            send_ref[p, :, at : at + tile] = part[half:].astype(BF16)
        if extra is not None:
            send_ref[p, :, width:] = extra


def pool_kernel(length_ref, own_ref, other_ref, tokens_ref, keep_ref, send_ref, peak_ref, w_ref):
    scores = project(own_ref, other_ref, tokens_ref, keep_ref.shape[2])
    shard = lax.axis_index("ctx") * lax.axis_size("cls") + lax.axis_index("cls")
    valid = lax.broadcasted_iota(jnp.int32, scores.shape, 1) < length_ref[0] - shard * scores.shape[1]
    peak = jnp.max(jnp.where(valid, scores, MASKED), axis=1, keepdims=True)
    weights = jnp.where(valid, jnp.exp(scores - peak), 0.0)
    w_ref[...] = weights
    peak_ref[...] = jnp.broadcast_to(peak, peak_ref.shape)
    half = keep_ref.shape[1]
    spread(weights.astype(BF16), tokens_ref, keep_ref, send_ref, into_lanes([peak[half:]], half))


def grad_kernel(scale, classes, own_ref, other_ref, tokens_ref, w_ref, peak_ref, keep_ref, send_ref, loss_ref):
    width = keep_ref.shape[2]
    projected = project(own_ref, other_ref, tokens_ref, width)
    own, other = own_ref[0], other_ref[0]
    top = jnp.concatenate([from_lanes(own, width, 0), from_lanes(other, width, 0)], axis=0)
    weights = w_ref[...] * jnp.exp(peak_ref[:, :1] - top)
    spread((weights * projected).astype(BF16), tokens_ref, keep_ref, send_ref, None)
    rows = classes // 2
    each = own.shape[0] // rows
    sums = []
    for block in (own, other):
        column = from_lanes(block, width, 1)
        level = [column[i * each : i * each + 1] for i in range(rows)]
        while len(level) > 1:
            level = [a + b for a, b in zip(level[::2], level[1::2])]
        sums.append(level[0])
    loss_ref[...] = (sums[0] + sums[1]) * scale


def total_of(keep, peak, received, width):
    if peak is None:
        for block in received:
            keep = keep + block.astype(F32)
        return keep, None
    others = [from_lanes(block, width, 0) for block in received]
    top = peak
    for other in others:
        top = jnp.maximum(top, other)
    keep = keep * jnp.exp(peak - top)
    for block, other in zip(received, others):
        keep = keep + block[:, :width].astype(F32) * jnp.exp(other - top)
    return keep, top


def put(ref, p, total, top, width):
    ref[p, :, :width] = total.astype(BF16)
    if top is not None:
        ref[p, :, width:] = into_lanes([top], total.shape[0])


def core_kernel(peaks, steps, *refs):
    keep_ref, recv_ref, *refs = refs
    peak = refs.pop(0)[: keep_ref.shape[1], :1] if peaks else None
    top_ref = refs.pop() if peaks else None
    width = keep_ref.shape[2]
    blocks, rows = refs[0].shape[:2]
    for i in range(2):
        for b in range(blocks):
            p = i * blocks + b
            total, top = total_of(keep_ref[p], peak, [recv_ref[p]], width)
            for ref, (_, k) in [(r, step) for r, step in zip(refs, steps) if step[0] == i]:
                at = k // 2 * rows
                part = total[at : at + rows]
                if ref is refs[0]:
                    ref[b] = part
                else:
                    put(ref, b, part, top[at : at + rows] if peaks else None, width)
    if peaks:
        top_ref[...] = jnp.broadcast_to(top[:rows], top_ref.shape)


def near_sum_kernel(peaks, count, steps, *refs):
    keep_ref, *refs = refs
    received, refs = refs[:count], list(refs[count:])
    peak = refs.pop(0)[:, :1] if peaks else None
    top_ref = refs.pop() if peaks else None
    width = keep_ref.shape[2]
    for p in range(keep_ref.shape[0]):
        total, top = total_of(keep_ref[p], peak, [ref[p] for ref in received], width)
        if p == 0:
            refs[0][0] = total
        else:
            put(refs[steps.index((2 * p, 0)) + 1], 0, total, top, width)
    if peaks:
        top_ref[...] = jnp.broadcast_to(top, top_ref.shape)


def scatter_sum(keep, send, peak):
    peaks = peak is not None
    contexts, half, width = keep.shape
    lanes = send.shape[2]
    near, far = near_steps(), far_steps()
    across = (len(near) + 1) // 2
    blocks, rows = contexts // 2, half // across
    top_out = [((rows, LANES), F32)] if peaks else []
    outs = [((blocks, rows, width), F32)] + [((blocks, rows, lanes), BF16)] * len(near) + top_out
    args = [keep, swap(send, 0, 1)] + ([peak] if peaks else [])
    out = call(functools.partial(core_kernel, peaks, [(0, 0)] + near), outs, "core_sum", args)
    received = [swap(s, *step) for s, step in zip(out[1:], near)]
    outs = [((1, rows, width), F32)] + [((1, rows, lanes), BF16)] * len(far) + top_out
    args = [out[0], *received] + (out[-1:] if peaks else [])
    out = call(functools.partial(near_sum_kernel, peaks, len(received), far), outs, "near_sum", args)
    received = [swap(s, *step) for s, step in zip(out[1:], far)]
    return [out[0], *received] + (out[-1:] if peaks else [])


def far_sum_kernel(*refs):
    keep_ref, *received, out_ref = refs
    out_ref[...] = total_of(keep_ref[0], None, [ref[0] for ref in received], keep_ref.shape[2])[0]


def head_mask(shape, attributes):
    row = lax.broadcasted_iota(jnp.int32, shape, 0)
    column = lax.broadcasted_iota(jnp.int32, shape, 1)
    return column // attributes == row


def head_sums_kernel(*refs):
    keep_ref, *received, peak_ref, gain_ref, weight_ref, sums_ref, pooled_ref, top_ref = refs
    pooled, top = total_of(keep_ref[0], peak_ref[:, :1], [ref[0] for ref in received], keep_ref.shape[2])
    pooled_ref[...] = pooled
    top_ref[...] = jnp.broadcast_to(top, top_ref.shape)
    scaled_b = (pooled * gain_ref[...]).astype(BF16)
    product = jnp.dot(scaled_b, weight_ref[...], preferred_element_type=F32)
    mask = head_mask(product.shape, product.shape[1] // product.shape[0])
    squares = jnp.sum(pooled * pooled, axis=1, keepdims=True)
    product_flat = jnp.sum(jnp.where(mask, product, 0.0), axis=0, keepdims=True)
    squares_flat = jnp.sum(jnp.where(mask, squares, 0.0), axis=0, keepdims=True)
    sums_ref[0:1, :] = product_flat
    sums_ref[1:2, :] = squares_flat


def tree_sum_kernel(*refs):
    level = [ref[...] for ref in refs[:-1]]
    while len(level) > 1:
        level = [a + b for a, b in zip(level[::2], level[1::2])]
    refs[-1][...] = level[0]


def head_grads_kernel(
    full_width, sums_ref, other_sums_ref, pooled_ref, top_ref, gain_ref, weight_ref, bias_ref, label_ref, bias_grad_ref, copy_ref, grad_ref, normed_ref
):
    pooled, gain = pooled_ref[...], gain_ref[...]
    heads, width = pooled.shape
    columns = sums_ref.shape[1]
    sums = sums_ref[...] + other_sums_ref[...]
    mask = head_mask((heads, columns), columns // heads)
    inverse_flat = lax.rsqrt(sums[1:2] / full_width + 1e-05)
    inverse_rms = jnp.max(jnp.where(mask, inverse_flat, 0.0), axis=1, keepdims=True)
    product = inverse_flat * sums[0:1]
    logits = product + bias_ref[...]
    target = label_ref[...].astype(F32)
    losses = jnp.maximum(logits, 0.0) + jnp.log1p(jnp.exp(-jnp.abs(logits))) - target * logits
    loss = jnp.sum(losses, axis=1, keepdims=True)
    bias_grad = jax.nn.sigmoid(logits) - target
    bias_grad_ref[...] = bias_grad
    copy_ref[...] = bias_grad
    by_head = jnp.where(mask, bias_grad, 0.0)
    high = by_head.astype(BF16)
    low = (by_head - high.astype(F32)).astype(BF16)
    both = jnp.concatenate([high, low], axis=0)
    back = lax.dot_general(both, weight_ref[...], (((1,), (1,)), ((), ())), preferred_element_type=F32)
    normed_grad = (back[:heads] + back[heads:]) * gain
    inner = jnp.sum(by_head * product, axis=1, keepdims=True) / full_width
    unit = pooled * inverse_rms
    grad_ref[:, :width] = (inverse_rms * (normed_grad - unit * inner)).astype(BF16)
    grad_ref[:, width:] = into_lanes([top_ref[:, :1], jnp.broadcast_to(loss, (heads, 1))], heads)
    normed_ref[...] = unit * gain


def head_weight_grad_kernel(attributes, normed_ref, bias_grad_ref, out_ref, done_ref):
    heads = normed_ref.shape[0]
    columns = out_ref.shape[1]
    parts = jnp.concatenate(pieces(normed_ref[...]), axis=0)
    row = lax.broadcasted_iota(jnp.int32, (3 * heads, columns), 0) % heads
    column = pl.program_id(0) * columns + lax.broadcasted_iota(jnp.int32, (3 * heads, columns), 1)
    ones = jnp.where(column // attributes == row, 1.0, 0.0).astype(BF16)
    normed = lax.dot_general(parts, ones, (((0,), (0,)), ((), ())), preferred_element_type=F32)
    out_ref[...] = normed * bias_grad_ref[...]
    done_ref[...] = jnp.zeros_like(done_ref)


def head_weight_grad(normed, bias_grad):
    rows, width = normed.shape
    columns = bias_grad.shape[1]
    block = columns // 4
    return pl.pallas_call(
        functools.partial(head_weight_grad_kernel, columns // rows),
        out_shape=[jax.ShapeDtypeStruct((width, columns), F32), jax.ShapeDtypeStruct((8, LANES), F32)],
        grid=(columns // block,),
        in_specs=[
            pl.BlockSpec((rows, width), lambda i: (0, 0)),
            pl.BlockSpec((1, block), lambda i: (0, i)),
        ],
        out_specs=[pl.BlockSpec((width, block), lambda i: (0, i)), pl.BlockSpec((8, LANES), lambda i: (0, 0))],
        compiler_params=pltpu.CompilerParams(vmem_limit_bytes=16 * MIB),
        cost_estimate=pl.CostEstimate(flops=6 * rows * width * columns, bytes_accessed=4 * width * columns, transcendentals=0),
        name="head_weight_grad",
    )(normed, bias_grad)


def shards(tokens, doc_length, queries, norm_gain, head_weight, head_bias, labels):
    contexts, classes = lax.axis_size("ctx"), lax.axis_size("cls")
    token_count = tokens.shape[0]
    rows, width = queries.shape
    full_width = width * contexts
    heads = rows * classes
    half = heads // 2
    columns = labels.shape[0]
    held, queries_here = load(tokens, queries)
    own, other = gather(queries, queries_here)
    keep, send, own_peak, weights = call(
        pool_kernel,
        [
            ((contexts, half, width), F32),
            ((contexts, half, width + LANES), BF16),
            ((heads, LANES), F32),
            ((heads, token_count), F32),
        ],
        "pool",
        [doc_length, own, other, held],
        smem_args=(0,),
        limit=16,
    )
    parts = scatter_sum(keep, send, own_peak)
    gain = norm_gain[None, :]
    sums, pooled, top = call(
        head_sums_kernel,
        [((2, columns), F32), ((rows, width), F32), ((rows, LANES), F32)],
        "head_sums",
        [*parts, gain, head_weight],
    )
    far_sums = [swap(sums, *step) for step in far_steps()[::-1]]
    (sums,) = call(tree_sum_kernel, [((2, columns), F32)], "tree_sum", [sums, *far_sums])
    bias_grad, bias_grad_here, pooled_grad, normed = call(
        functools.partial(head_grads_kernel, full_width),
        [((1, columns), F32), ((1, columns), F32), ((rows, width + LANES), BF16), ((rows, width), F32)],
        "head_grads",
        [sums, swap(sums, 1, 0), pooled, top, gain, head_weight, head_bias[None, :], labels[None, :]],
    )
    head_grad, done = head_weight_grad(normed, bias_grad_here)
    own, other = gather(pooled_grad, after=(done,))
    keep, send, loss = call(
        functools.partial(grad_kernel, 1.0 / (columns * classes), classes),
        [((contexts, half, width), F32), ((contexts, half, width), BF16), ((1, 1), F32)],
        "grad",
        [own, other, held, weights, own_peak],
        limit=16,
    )
    (query_grad,) = call(far_sum_kernel, [((rows, width), F32)], "far_sum", scatter_sum(keep, send, None))
    return (loss.reshape(()), query_grad, head_grad, bias_grad.reshape(-1))


def solution(mesh):
    return jax.shard_map(
        shards,
        mesh=mesh,
        in_specs=(
            P(("ctx", "cls"), None),
            P(),
            P("cls", "ctx"),
            P("ctx"),
            P("ctx", "cls"),
            P("cls"),
            P("cls"),
        ),
        out_specs=(P(), P("cls", "ctx"), P("ctx", "cls"), P("cls")),
        check_vma=False,
    )
```

```python
import functools

import jax
import jax.numpy as jnp
from jax import lax
from jax.experimental import pallas as pl
from jax.experimental.pallas import tpu as pltpu
from jax.sharding import PartitionSpec as P

F32 = jnp.float32
BF16 = jnp.bfloat16
LANES = 128
MASKED = -1e30
MIB = 1024 * 1024


def swap(x, ctx_bits, cls_bits):
    contexts, classes = lax.axis_size("ctx"), lax.axis_size("cls")
    pairs = [
        (c * classes + k, (c ^ ctx_bits) * classes + (k ^ cls_bits)) for c in range(contexts) for k in range(classes)
    ]
    return lax.ppermute(x, ("ctx", "cls"), pairs)


def far_steps():
    return [(2 * j, 0) for j in reversed(range(1, lax.axis_size("ctx") // 2))]


def near_steps():
    steps = [(i, 2 * k) for i in range(2) for k in range(lax.axis_size("cls") // 2) if i or k]
    return sorted(steps, key=lambda step: not (step[0] and step[1]))


def call(kernel, outs, name, args, scratch=(), hbm_args=(), smem_args=(), limit=16, cost=None):
    def spec(i):
        if i in hbm_args:
            return pl.BlockSpec(memory_space=pltpu.HBM)
        if i in smem_args:
            return pl.BlockSpec(memory_space=pltpu.SMEM)
        return pl.BlockSpec(memory_space=pltpu.VMEM)

    run = pl.pallas_call(
        kernel,
        out_shape=[jax.ShapeDtypeStruct(s, d) for s, d in outs],
        in_specs=[spec(i) for i in range(len(args))],
        out_specs=[pl.BlockSpec(memory_space=pltpu.VMEM)] * len(outs),
        scratch_shapes=list(scratch),
        compiler_params=pltpu.CompilerParams(vmem_limit_bytes=limit * MIB),
        cost_estimate=cost,
        name=name,
    )
    return list(run(*args))


def stack_kernel(*refs):
    out_ref = refs[-1]
    for at, ref in enumerate(refs[:-1]):
        out_ref[at] = ref[...].reshape(out_ref.shape[1:])


def gather(block, local=None):
    far = [swap(block, *step) for step in far_steps()[::-1]]
    rows, width = block.shape
    (held,) = call(
        stack_kernel, [((len(far) + 1, rows, width), block.dtype)], "stack", [block if local is None else local, *far]
    )
    parts = {step: swap(held, *step) for step in near_steps()[::-1]}
    parts[0, 0] = held
    other = {step: swap(part, 0, 1) for step, part in parts.items()}
    steps = sorted(parts)
    return [[group[step] for group in (parts, other) for step in steps if step[0] == i] for i in range(2)]


def pieces(x):
    high = x.astype(BF16)
    rest = x - high.astype(F32)
    middle = rest.astype(BF16)
    return high, middle, (rest - middle.astype(F32)).astype(BF16)


def into_lanes(columns, rows):
    lane = lax.broadcasted_iota(jnp.int32, (rows, LANES), 1)
    out = jnp.zeros((rows, LANES), F32)
    for i, column in enumerate(columns):
        for j, piece in enumerate(pieces(column)):
            out = jnp.where(lane == 3 * i + j, piece.astype(F32), out)
    return out.astype(BF16)


def from_lanes(block, width, i):
    at = width + 3 * i
    block = block.astype(F32)
    return block[:, at : at + 1] + (block[:, at + 1 : at + 2] + block[:, at + 2 : at + 3])


def load_kernel(half, tokens_ref, *refs):
    count = (len(refs) - 2) // 2
    others, held_ref, copies_of, sems = refs[:count], refs[count], refs[count + 1 : -1], refs[-1]
    width = held_ref.shape[2]
    copies = [pltpu.make_async_copy(src, dst, sems.at[i]) for i, (src, dst) in enumerate(zip(others, copies_of))]
    for j in range(held_ref.shape[0]):
        start = pl.multiple_of((lax.axis_index("ctx") ^ half ^ (2 * j)) * width, LANES)
        copies.append(
            pltpu.make_async_copy(tokens_ref.at[:, pl.ds(start, width)], held_ref.at[j], sems.at[count + j])
        )
    for copy in copies:
        copy.start()
    for copy in copies:
        copy.wait()


def load(half, width, tokens, *others):
    rows, full_width = tokens.shape
    blocks = full_width // width // 2
    outs = [pltpu.VMEM((blocks, rows, width), tokens.dtype)] + [pltpu.VMEM(x.shape, x.dtype) for x in others]
    run = pl.pallas_call(
        functools.partial(load_kernel, half),
        out_shape=outs,
        in_specs=[pl.BlockSpec(memory_space=pltpu.HBM)] * (1 + len(others)),
        out_specs=[pl.BlockSpec(memory_space=pltpu.VMEM)] * len(outs),
        scratch_shapes=[pltpu.SemaphoreType.DMA((blocks + len(others),))],
        compiler_params=pltpu.CompilerParams(vmem_limit_bytes=16 * MIB),
        name="load",
    )
    return run(*[pltpu.with_memory_space_constraint(x, pltpu.HBM) for x in (tokens, *others)])


def project(parts, held_ref, tile=256):
    blocks, token_count, width = held_ref.shape
    tiles = []
    for at in range(0, token_count, tile):
        total = None
        for j in range(blocks):
            left = jnp.concatenate([ref[j] for ref in parts], axis=0)[:, :width]
            block = held_ref[j, at : at + tile, :]
            part = lax.dot_general(left, block, (((1,), (1,)), ((), ())), preferred_element_type=F32)
            total = part if total is None else total + part
        tiles.append(total)
    return jnp.concatenate(tiles, axis=1)


def spread(left, held_ref, keep_ref, send_ref, extra, tile=256):
    blocks, half, width = keep_ref.shape
    for j in range(blocks):
        for at in range(0, width, tile):
            part = jnp.dot(left, held_ref[j, :, at : at + tile], preferred_element_type=F32)
            keep_ref[j, :, at : at + tile] = part[:half]
            send_ref[j, :, at : at + tile] = part[half:].astype(BF16)
        if extra is not None:
            send_ref[j, :, width:] = extra


def project_kernel(count, *refs):
    refs[-1][...] = project(refs[:count], refs[count])


def peak_lanes(peak, half):
    return into_lanes([peak[half:, :1]], half)


def pool_kernel(count, length_ref, *refs):
    parts, refs = refs[:count], refs[count:]
    part_ref, held_ref, keep_ref, send_ref, peak_ref, w_ref, left_ref = refs
    scores = part_ref[...] + project(parts, held_ref)
    shard = lax.axis_index("ctx") * lax.axis_size("cls") + lax.axis_index("cls")
    valid = lax.broadcasted_iota(jnp.int32, scores.shape, 1) < length_ref[0] - shard * scores.shape[1]
    peak = jnp.max(jnp.where(valid, scores, MASKED), axis=1, keepdims=True)
    weights = jnp.where(valid, jnp.exp(scores - peak), 0.0)
    left = weights.astype(BF16)
    w_ref[...] = weights
    left_ref[...] = left
    peak_ref[...] = jnp.broadcast_to(peak, peak_ref.shape)
    spread(left, held_ref, keep_ref, send_ref, peak_lanes(peak, keep_ref.shape[1]))


def pool_rest_kernel(left_ref, peak_ref, held_ref, keep_ref, send_ref):
    spread(left_ref[...], held_ref, keep_ref, send_ref, peak_lanes(peak_ref[...], keep_ref.shape[1]))


def grad_kernel(scale, count, *refs):
    parts, refs = refs[:count], refs[count:]
    part_ref, held_ref, w_ref, peak_ref, keep_ref, send_ref, left_ref, loss_ref = refs
    width = held_ref.shape[2]
    projected = part_ref[...] + project(parts, held_ref)
    blocks = [ref[0] for ref in parts]
    top = jnp.concatenate([from_lanes(block, width, 0) for block in blocks], axis=0)
    weights = w_ref[...] * jnp.exp(peak_ref[:, :1] - top)
    left = (weights * projected).astype(BF16)
    left_ref[...] = left
    spread(left, held_ref, keep_ref, send_ref, None)
    loss_ref[...] = tree_sum([from_lanes(block, width, 1)[:1] for block in blocks]) * scale


def grad_rest_kernel(left_ref, held_ref, keep_ref, send_ref):
    spread(left_ref[...], held_ref, keep_ref, send_ref, None)


def total_of(keep, peak, received, width):
    if peak is None:
        for block in received:
            keep = keep + block.astype(F32)
        return keep, None
    others = [from_lanes(block, width, 0) for block in received]
    top = peak
    for other in others:
        top = jnp.maximum(top, other)
    keep = keep * jnp.exp(peak - top)
    for block, other in zip(received, others):
        keep = keep + block[:, :width].astype(F32) * jnp.exp(other - top)
    return keep, top


def put(ref, p, total, top, width):
    ref[p, :, :width] = total.astype(BF16)
    if top is not None:
        ref[p, :, width:] = into_lanes([top], total.shape[0])


def core_kernel(peaks, first, *refs):
    keep_ref, recv_ref, *refs = refs
    peak = refs.pop(0)[: keep_ref.shape[1], :1] if peaks else None
    refs = refs[1:] if first else refs
    top_ref = refs.pop() if peaks and first else None
    width = keep_ref.shape[2]
    rows = refs[0].shape[1]
    for j in range(keep_ref.shape[0]):
        total, top = total_of(keep_ref[j], peak, [recv_ref[j]], width)
        for k, ref in enumerate(refs):
            at = slice(k * rows, (k + 1) * rows)
            if first and k == 0:
                ref[j] = total[at]
            else:
                put(ref, j, total[at], top[at] if peaks else None, width)
    if peaks and first:
        top_ref[...] = jnp.broadcast_to(top[:rows], top_ref.shape)


def near_sum_kernel(peaks, count, steps, after, *refs):
    keep_ref, *refs = refs
    received, refs = refs[:count], refs[count:]
    peak = refs.pop(0)[:, :1] if peaks else None
    refs = refs[after:]
    top_ref = refs.pop() if peaks else None
    width = keep_ref.shape[2]
    for p in range(keep_ref.shape[0]):
        total, top = total_of(keep_ref[p], peak, [ref[p] for ref in received], width)
        if p == 0:
            refs[0][0] = total
        else:
            put(refs[steps.index((2 * p, 0)) + 1], 0, total, top, width)
    if peaks:
        top_ref[...] = jnp.broadcast_to(top, top_ref.shape)


def scatter_sum(halves, peak, after=()):
    peaks = peak is not None
    near, far = near_steps(), far_steps()
    across = (len(near) + 1) // 2
    blocks, half, width = halves[0][0].shape
    lanes = halves[0][1].shape[2]
    rows = half // across
    top_out = [((rows, LANES), F32)] if peaks else []
    parts = {}
    for i in reversed(range(2)):
        keep, send = halves[i]
        outs = [((blocks, rows, lanes), BF16)] * across
        if i == 0:
            outs = [((blocks, rows, width), F32)] + outs[1:] + top_out
        args = [keep, swap(send, 0, 1)] + ([peak] if peaks else [])
        if i == 0:
            args.append(parts[1, 0])
        out = call(functools.partial(core_kernel, peaks, i == 0), outs, "core_sum", args)
        parts.update({(i, 2 * k): out[k] for k in range(across)})
    received = [swap(parts[step], *step) for step in near]
    outs = [((1, rows, width), F32)] + [((1, rows, lanes), BF16)] * len(far) + top_out
    args = [parts[0, 0], *received] + (out[-1:] if peaks else []) + list(after)
    out = call(functools.partial(near_sum_kernel, peaks, len(received), far, len(after)), outs, "near_sum", args)
    received = [swap(x, *step) for x, step in zip(out[1:], far)]
    return [out[0], *received] + (out[-1:] if peaks else [])


def far_sum_kernel(*refs):
    keep_ref, *received, out_ref = refs
    out_ref[...] = total_of(keep_ref[0], None, [ref[0] for ref in received], keep_ref.shape[2])[0]


def head_mask(shape, attributes):
    row = lax.broadcasted_iota(jnp.int32, shape, 0)
    column = lax.broadcasted_iota(jnp.int32, shape, 1)
    return column // attributes == row


def head_sums_kernel(*refs):
    keep_ref, *received, peak_ref, gain_ref, weight_ref, sums_ref, pooled_ref, top_ref = refs
    pooled, top = total_of(keep_ref[0], peak_ref[:, :1], [ref[0] for ref in received], keep_ref.shape[2])
    pooled_ref[...] = pooled
    top_ref[...] = jnp.broadcast_to(top, top_ref.shape)
    scaled_b = (pooled * gain_ref[...]).astype(BF16)
    product = jnp.dot(scaled_b, weight_ref[...], preferred_element_type=F32)
    mask = head_mask(product.shape, product.shape[1] // product.shape[0])
    squares = jnp.sum(pooled * pooled, axis=1, keepdims=True)
    product_flat = jnp.sum(jnp.where(mask, product, 0.0), axis=0, keepdims=True)
    squares_flat = jnp.sum(jnp.where(mask, squares, 0.0), axis=0, keepdims=True)
    sums_ref[0:1, :] = product_flat
    sums_ref[1:2, :] = squares_flat


def tree_sum(level):
    while len(level) > 1:
        level = [a + b for a, b in zip(level[::2], level[1::2])]
    return level[0]


def head_grads_kernel(full_width, count, *refs):
    pooled_ref, top_ref, gain_ref, weight_ref, bias_ref, label_ref = refs[count : count + 6]
    bias_grad_ref, copy_ref, grad_ref, normed_ref = refs[count + 6 :]
    pooled, gain = pooled_ref[...], gain_ref[...]
    heads, width = pooled.shape
    columns = bias_ref.shape[1]
    sums = tree_sum([ref[...] for ref in refs[:count]])
    mask = head_mask((heads, columns), columns // heads)
    inverse_flat = lax.rsqrt(sums[1:2] / full_width + 1e-05)
    inverse_rms = jnp.max(jnp.where(mask, inverse_flat, 0.0), axis=1, keepdims=True)
    product = inverse_flat * sums[0:1]
    logits = product + bias_ref[...]
    target = label_ref[...].astype(F32)
    losses = jnp.maximum(logits, 0.0) + jnp.log1p(jnp.exp(-jnp.abs(logits))) - target * logits
    loss = jnp.sum(losses, axis=1, keepdims=True)
    bias_grad = jax.nn.sigmoid(logits) - target
    bias_grad_ref[...] = bias_grad
    copy_ref[...] = bias_grad
    by_head = jnp.where(mask, bias_grad, 0.0)
    high = by_head.astype(BF16)
    low = (by_head - high.astype(F32)).astype(BF16)
    both = jnp.concatenate([high, low], axis=0)
    back = lax.dot_general(both, weight_ref[...], (((1,), (1,)), ((), ())), preferred_element_type=F32)
    normed_grad = (back[:heads] + back[heads:]) * gain
    inner = jnp.sum(by_head * product, axis=1, keepdims=True) / full_width
    unit = pooled * inverse_rms
    grad_ref[:, :width] = (inverse_rms * (normed_grad - unit * inner)).astype(BF16)
    grad_ref[:, width:] = into_lanes([top_ref[:, :1], jnp.broadcast_to(loss, (heads, 1))], heads)
    normed_ref[...] = unit * gain


def head_weight_grad_kernel(attributes, normed_ref, bias_grad_ref, out_ref, done_ref):
    heads = normed_ref.shape[0]
    columns = out_ref.shape[1]
    parts = jnp.concatenate(pieces(normed_ref[...]), axis=0)
    row = lax.broadcasted_iota(jnp.int32, (3 * heads, columns), 0) % heads
    column = pl.program_id(0) * columns + lax.broadcasted_iota(jnp.int32, (3 * heads, columns), 1)
    ones = jnp.where(column // attributes == row, 1.0, 0.0).astype(BF16)
    normed = lax.dot_general(parts, ones, (((0,), (0,)), ((), ())), preferred_element_type=F32)
    out_ref[...] = normed * bias_grad_ref[...]
    done_ref[...] = jnp.zeros_like(done_ref)


def head_weight_grad(normed, bias_grad):
    rows, width = normed.shape
    columns = bias_grad.shape[1]
    block = columns // 4
    return pl.pallas_call(
        functools.partial(head_weight_grad_kernel, columns // rows),
        out_shape=[jax.ShapeDtypeStruct((width, columns), F32), jax.ShapeDtypeStruct((8, LANES), F32)],
        grid=(columns // block,),
        in_specs=[
            pl.BlockSpec((rows, width), lambda i: (0, 0)),
            pl.BlockSpec((1, block), lambda i: (0, i)),
        ],
        out_specs=[pl.BlockSpec((width, block), lambda i: (0, i)), pl.BlockSpec((8, LANES), lambda i: (0, 0))],
        compiler_params=pltpu.CompilerParams(vmem_limit_bytes=16 * MIB),
        cost_estimate=pl.CostEstimate(flops=6 * rows * width * columns, bytes_accessed=4 * width * columns, transcendentals=0),
        name="head_weight_grad",
    )(normed, bias_grad)


def shards(tokens, doc_length, queries, norm_gain, head_weight, head_bias, labels):
    contexts, classes = lax.axis_size("ctx"), lax.axis_size("cls")
    token_count = tokens.shape[0]
    rows, width = queries.shape
    full_width = width * contexts
    heads = rows * classes
    half = heads // 2
    columns = labels.shape[0]
    blocks = contexts // 2
    pair = [((blocks, half, width), F32), ((blocks, half, width + LANES), BF16)]
    product = ((heads, token_count), F32)
    cost = pl.CostEstimate(flops=256 * token_count * full_width, bytes_accessed=0, transcendentals=0)

    def project_half(parts, after=()):
        kernel = functools.partial(project_kernel, len(parts))
        return call(kernel, [product], "project", [*parts, held_a, *after], cost=cost)[0]

    held_a, queries_here = load(0, width, tokens, queries)
    held_b, gain = load(1, width, tokens, norm_gain[None, :])
    first, second = gather(queries, queries_here)
    part = project_half(first, [gain])
    keep_b, send_b, own_peak, weights, left = call(
        functools.partial(pool_kernel, classes),
        [*pair, ((heads, LANES), F32), product, ((heads, token_count), BF16)],
        "pool",
        [doc_length, *second, part, held_b],
        smem_args=(0,),
        cost=cost,
    )
    half_a = call(pool_rest_kernel, pair, "pool_rest", [left, own_peak, held_a], cost=cost)
    parts = scatter_sum([half_a, (keep_b, send_b)], own_peak)
    sums, pooled, top = call(
        head_sums_kernel,
        [((2, columns), F32), ((rows, width), F32), ((rows, LANES), F32)],
        "head_sums",
        [*parts, gain, head_weight],
    )
    all_sums = [sums] + [swap(sums, bits, 0) for bits in range(1, contexts)]
    bias_grad, bias_grad_here, pooled_grad, normed = call(
        functools.partial(head_grads_kernel, full_width, contexts),
        [((1, columns), F32), ((1, columns), F32), ((rows, width + LANES), BF16), ((rows, width), F32)],
        "head_grads",
        [*all_sums, pooled, top, gain, head_weight, head_bias[None, :], labels[None, :]],
    )
    head_grad, done = head_weight_grad(normed, bias_grad_here)
    first, second = gather(pooled_grad)
    part = project_half(first)
    pair = [((blocks, half, width), F32), ((blocks, half, width), BF16)]
    keep_b, send_b, left, loss = call(
        functools.partial(grad_kernel, 1.0 / (columns * classes), classes),
        [*pair, ((heads, token_count), BF16), ((1, 1), F32)],
        "grad",
        [*second, part, held_b, weights, own_peak],
        cost=cost,
    )
    half_a = call(grad_rest_kernel, pair, "grad_rest", [left, held_a], cost=cost)
    parts = scatter_sum([half_a, (keep_b, send_b)], None, after=(done,))
    (query_grad,) = call(far_sum_kernel, [((rows, width), F32)], "far_sum", parts)
    return (loss.reshape(()), query_grad, head_grad, bias_grad.reshape(-1))


def solution(mesh):
    return jax.shard_map(
        shards,
        mesh=mesh,
        in_specs=(
            P(("ctx", "cls"), None),
            P(),
            P("cls", "ctx"),
            P("ctx"),
            P("ctx", "cls"),
            P("cls"),
            P("cls"),
        ),
        out_specs=(P(), P("cls", "ctx"), P("ctx", "cls"), P("cls")),
        check_vma=False,
    )
```

```python
import functools

import jax
import jax.numpy as jnp
from jax import lax
from jax.experimental import pallas as pl
from jax.experimental.pallas import tpu as pltpu
from jax.sharding import PartitionSpec as P

F32 = jnp.float32
BF16 = jnp.bfloat16
LANES = 128
MASKED = -1e30
MIB = 1024 * 1024


def swap(x, ctx_bits, cls_bits):
    contexts, classes = lax.axis_size("ctx"), lax.axis_size("cls")
    pairs = [
        (c * classes + k, (c ^ ctx_bits) * classes + (k ^ cls_bits)) for c in range(contexts) for k in range(classes)
    ]
    return lax.ppermute(x, ("ctx", "cls"), pairs)


def far_steps():
    return [(2 * j, 0) for j in reversed(range(1, lax.axis_size("ctx") // 2))]


def near_steps():
    steps = [(i, 2 * k) for i in range(2) for k in range(lax.axis_size("cls") // 2) if i or k]
    return sorted(steps, key=lambda step: (not (step[0] and step[1]), not step[0]))


def call(kernel, outs, name, args, smem_args=(), aliases=None, limit=16, cost=None):
    def spec(i):
        if i in smem_args:
            return pl.BlockSpec(memory_space=pltpu.SMEM)
        return pl.BlockSpec(memory_space=pltpu.VMEM)

    run = pl.pallas_call(
        kernel,
        out_shape=[jax.ShapeDtypeStruct(s, d) for s, d in outs],
        in_specs=[spec(i) for i in range(len(args))],
        out_specs=[pl.BlockSpec(memory_space=pltpu.VMEM)] * len(outs),
        input_output_aliases=aliases or {},
        compiler_params=pltpu.CompilerParams(vmem_limit_bytes=limit * MIB),
        cost_estimate=cost,
        name=name,
    )
    return list(run(*args))


def stack_kernel(*refs):
    out_ref = refs[-1]
    for at, ref in enumerate(refs[:-1]):
        out_ref[at] = ref[...].reshape(out_ref.shape[1:])


def gather(block, local=None):
    far = [swap(block, *step) for step in far_steps()[::-1]]
    rows, width = block.shape
    (held,) = call(
        stack_kernel, [((len(far) + 1, rows, width), block.dtype)], "stack", [block if local is None else local, *far]
    )
    parts = {step: swap(held, *step) for step in near_steps()[::-1]}
    parts[0, 0] = held
    other = {step: swap(part, 0, 1) for step, part in parts.items()}
    steps = sorted(parts)
    return [[group[step] for group in (parts, other) for step in steps if step[0] == i] for i in range(2)]


def pieces(x):
    high = x.astype(BF16)
    rest = x - high.astype(F32)
    middle = rest.astype(BF16)
    return high, middle, (rest - middle.astype(F32)).astype(BF16)


def into_lanes(columns, rows):
    lane = lax.broadcasted_iota(jnp.int32, (rows, LANES), 1)
    out = jnp.zeros((rows, LANES), F32)
    for i, column in enumerate(columns):
        for j, piece in enumerate(pieces(column)):
            out = jnp.where(lane == 3 * i + j, piece.astype(F32), out)
    return out.astype(BF16)


def from_lanes(block, width, i):
    at = width + 3 * i
    block = block.astype(F32)
    return block[:, at : at + 1] + (block[:, at + 1 : at + 2] + block[:, at + 2 : at + 3])


def load_kernel(tokens_ref, *refs):
    count = (len(refs) - 3) // 2
    others, halves, copies_of, sems = refs[:count], refs[count : count + 2], refs[count + 2 : -1], refs[-1]
    blocks, _, width = halves[0].shape
    copies = [pltpu.make_async_copy(src, dst, sems.at[i]) for i, (src, dst) in enumerate(zip(others, copies_of))]
    for i in range(2):
        for j in range(blocks):
            start = pl.multiple_of((lax.axis_index("ctx") ^ i ^ (2 * j)) * width, LANES)
            sem = sems.at[count + i * blocks + j]
            copies.append(pltpu.make_async_copy(tokens_ref.at[:, pl.ds(start, width)], halves[i].at[j], sem))
    for copy in copies:
        copy.start()
    for copy in copies:
        copy.wait()


def load(width, tokens, *others):
    rows, full_width = tokens.shape
    blocks = full_width // width // 2
    outs = [pltpu.VMEM((blocks, rows, width), tokens.dtype)] * 2 + [pltpu.VMEM(x.shape, x.dtype) for x in others]
    run = pl.pallas_call(
        load_kernel,
        out_shape=outs,
        in_specs=[pl.BlockSpec(memory_space=pltpu.HBM)] * (1 + len(others)),
        out_specs=[pl.BlockSpec(memory_space=pltpu.VMEM)] * len(outs),
        scratch_shapes=[pltpu.SemaphoreType.DMA((2 * blocks + len(others),))],
        compiler_params=pltpu.CompilerParams(vmem_limit_bytes=16 * MIB),
        name="load",
    )
    return run(*[pltpu.with_memory_space_constraint(x, pltpu.HBM) for x in (tokens, *others)])


def project(parts, held_ref, tile=256):
    blocks, token_count, width = held_ref.shape
    tiles = []
    for at in range(0, token_count, tile):
        total = None
        for j in range(blocks):
            left = jnp.concatenate([ref[j] for ref in parts], axis=0)[:, :width]
            block = held_ref[j, at : at + tile, :]
            part = lax.dot_general(left, block, (((1,), (1,)), ((), ())), preferred_element_type=F32)
            total = part if total is None else total + part
        tiles.append(total)
    return jnp.concatenate(tiles, axis=1)


def spread(left, held_ref, keep_ref, send_ref, extra, tile=256):
    blocks, half, width = keep_ref.shape
    for j in range(blocks):
        for at in range(0, width, tile):
            part = jnp.dot(left, held_ref[j, :, at : at + tile], preferred_element_type=F32)
            keep_ref[j, :, at : at + tile] = part[:half]
            send_ref[j, :, at : at + tile] = part[half:].astype(BF16)
        if extra is not None:
            send_ref[j, :, width:] = extra


def project_kernel(count, *refs):
    refs[-1][...] = project(refs[:count], refs[count])


def peak_lanes(peak, half):
    return into_lanes([peak[half:, :1]], half)


def pool_kernel(count, length_ref, *refs):
    parts, refs = refs[:count], refs[count:]
    part_ref, held_ref, keep_ref, send_ref, peak_ref, w_ref, left_ref = refs
    scores = part_ref[...] + project(parts, held_ref)
    shard = lax.axis_index("ctx") * lax.axis_size("cls") + lax.axis_index("cls")
    valid = lax.broadcasted_iota(jnp.int32, scores.shape, 1) < length_ref[0] - shard * scores.shape[1]
    peak = jnp.max(jnp.where(valid, scores, MASKED), axis=1, keepdims=True)
    weights = jnp.where(valid, jnp.exp(scores - peak), 0.0)
    left = weights.astype(BF16)
    w_ref[...] = weights
    left_ref[...] = left
    peak_ref[...] = jnp.broadcast_to(peak, peak_ref.shape)
    spread(left, held_ref, keep_ref, send_ref, peak_lanes(peak, keep_ref.shape[1]))


def pool_rest_kernel(left_ref, peak_ref, held_ref, keep_ref, send_ref):
    spread(left_ref[...], held_ref, keep_ref, send_ref, peak_lanes(peak_ref[...], keep_ref.shape[1]))


def grad_kernel(scale, count, *refs):
    parts, refs = refs[:count], refs[count:]
    part_ref, held_ref, w_ref, peak_ref, keep_ref, send_ref, left_ref, loss_ref = refs
    width = held_ref.shape[2]
    projected = part_ref[...] + project(parts, held_ref)
    blocks = [ref[0] for ref in parts]
    top = jnp.concatenate([from_lanes(block, width, 0) for block in blocks], axis=0)
    weights = w_ref[...] * jnp.exp(peak_ref[:, :1] - top)
    left = (weights * projected).astype(BF16)
    left_ref[...] = left
    spread(left, held_ref, keep_ref, send_ref, None)
    loss_ref[...] = tree_sum([from_lanes(block, width, 1)[:1] for block in blocks]) * scale


def grad_rest_kernel(left_ref, held_ref, keep_ref, send_ref):
    spread(left_ref[...], held_ref, keep_ref, send_ref, None)


def rescaling(peak, received, width):
    if peak is None:
        return None, None
    others = [from_lanes(block, width, 0) for block in received]
    top = peak
    for other in others:
        top = jnp.maximum(top, other)
    return top, [jnp.exp(p - top) for p in [peak, *others]]


def total_of(keep, received, factors):
    total = keep if factors is None else keep * factors[0]
    for i, block in enumerate(received):
        block = block[:, : keep.shape[1]].astype(F32)
        total = total + (block if factors is None else block * factors[i + 1])
    return total


def put(ref, j, total, lanes):
    width = total.shape[1]
    ref[j, :, :width] = total.astype(BF16)
    if lanes is not None:
        ref[j, :, width:] = lanes


def core_kernel(peaks, first, *refs):
    keep_ref, recv_ref, *refs = refs
    peak = refs.pop(0)[: keep_ref.shape[1], :1] if peaks else None
    refs = refs if first else refs[1:-1]
    top_ref = refs.pop() if peaks and first else None
    width = keep_ref.shape[2]
    rows = refs[0].shape[1]
    top, factors = rescaling(peak, [recv_ref[0]], width)
    lanes = into_lanes([top], top.shape[0]) if peaks else None
    for j in range(keep_ref.shape[0]):
        total = total_of(keep_ref[j], [recv_ref[j]], factors)
        for k, ref in enumerate(refs):
            at = slice(k * rows, (k + 1) * rows)
            if first and k == 0:
                ref[j] = total[at]
            else:
                put(ref, j, total[at], lanes[at] if peaks else None)
    if peaks and first:
        top_ref[...] = jnp.broadcast_to(top[:rows], top_ref.shape)


def near_sum_kernel(peaks, count, steps, *refs):
    keep_ref, *refs = refs
    received, refs = refs[:count], refs[count:]
    peak = refs.pop(0)[:, :1] if peaks else None
    top_ref = refs.pop() if peaks else None
    top, factors = rescaling(peak, [ref[0] for ref in received], keep_ref.shape[2])
    lanes = into_lanes([top], top.shape[0]) if peaks else None
    for p in range(keep_ref.shape[0]):
        total = total_of(keep_ref[p], [ref[p] for ref in received], factors)
        if p == 0:
            refs[0][0] = total
        else:
            put(refs[steps.index((2 * p, 0)) + 1], 0, total, lanes)
    if peaks:
        top_ref[...] = jnp.broadcast_to(top, top_ref.shape)


def scatter_sum(halves, peak):
    peaks = peak is not None
    near, far = near_steps(), far_steps()
    across = (len(near) + 1) // 2
    blocks, half, width = halves[0][0].shape
    lanes = halves[0][1].shape[2]
    rows = half // across
    top_out = [((rows, LANES), F32)] if peaks else []
    part = ((blocks, rows, lanes), BF16)
    (keep_a, send_a), (keep_b, send_b) = halves
    args = [keep_b, swap(send_b, 0, 1)] + ([peak] if peaks else []) + [send_a]
    outs = [part] * across + [((blocks, half, lanes), BF16)]
    *parts_b, send_a = call(
        functools.partial(core_kernel, peaks, False), outs, "core_sum", args, aliases={len(args) - 1: across}
    )
    args = [keep_a, swap(send_a, 0, 1)] + ([peak] if peaks else [])
    outs = [((blocks, rows, width), F32)] + [part] * (across - 1) + top_out
    out = call(functools.partial(core_kernel, peaks, True), outs, "core_sum", args)
    parts = {(i, 2 * k): x for i, group in enumerate((out, parts_b)) for k, x in enumerate(group[:across])}
    received = [swap(parts[step], *step) for step in near]
    outs = [((1, rows, width), F32)] + [((1, rows, lanes), BF16)] * len(far) + top_out
    args = [parts[0, 0], *received] + (out[-1:] if peaks else [])
    out = call(functools.partial(near_sum_kernel, peaks, len(received), far), outs, "near_sum", args)
    received = [swap(x, *step) for x, step in zip(out[1:], far)]
    return [out[0], *received] + (out[-1:] if peaks else [])


def far_sum_kernel(*refs):
    keep_ref, *received, out_ref = refs
    out_ref[...] = total_of(keep_ref[0], [ref[0] for ref in received], None)


def head_mask(shape, attributes):
    row = lax.broadcasted_iota(jnp.int32, shape, 0)
    column = lax.broadcasted_iota(jnp.int32, shape, 1)
    return column // attributes == row


def head_sums_kernel(*refs):
    keep_ref, *received, peak_ref, gain_ref, weight_ref, sums_ref, pooled_ref, top_ref = refs
    received = [ref[0] for ref in received]
    top, factors = rescaling(peak_ref[:, :1], received, keep_ref.shape[2])
    pooled = total_of(keep_ref[0], received, factors)
    pooled_ref[...] = pooled
    top_ref[...] = jnp.broadcast_to(top, top_ref.shape)
    scaled_b = (pooled * gain_ref[...]).astype(BF16)
    product = jnp.dot(scaled_b, weight_ref[...], preferred_element_type=F32)
    mask = head_mask(product.shape, product.shape[1] // product.shape[0])
    squares = jnp.sum(pooled * pooled, axis=1, keepdims=True)
    product_flat = jnp.sum(jnp.where(mask, product, 0.0), axis=0, keepdims=True)
    squares_flat = jnp.sum(jnp.where(mask, squares, 0.0), axis=0, keepdims=True)
    sums_ref[0:1, :] = product_flat
    sums_ref[1:2, :] = squares_flat


def tree_sum(level):
    while len(level) > 1:
        level = [a + b for a, b in zip(level[::2], level[1::2])]
    return level[0]


def tree_sum_kernel(*refs):
    refs[-1][...] = tree_sum([ref[...] for ref in refs[:-1]])


def head_grads_kernel(full_width, sums_ref, other_sums_ref, *refs):
    pooled_ref, top_ref, gain_ref, weight_ref, bias_ref, label_ref, *refs = refs
    bias_grad_ref, copy_ref, grad_ref, normed_ref = refs
    pooled, gain = pooled_ref[...], gain_ref[...]
    heads, width = pooled.shape
    columns = bias_ref.shape[1]
    sums = sums_ref[...] + other_sums_ref[...]
    mask = head_mask((heads, columns), columns // heads)
    inverse_flat = lax.rsqrt(sums[1:2] / full_width + 1e-05)
    inverse_rms = jnp.max(jnp.where(mask, inverse_flat, 0.0), axis=1, keepdims=True)
    product = inverse_flat * sums[0:1]
    logits = product + bias_ref[...]
    target = label_ref[...].astype(F32)
    losses = jnp.maximum(logits, 0.0) + jnp.log1p(jnp.exp(-jnp.abs(logits))) - target * logits
    loss = jnp.sum(losses, axis=1, keepdims=True)
    bias_grad = jax.nn.sigmoid(logits) - target
    bias_grad_ref[...] = bias_grad
    copy_ref[...] = bias_grad
    by_head = jnp.where(mask, bias_grad, 0.0)
    high = by_head.astype(BF16)
    low = (by_head - high.astype(F32)).astype(BF16)
    both = jnp.concatenate([high, low], axis=0)
    back = lax.dot_general(both, weight_ref[...], (((1,), (1,)), ((), ())), preferred_element_type=F32)
    normed_grad = (back[:heads] + back[heads:]) * gain
    inner = jnp.sum(by_head * product, axis=1, keepdims=True) / full_width
    unit = pooled * inverse_rms
    grad_ref[:, :width] = (inverse_rms * (normed_grad - unit * inner)).astype(BF16)
    grad_ref[:, width:] = into_lanes([top_ref[:, :1], jnp.broadcast_to(loss, (heads, 1))], heads)
    normed_ref[...] = unit * gain


def head_weight_grad_kernel(attributes, normed_ref, bias_grad_ref, out_ref):
    heads = normed_ref.shape[0]
    columns = out_ref.shape[1]
    parts = jnp.concatenate(pieces(normed_ref[...]), axis=0)
    row = lax.broadcasted_iota(jnp.int32, (3 * heads, columns), 0) % heads
    column = pl.program_id(0) * columns + lax.broadcasted_iota(jnp.int32, (3 * heads, columns), 1)
    ones = jnp.where(column // attributes == row, 1.0, 0.0).astype(BF16)
    normed = lax.dot_general(parts, ones, (((0,), (0,)), ((), ())), preferred_element_type=F32)
    out_ref[...] = normed * bias_grad_ref[...]


def head_weight_grad(normed, bias_grad):
    rows, width = normed.shape
    columns = bias_grad.shape[1]
    block = columns // 4
    return pl.pallas_call(
        functools.partial(head_weight_grad_kernel, columns // rows),
        out_shape=jax.ShapeDtypeStruct((width, columns), F32),
        grid=(columns // block,),
        in_specs=[
            pl.BlockSpec((rows, width), lambda i: (0, 0)),
            pl.BlockSpec((1, block), lambda i: (0, i)),
        ],
        out_specs=pl.BlockSpec((width, block), lambda i: (0, i)),
        compiler_params=pltpu.CompilerParams(vmem_limit_bytes=16 * MIB),
        name="head_weight_grad",
    )(normed, bias_grad)


def shards(tokens, doc_length, queries, norm_gain, head_weight, head_bias, labels):
    contexts, classes = lax.axis_size("ctx"), lax.axis_size("cls")
    token_count = tokens.shape[0]
    rows, width = queries.shape
    full_width = width * contexts
    heads = rows * classes
    half = heads // 2
    columns = labels.shape[0]
    blocks = contexts // 2
    pair = [((blocks, half, width), F32), ((blocks, half, width + LANES), BF16)]
    product = ((heads, token_count), F32)
    cost = pl.CostEstimate(flops=256 * token_count * full_width, bytes_accessed=0, transcendentals=0)

    def project_half(parts):
        return call(functools.partial(project_kernel, len(parts)), [product], "project", [*parts, held_a], cost=cost)[0]

    held_a, held_b, queries_here, gain = load(width, tokens, queries, norm_gain[None, :])
    first, second = gather(queries, queries_here)
    part = project_half(first)
    keep_b, send_b, own_peak, weights, left = call(
        functools.partial(pool_kernel, classes),
        [*pair, ((heads, LANES), F32), product, ((heads, token_count), BF16)],
        "pool",
        [doc_length, *second, part, held_b],
        smem_args=(0,),
        cost=cost,
    )
    half_a = call(pool_rest_kernel, pair, "pool_rest", [left, own_peak, held_a], cost=cost)
    parts = scatter_sum([half_a, (keep_b, send_b)], own_peak)
    sums, pooled, top = call(
        head_sums_kernel,
        [((2, columns), F32), ((rows, width), F32), ((rows, LANES), F32)],
        "head_sums",
        [*parts, gain, head_weight],
    )
    far_sums = [swap(sums, *step) for step in far_steps()[::-1]]
    (sums,) = call(tree_sum_kernel, [((2, columns), F32)], "tree_sum", [sums, *far_sums])
    bias_grad, bias_grad_here, pooled_grad, normed = call(
        functools.partial(head_grads_kernel, full_width),
        [((1, columns), F32), ((1, columns), F32), ((rows, width + LANES), BF16), ((rows, width), F32)],
        "head_grads",
        [sums, swap(sums, 1, 0), pooled, top, gain, head_weight, head_bias[None, :], labels[None, :]],
    )
    head_grad = head_weight_grad(normed, bias_grad_here)
    first, second = gather(pooled_grad)
    part = project_half(first)
    pair = [((blocks, half, width), F32), ((blocks, half, width), BF16)]
    keep_b, send_b, left, loss = call(
        functools.partial(grad_kernel, 1.0 / (columns * classes), classes),
        [*pair, ((heads, token_count), BF16), ((1, 1), F32)],
        "grad",
        [*second, part, held_b, weights, own_peak],
        cost=cost,
    )
    half_a = call(grad_rest_kernel, pair, "grad_rest", [left, held_a], cost=cost)
    parts = scatter_sum([half_a, (keep_b, send_b)], None)
    (query_grad,) = call(far_sum_kernel, [((rows, width), F32)], "far_sum", parts)
    return (loss.reshape(()), query_grad, head_grad, bias_grad.reshape(-1))


def solution(mesh):
    return jax.shard_map(
        shards,
        mesh=mesh,
        in_specs=(
            P(("ctx", "cls"), None),
            P(),
            P("cls", "ctx"),
            P("ctx"),
            P("ctx", "cls"),
            P("cls"),
            P("cls"),
        ),
        out_specs=(P(), P("cls", "ctx"), P("ctx", "cls"), P("cls")),
        check_vma=False,
    )
```

```python
import functools

import jax
import jax.numpy as jnp
from jax import lax
from jax.experimental import pallas as pl
from jax.experimental.pallas import tpu as pltpu
from jax.sharding import PartitionSpec as P

F32 = jnp.float32
BF16 = jnp.bfloat16
LANES = 128
MASKED = -1e30
MIB = 1024 * 1024


def swap(x, ctx_bits, cls_bits):
    contexts, classes = lax.axis_size("ctx"), lax.axis_size("cls")
    pairs = [
        (c * classes + k, (c ^ ctx_bits) * classes + (k ^ cls_bits)) for c in range(contexts) for k in range(classes)
    ]
    return lax.ppermute(x, ("ctx", "cls"), pairs)


def far_steps():
    return [(2 * j, 0) for j in reversed(range(1, lax.axis_size("ctx") // 2))]


def near_steps():
    steps = [(i, 2 * k) for i in range(2) for k in range(lax.axis_size("cls") // 2) if i or k]
    return sorted(steps, key=lambda step: (not step[0], bool(step[1])))


def call(kernel, outs, name, args, aliases=None, limit=16, cost=None):
    run = pl.pallas_call(
        kernel,
        out_shape=[jax.ShapeDtypeStruct(s, d) for s, d in outs],
        in_specs=[pl.BlockSpec(memory_space=pltpu.VMEM)] * len(args),
        out_specs=[pl.BlockSpec(memory_space=pltpu.VMEM)] * len(outs),
        input_output_aliases=aliases or {},
        compiler_params=pltpu.CompilerParams(vmem_limit_bytes=limit * MIB),
        cost_estimate=cost,
        name=name,
    )
    return list(run(*args))


def stack_kernel(*refs):
    out_ref = refs[-1]
    for at, ref in enumerate(refs[:-1]):
        out_ref[at] = ref[...].reshape(out_ref.shape[1:])


def hand_on_kernel(*refs):
    del refs


def hand_on(arrays, after):
    outs = [(x.shape, x.dtype) for x in arrays]
    return call(hand_on_kernel, outs, "hand_on", [*arrays, *after], aliases={i: i for i in range(len(arrays))})


def gather(block, local=None, after=()):
    far = [swap(block, *step) for step in far_steps()[::-1]]
    rows, width = block.shape
    (held,) = call(
        stack_kernel, [((len(far) + 1, rows, width), block.dtype)], "stack", [block if local is None else local, *far]
    )
    steps = sorted(near_steps(), reverse=True)
    parts = dict(zip(steps, hand_on([swap(held, *step) for step in steps], after)))
    parts[0, 0] = held
    other = {step: swap(part, 0, 1) for step, part in parts.items()}
    steps = sorted(parts)
    return [[group[step] for group in (parts, other) for step in steps if step[0] == i] for i in range(2)]


def pieces(x):
    high = x.astype(BF16)
    rest = x - high.astype(F32)
    middle = rest.astype(BF16)
    return high, middle, (rest - middle.astype(F32)).astype(BF16)


def into_lanes(columns, rows):
    lane = lax.broadcasted_iota(jnp.int32, (rows, LANES), 1)
    out = jnp.zeros((rows, LANES), F32)
    for i, column in enumerate(columns):
        for j, piece in enumerate(pieces(column)):
            out = jnp.where(lane == 3 * i + j, piece.astype(F32), out)
    return out.astype(BF16)


def from_lanes(block, width, i):
    at = width + 3 * i
    block = block.astype(F32)
    return block[:, at : at + 1] + (block[:, at + 1 : at + 2] + block[:, at + 2 : at + 3])


def load_kernel(half, count, length_ref, tokens_ref, *refs):
    others, held_ref, copies_of = refs[:count], refs[count], refs[count + 1 : 2 * count + 1]
    length_out_ref, sems = refs[2 * count + 1 :]
    blocks, _, width = held_ref.shape
    copies = [pltpu.make_async_copy(src, dst, sems.at[i]) for i, (src, dst) in enumerate(zip(others, copies_of))]
    for j in range(blocks):
        start = pl.multiple_of((lax.axis_index("ctx") ^ half ^ (2 * j)) * width, LANES)
        copies.append(
            pltpu.make_async_copy(tokens_ref.at[:, pl.ds(start, width)], held_ref.at[j], sems.at[count + j])
        )
    for copy in copies:
        copy.start()
    length_out_ref[...] = jnp.full(length_out_ref.shape, length_ref[0], jnp.int32)
    for copy in copies:
        copy.wait()


def load(half, width, length, tokens, *others):
    rows, full_width = tokens.shape
    blocks = full_width // width // 2
    outs = [((blocks, rows, width), tokens.dtype)] + [(x.shape, x.dtype) for x in others] + [((1, LANES), jnp.int32)]
    hbm = (tokens, *others)
    run = pl.pallas_call(
        functools.partial(load_kernel, half, len(others)),
        out_shape=[pltpu.VMEM(*out) for out in outs],
        in_specs=[pl.BlockSpec(memory_space=pltpu.SMEM)] + [pl.BlockSpec(memory_space=pltpu.HBM)] * len(hbm),
        out_specs=[pl.BlockSpec(memory_space=pltpu.VMEM)] * len(outs),
        scratch_shapes=[pltpu.SemaphoreType.DMA((blocks + len(others),))],
        compiler_params=pltpu.CompilerParams(vmem_limit_bytes=16 * MIB),
        name="load",
    )
    return run(length, *[pltpu.with_memory_space_constraint(x, pltpu.HBM) for x in hbm])


def project(parts, held_ref, tile=256):
    blocks, token_count, width = held_ref.shape
    tiles = []
    for at in range(0, token_count, tile):
        total = None
        for j in range(blocks):
            left = jnp.concatenate([ref[j] for ref in parts], axis=0)[:, :width]
            block = held_ref[j, at : at + tile, :]
            part = lax.dot_general(left, block, (((1,), (1,)), ((), ())), preferred_element_type=F32)
            total = part if total is None else total + part
        tiles.append(total)
    return jnp.concatenate(tiles, axis=1)


def spread(left, held_ref, keep_ref, send_ref, extra, tile=256):
    blocks, half, width = keep_ref.shape
    for j in range(blocks):
        for at in range(0, width, tile):
            part = jnp.dot(left, held_ref[j, :, at : at + tile], preferred_element_type=F32)
            keep_ref[j, :, at : at + tile] = part[:half]
            send_ref[j, :, at : at + tile] = part[half:].astype(BF16)
        if extra is not None:
            send_ref[j, :, width:] = extra


def project_kernel(count, *refs):
    refs[-1][...] = project(refs[:count], refs[count])


def peak_lanes(peak, half):
    return into_lanes([peak[half:, :1]], half)


def pool_kernel(count, length_ref, *refs):
    parts, refs = refs[:count], refs[count:]
    part_ref, held_ref, keep_ref, send_ref, peak_ref, w_ref, left_ref = refs
    scores = part_ref[...] + project(parts, held_ref)
    shard = lax.axis_index("ctx") * lax.axis_size("cls") + lax.axis_index("cls")
    valid = lax.broadcasted_iota(jnp.int32, scores.shape, 1) < length_ref[:, :1] - shard * scores.shape[1]
    peak = jnp.max(jnp.where(valid, scores, MASKED), axis=1, keepdims=True)
    weights = jnp.where(valid, jnp.exp(scores - peak), 0.0)
    left = weights.astype(BF16)
    w_ref[...] = weights
    left_ref[...] = left
    peak_ref[...] = jnp.broadcast_to(peak, peak_ref.shape)
    spread(left, held_ref, keep_ref, send_ref, peak_lanes(peak, keep_ref.shape[1]))


def pool_rest_kernel(left_ref, peak_ref, held_ref, keep_ref, send_ref):
    spread(left_ref[...], held_ref, keep_ref, send_ref, peak_lanes(peak_ref[...], keep_ref.shape[1]))


def grad_kernel(scale, count, *refs):
    parts, refs = refs[:count], refs[count:]
    part_ref, held_ref, w_ref, peak_ref, keep_ref, send_ref, left_ref, loss_ref = refs
    width = held_ref.shape[2]
    projected = part_ref[...] + project(parts, held_ref)
    blocks = [ref[0] for ref in parts]
    top = jnp.concatenate([from_lanes(block, width, 0) for block in blocks], axis=0)
    weights = w_ref[...] * jnp.exp(peak_ref[:, :1] - top)
    left = (weights * projected).astype(BF16)
    left_ref[...] = left
    spread(left, held_ref, keep_ref, send_ref, None)
    loss_ref[...] = tree_sum([from_lanes(block, width, 1)[:1] for block in blocks]) * scale


def grad_rest_kernel(left_ref, held_ref, keep_ref, send_ref):
    spread(left_ref[...], held_ref, keep_ref, send_ref, None)


def rescaling(peak, received, width):
    if peak is None:
        return None, None
    others = [from_lanes(block, width, 0) for block in received]
    top = peak
    for other in others:
        top = jnp.maximum(top, other)
    return top, [jnp.exp(p - top) for p in [peak, *others]]


def total_of(keep, received, factors):
    total = keep if factors is None else keep * factors[0]
    for i, block in enumerate(received):
        block = block[:, : keep.shape[1]].astype(F32)
        total = total + (block if factors is None else block * factors[i + 1])
    return total


def put(ref, j, total, lanes):
    width = total.shape[1]
    ref[j, :, :width] = total.astype(BF16)
    if lanes is not None:
        ref[j, :, width:] = lanes


def core_kernel(peaks, first, *refs):
    keep_ref, recv_ref, *refs = refs
    peak = refs.pop(0)[: keep_ref.shape[1], :1] if peaks else None
    refs = refs if first else refs[1:-1]
    top_ref = refs.pop() if peaks and first else None
    width = keep_ref.shape[2]
    rows = refs[0].shape[1]
    top, factors = rescaling(peak, [recv_ref[0]], width)
    lanes = into_lanes([top], top.shape[0]) if peaks else None
    for j in range(keep_ref.shape[0]):
        total = total_of(keep_ref[j], [recv_ref[j]], factors)
        for k, ref in enumerate(refs):
            at = slice(k * rows, (k + 1) * rows)
            if first and k == 0:
                ref[j] = total[at]
            else:
                put(ref, j, total[at], lanes[at] if peaks else None)
    if peaks and first:
        top_ref[...] = jnp.broadcast_to(top[:rows], top_ref.shape)


def near_sum_kernel(peaks, count, steps, *refs):
    keep_ref, *refs = refs
    received, refs = refs[:count], refs[count:]
    peak = refs.pop(0)[:, :1] if peaks else None
    top_ref = refs.pop() if peaks else None
    top, factors = rescaling(peak, [ref[0] for ref in received], keep_ref.shape[2])
    lanes = into_lanes([top], top.shape[0]) if peaks else None
    for p in range(keep_ref.shape[0]):
        total = total_of(keep_ref[p], [ref[p] for ref in received], factors)
        if p == 0:
            refs[0][0] = total
        else:
            put(refs[steps.index((2 * p, 0)) + 1], 0, total, lanes)
    if peaks:
        top_ref[...] = jnp.broadcast_to(top, top_ref.shape)


def scatter_sum(halves, peak):
    peaks = peak is not None
    near, far = near_steps(), far_steps()
    across = (len(near) + 1) // 2
    blocks, half, width = halves[0][0].shape
    lanes = halves[0][1].shape[2]
    rows = half // across
    top_out = [((rows, LANES), F32)] if peaks else []
    part = ((blocks, rows, lanes), BF16)
    (keep_a, send_a), (keep_b, send_b) = halves
    args = [keep_b, swap(send_b, 0, 1)] + ([peak] if peaks else []) + [send_a]
    outs = [part] * across + [((blocks, half, lanes), BF16)]
    *parts_b, send_a = call(
        functools.partial(core_kernel, peaks, False), outs, "core_sum", args, aliases={len(args) - 1: across}
    )
    args = [keep_a, swap(send_a, 0, 1)] + ([peak] if peaks else [])
    outs = [((blocks, rows, width), F32)] + [part] * (across - 1) + top_out
    out = call(functools.partial(core_kernel, peaks, True), outs, "core_sum", args)
    parts = {(i, 2 * k): x for i, group in enumerate((out, parts_b)) for k, x in enumerate(group[:across])}
    received = [swap(parts[step], *step) for step in near]
    outs = [((1, rows, width), F32)] + [((1, rows, lanes), BF16)] * len(far) + top_out
    args = [parts[0, 0], *received] + (out[-1:] if peaks else [])
    out = call(functools.partial(near_sum_kernel, peaks, len(received), far), outs, "near_sum", args)
    received = [swap(x, *step) for x, step in zip(out[1:], far)]
    return [out[0], *received] + (out[-1:] if peaks else [])


def far_sum_kernel(*refs):
    keep_ref, *received, out_ref = refs
    out_ref[...] = total_of(keep_ref[0], [ref[0] for ref in received], None)


def head_mask(shape, attributes):
    row = lax.broadcasted_iota(jnp.int32, shape, 0)
    column = lax.broadcasted_iota(jnp.int32, shape, 1)
    return column // attributes == row


def head_sums_kernel(*refs):
    keep_ref, *received, peak_ref, gain_ref, weight_ref, sums_ref, pooled_ref, top_ref = refs
    received = [ref[0] for ref in received]
    top, factors = rescaling(peak_ref[:, :1], received, keep_ref.shape[2])
    pooled = total_of(keep_ref[0], received, factors)
    pooled_ref[...] = pooled
    top_ref[...] = jnp.broadcast_to(top, top_ref.shape)
    scaled_b = (pooled * gain_ref[...]).astype(BF16)
    product = jnp.dot(scaled_b, weight_ref[...], preferred_element_type=F32)
    mask = head_mask(product.shape, product.shape[1] // product.shape[0])
    squares = jnp.sum(pooled * pooled, axis=1, keepdims=True)
    product_flat = jnp.sum(jnp.where(mask, product, 0.0), axis=0, keepdims=True)
    squares_flat = jnp.sum(jnp.where(mask, squares, 0.0), axis=0, keepdims=True)
    sums_ref[0:1, :] = product_flat
    sums_ref[1:2, :] = squares_flat


def tree_sum(level):
    while len(level) > 1:
        level = [a + b for a, b in zip(level[::2], level[1::2])]
    return level[0]


def tree_sum_kernel(*refs):
    refs[-1][...] = tree_sum([ref[...] for ref in refs[:-1]])


def head_grads_kernel(full_width, sums_ref, other_sums_ref, *refs):
    pooled_ref, top_ref, gain_ref, weight_ref, bias_ref, label_ref, *refs = refs
    bias_grad_ref, copy_ref, grad_ref, normed_ref = refs
    pooled, gain = pooled_ref[...], gain_ref[...]
    heads, width = pooled.shape
    columns = bias_ref.shape[1]
    sums = sums_ref[...] + other_sums_ref[...]
    mask = head_mask((heads, columns), columns // heads)
    inverse_flat = lax.rsqrt(sums[1:2] / full_width + 1e-05)
    inverse_rms = jnp.max(jnp.where(mask, inverse_flat, 0.0), axis=1, keepdims=True)
    product = inverse_flat * sums[0:1]
    logits = product + bias_ref[...]
    target = label_ref[...].astype(F32)
    losses = jnp.maximum(logits, 0.0) + jnp.log1p(jnp.exp(-jnp.abs(logits))) - target * logits
    loss = jnp.sum(losses, axis=1, keepdims=True)
    bias_grad = jax.nn.sigmoid(logits) - target
    bias_grad_ref[...] = bias_grad
    copy_ref[...] = bias_grad
    by_head = jnp.where(mask, bias_grad, 0.0)
    high = by_head.astype(BF16)
    low = (by_head - high.astype(F32)).astype(BF16)
    both = jnp.concatenate([high, low], axis=0)
    back = lax.dot_general(both, weight_ref[...], (((1,), (1,)), ((), ())), preferred_element_type=F32)
    normed_grad = (back[:heads] + back[heads:]) * gain
    inner = jnp.sum(by_head * product, axis=1, keepdims=True) / full_width
    unit = pooled * inverse_rms
    grad_ref[:, :width] = (inverse_rms * (normed_grad - unit * inner)).astype(BF16)
    grad_ref[:, width:] = into_lanes([top_ref[:, :1], jnp.broadcast_to(loss, (heads, 1))], heads)
    normed_ref[...] = unit * gain


def head_weight_grad_kernel(attributes, normed_ref, bias_grad_ref, out_ref, done_ref):
    heads = normed_ref.shape[0]
    columns = out_ref.shape[1]
    parts = jnp.concatenate(pieces(normed_ref[...]), axis=0)
    row = lax.broadcasted_iota(jnp.int32, (3 * heads, columns), 0) % heads
    column = pl.program_id(0) * columns + lax.broadcasted_iota(jnp.int32, (3 * heads, columns), 1)
    ones = jnp.where(column // attributes == row, 1.0, 0.0).astype(BF16)
    normed = lax.dot_general(parts, ones, (((0,), (0,)), ((), ())), preferred_element_type=F32)
    out_ref[...] = normed * bias_grad_ref[...]
    done_ref[...] = jnp.zeros_like(done_ref)


def head_weight_grad(normed, bias_grad):
    rows, width = normed.shape
    columns = bias_grad.shape[1]
    block = columns // 4
    return pl.pallas_call(
        functools.partial(head_weight_grad_kernel, columns // rows),
        out_shape=[jax.ShapeDtypeStruct((width, columns), F32), jax.ShapeDtypeStruct((8, LANES), F32)],
        grid=(columns // block,),
        in_specs=[
            pl.BlockSpec((rows, width), lambda i: (0, 0)),
            pl.BlockSpec((1, block), lambda i: (0, i)),
        ],
        out_specs=[pl.BlockSpec((width, block), lambda i: (0, i)), pl.BlockSpec((8, LANES), lambda i: (0, 0))],
        compiler_params=pltpu.CompilerParams(vmem_limit_bytes=16 * MIB),
        name="head_weight_grad",
    )(normed, bias_grad)


def shards(tokens, doc_length, queries, norm_gain, head_weight, head_bias, labels):
    contexts, classes = lax.axis_size("ctx"), lax.axis_size("cls")
    token_count = tokens.shape[0]
    rows, width = queries.shape
    full_width = width * contexts
    heads = rows * classes
    half = heads // 2
    columns = labels.shape[0]
    blocks = contexts // 2
    pair = [((blocks, half, width), F32), ((blocks, half, width + LANES), BF16)]
    product = ((heads, token_count), F32)
    cost = pl.CostEstimate(flops=256 * token_count * full_width, bytes_accessed=0, transcendentals=0)

    def project_half(parts):
        return call(functools.partial(project_kernel, len(parts)), [product], "project", [*parts, held_a], cost=cost)[0]

    held_a, queries_here, length = load(0, width, doc_length, tokens, queries)
    held_b, gain, _ = load(1, width, doc_length, tokens, norm_gain[None, :])
    first, second = gather(queries, queries_here, after=(gain,))
    part = project_half(first)
    keep_b, send_b, own_peak, weights, left = call(
        functools.partial(pool_kernel, classes),
        [*pair, ((heads, LANES), F32), product, ((heads, token_count), BF16)],
        "pool",
        [length, *second, part, held_b],
        cost=cost,
    )
    half_a = call(pool_rest_kernel, pair, "pool_rest", [left, own_peak, held_a], cost=cost)
    parts = scatter_sum([half_a, (keep_b, send_b)], own_peak)
    sums, pooled, top = call(
        head_sums_kernel,
        [((2, columns), F32), ((rows, width), F32), ((rows, LANES), F32)],
        "head_sums",
        [*parts, gain, head_weight],
    )
    far_sums = [swap(sums, *step) for step in far_steps()[::-1]]
    (sums,) = call(tree_sum_kernel, [((2, columns), F32)], "tree_sum", [sums, *far_sums])
    bias_grad, bias_grad_here, pooled_grad, normed = call(
        functools.partial(head_grads_kernel, full_width),
        [((1, columns), F32), ((1, columns), F32), ((rows, width + LANES), BF16), ((rows, width), F32)],
        "head_grads",
        [sums, swap(sums, 1, 0), pooled, top, gain, head_weight, head_bias[None, :], labels[None, :]],
    )
    head_grad, done = head_weight_grad(normed, bias_grad_here)
    first, second = gather(pooled_grad, after=(done,))
    part = project_half(first)
    pair = [((blocks, half, width), F32), ((blocks, half, width), BF16)]
    keep_b, send_b, left, loss = call(
        functools.partial(grad_kernel, 1.0 / (columns * classes), classes),
        [*pair, ((heads, token_count), BF16), ((1, 1), F32)],
        "grad",
        [*second, part, held_b, weights, own_peak],
        cost=cost,
    )
    half_a = call(grad_rest_kernel, pair, "grad_rest", [left, held_a], cost=cost)
    parts = scatter_sum([half_a, (keep_b, send_b)], None)
    (query_grad,) = call(far_sum_kernel, [((rows, width), F32)], "far_sum", parts)
    return (loss.reshape(()), query_grad, head_grad, bias_grad.reshape(-1))


def solution(mesh):
    return jax.shard_map(
        shards,
        mesh=mesh,
        in_specs=(
            P(("ctx", "cls"), None),
            P(),
            P("cls", "ctx"),
            P("ctx"),
            P("ctx", "cls"),
            P("cls"),
            P("cls"),
        ),
        out_specs=(P(), P("cls", "ctx"), P("ctx", "cls"), P("cls")),
        check_vma=False,
    )
```

```python
import functools

import jax
import jax.numpy as jnp
from jax import lax
from jax.experimental import pallas as pl
from jax.experimental.pallas import tpu as pltpu
from jax.sharding import PartitionSpec as P

F32 = jnp.float32
BF16 = jnp.bfloat16
LANES = 128
MASKED = -1e30
MIB = 1024 * 1024


def swap(x, ctx_bits, cls_bits):
    contexts, classes = lax.axis_size("ctx"), lax.axis_size("cls")
    pairs = [
        (c * classes + k, (c ^ ctx_bits) * classes + (k ^ cls_bits)) for c in range(contexts) for k in range(classes)
    ]
    return lax.ppermute(x, ("ctx", "cls"), pairs)


def far_steps():
    return [(2 * j, 0) for j in reversed(range(1, lax.axis_size("ctx") // 2))]


def near_steps():
    steps = [(i, 2 * k) for i in range(2) for k in range(lax.axis_size("cls") // 2) if i or k]
    return sorted(steps, key=lambda step: (not (step[0] and step[1]), not step[0]))


def call(kernel, outs, name, args, smem_args=(), aliases=None, limit=16, cost=None):
    def spec(i):
        if i in smem_args:
            return pl.BlockSpec(memory_space=pltpu.SMEM)
        return pl.BlockSpec(memory_space=pltpu.VMEM)

    run = pl.pallas_call(
        kernel,
        out_shape=[jax.ShapeDtypeStruct(s, d) for s, d in outs],
        in_specs=[spec(i) for i in range(len(args))],
        out_specs=[pl.BlockSpec(memory_space=pltpu.VMEM)] * len(outs),
        input_output_aliases=aliases or {},
        compiler_params=pltpu.CompilerParams(vmem_limit_bytes=limit * MIB),
        cost_estimate=cost,
        name=name,
    )
    return list(run(*args))


def stack_kernel(*refs):
    out_ref = refs[-1]
    for at, ref in enumerate(refs[:-1]):
        out_ref[at] = ref[...].reshape(out_ref.shape[1:])


def gather(block, local=None):
    far = [swap(block, *step) for step in far_steps()[::-1]]
    rows, width = block.shape
    (held,) = call(
        stack_kernel, [((len(far) + 1, rows, width), block.dtype)], "stack", [block if local is None else local, *far]
    )
    parts = {step: swap(held, *step) for step in near_steps()[::-1]}
    parts[0, 0] = held
    other = {step: swap(part, 0, 1) for step, part in parts.items()}
    steps = sorted(parts)
    return [[group[step] for group in (parts, other) for step in steps if step[0] == i] for i in range(2)]


def pieces(x):
    high = x.astype(BF16)
    rest = x - high.astype(F32)
    middle = rest.astype(BF16)
    return high, middle, (rest - middle.astype(F32)).astype(BF16)


def into_lanes(columns, rows):
    lane = lax.broadcasted_iota(jnp.int32, (rows, LANES), 1)
    out = jnp.zeros((rows, LANES), F32)
    for i, column in enumerate(columns):
        for j, piece in enumerate(pieces(column)):
            out = jnp.where(lane == 3 * i + j, piece.astype(F32), out)
    return out.astype(BF16)


def from_lanes(block, width, i):
    at = width + 3 * i
    block = block.astype(F32)
    return block[:, at : at + 1] + (block[:, at + 1 : at + 2] + block[:, at + 2 : at + 3])


def load_kernel(tokens_ref, *refs):
    count = (len(refs) - 3) // 2
    others, halves, copies_of, sems = refs[:count], refs[count : count + 2], refs[count + 2 : -1], refs[-1]
    blocks, _, width = halves[0].shape
    copies = [pltpu.make_async_copy(src, dst, sems.at[i]) for i, (src, dst) in enumerate(zip(others, copies_of))]
    for i in range(2):
        for j in range(blocks):
            start = pl.multiple_of((lax.axis_index("ctx") ^ i ^ (2 * j)) * width, LANES)
            sem = sems.at[count + i * blocks + j]
            copies.append(pltpu.make_async_copy(tokens_ref.at[:, pl.ds(start, width)], halves[i].at[j], sem))
    for copy in copies:
        copy.start()
    for copy in copies:
        copy.wait()


def load(width, tokens, *others):
    rows, full_width = tokens.shape
    blocks = full_width // width // 2
    outs = [pltpu.VMEM((blocks, rows, width), tokens.dtype)] * 2 + [pltpu.VMEM(x.shape, x.dtype) for x in others]
    run = pl.pallas_call(
        load_kernel,
        out_shape=outs,
        in_specs=[pl.BlockSpec(memory_space=pltpu.HBM)] * (1 + len(others)),
        out_specs=[pl.BlockSpec(memory_space=pltpu.VMEM)] * len(outs),
        scratch_shapes=[pltpu.SemaphoreType.DMA((2 * blocks + len(others),))],
        compiler_params=pltpu.CompilerParams(vmem_limit_bytes=16 * MIB),
        name="load",
    )
    return run(*[pltpu.with_memory_space_constraint(x, pltpu.HBM) for x in (tokens, *others)])


def project(parts, held_ref, tile=256):
    blocks, token_count, width = held_ref.shape
    tiles = []
    for at in range(0, token_count, tile):
        total = None
        for j in range(blocks):
            left = jnp.concatenate([ref[j] for ref in parts], axis=0)[:, :width]
            block = held_ref[j, at : at + tile, :]
            part = lax.dot_general(left, block, (((1,), (1,)), ((), ())), preferred_element_type=F32)
            total = part if total is None else total + part
        tiles.append(total)
    return jnp.concatenate(tiles, axis=1)


def spread(left, held_ref, keep_ref, send_ref, extra, tile=256):
    blocks, half, width = keep_ref.shape
    for j in range(blocks):
        for at in range(0, width, tile):
            part = jnp.dot(left, held_ref[j, :, at : at + tile], preferred_element_type=F32)
            keep_ref[j, :, at : at + tile] = part[:half]
            send_ref[j, :, at : at + tile] = part[half:].astype(BF16)
        if extra is not None:
            send_ref[j, :, width:] = extra


def project_kernel(count, *refs):
    refs[-1][...] = project(refs[:count], refs[count])


def peak_lanes(peak, half):
    return into_lanes([peak[half:, :1]], half)


def pool_kernel(count, length_ref, *refs):
    parts, refs = refs[:count], refs[count:]
    part_ref, held_ref, keep_ref, send_ref, peak_ref, w_ref, left_ref = refs
    scores = part_ref[...] + project(parts, held_ref)
    shard = lax.axis_index("ctx") * lax.axis_size("cls") + lax.axis_index("cls")
    valid = lax.broadcasted_iota(jnp.int32, scores.shape, 1) < length_ref[0] - shard * scores.shape[1]
    peak = jnp.max(jnp.where(valid, scores, MASKED), axis=1, keepdims=True)
    weights = jnp.where(valid, jnp.exp(scores - peak), 0.0)
    left = weights.astype(BF16)
    w_ref[...] = weights
    left_ref[...] = left
    peak_ref[...] = jnp.broadcast_to(peak, peak_ref.shape)
    spread(left, held_ref, keep_ref, send_ref, peak_lanes(peak, keep_ref.shape[1]))


def pool_rest_kernel(left_ref, peak_ref, held_ref, keep_ref, send_ref):
    spread(left_ref[...], held_ref, keep_ref, send_ref, peak_lanes(peak_ref[...], keep_ref.shape[1]))


def grad_kernel(scale, count, *refs):
    parts, notes, refs = refs[:count], refs[count : 2 * count], refs[2 * count :]
    part_ref, held_ref, w_ref, peak_ref, keep_ref, send_ref, left_ref, loss_ref = refs
    projected = part_ref[...] + project(parts, held_ref)
    notes = [ref[...] for ref in notes]
    top = jnp.concatenate([from_lanes(note, 0, 0) for note in notes], axis=0)
    weights = w_ref[...] * jnp.exp(peak_ref[:, :1] - top)
    left = (weights * projected).astype(BF16)
    left_ref[...] = left
    spread(left, held_ref, keep_ref, send_ref, None)
    loss_ref[...] = tree_sum([from_lanes(note, 0, 1)[:1] for note in notes]) * scale


def grad_rest_kernel(left_ref, held_ref, keep_ref, send_ref):
    spread(left_ref[...], held_ref, keep_ref, send_ref, None)


def rescaling(peak, received, width):
    if peak is None:
        return None, None
    others = [from_lanes(block, width, 0) for block in received]
    top = peak
    for other in others:
        top = jnp.maximum(top, other)
    return top, [jnp.exp(p - top) for p in [peak, *others]]


def total_of(keep, received, factors):
    total = keep if factors is None else keep * factors[0]
    for i, block in enumerate(received):
        block = block[:, : keep.shape[1]].astype(F32)
        total = total + (block if factors is None else block * factors[i + 1])
    return total


def put(ref, j, total, lanes):
    width = total.shape[1]
    ref[j, :, :width] = total.astype(BF16)
    if lanes is not None:
        ref[j, :, width:] = lanes


def core_kernel(peaks, first, *refs):
    keep_ref, recv_ref, *refs = refs
    peak = refs.pop(0)[: keep_ref.shape[1], :1] if peaks else None
    refs = refs if first else refs[1:-1]
    top_ref = refs.pop() if peaks and first else None
    width = keep_ref.shape[2]
    rows = refs[0].shape[1]
    top, factors = rescaling(peak, [recv_ref[0]], width)
    lanes = into_lanes([top], top.shape[0]) if peaks else None
    for j in range(keep_ref.shape[0]):
        total = total_of(keep_ref[j], [recv_ref[j]], factors)
        for k, ref in enumerate(refs):
            at = slice(k * rows, (k + 1) * rows)
            if first and k == 0:
                ref[j] = total[at]
            else:
                put(ref, j, total[at], lanes[at] if peaks else None)
    if peaks and first:
        top_ref[...] = jnp.broadcast_to(top[:rows], top_ref.shape)


def near_sum_kernel(peaks, count, steps, *refs):
    keep_ref, *refs = refs
    received, refs = refs[:count], refs[count:]
    peak = refs.pop(0)[:, :1] if peaks else None
    top_ref = refs.pop() if peaks else None
    top, factors = rescaling(peak, [ref[0] for ref in received], keep_ref.shape[2])
    lanes = into_lanes([top], top.shape[0]) if peaks else None
    for p in range(keep_ref.shape[0]):
        total = total_of(keep_ref[p], [ref[p] for ref in received], factors)
        if p == 0:
            refs[0][0] = total
        else:
            put(refs[steps.index((2 * p, 0)) + 1], 0, total, lanes)
    if peaks:
        top_ref[...] = jnp.broadcast_to(top, top_ref.shape)


def scatter_sum(halves, peak):
    peaks = peak is not None
    near, far = near_steps(), far_steps()
    across = (len(near) + 1) // 2
    blocks, half, width = halves[0][0].shape
    lanes = halves[0][1].shape[2]
    rows = half // across
    top_out = [((rows, LANES), F32)] if peaks else []
    part = ((blocks, rows, lanes), BF16)
    (keep_a, send_a), (keep_b, send_b) = halves
    args = [keep_b, swap(send_b, 0, 1)] + ([peak] if peaks else []) + [send_a]
    outs = [part] * across + [((blocks, half, lanes), BF16)]
    *parts_b, send_a = call(
        functools.partial(core_kernel, peaks, False), outs, "core_sum", args, aliases={len(args) - 1: across}
    )
    args = [keep_a, swap(send_a, 0, 1)] + ([peak] if peaks else [])
    outs = [((blocks, rows, width), F32)] + [part] * (across - 1) + top_out
    out = call(functools.partial(core_kernel, peaks, True), outs, "core_sum", args)
    parts = {(i, 2 * k): x for i, group in enumerate((out, parts_b)) for k, x in enumerate(group[:across])}
    received = [swap(parts[step], *step) for step in near]
    outs = [((1, rows, width), F32)] + [((1, rows, lanes), BF16)] * len(far) + top_out
    args = [parts[0, 0], *received] + (out[-1:] if peaks else [])
    out = call(functools.partial(near_sum_kernel, peaks, len(received), far), outs, "near_sum", args)
    received = [swap(x, *step) for x, step in zip(out[1:], far)]
    return [out[0], *received] + (out[-1:] if peaks else [])


def far_sum_kernel(*refs):
    keep_ref, *received, out_ref = refs
    out_ref[...] = total_of(keep_ref[0], [ref[0] for ref in received], None)


def head_mask(shape, attributes):
    row = lax.broadcasted_iota(jnp.int32, shape, 0)
    column = lax.broadcasted_iota(jnp.int32, shape, 1)
    return column // attributes == row


def head_sums_kernel(*refs):
    keep_ref, *received, peak_ref, gain_ref, weight_ref, sums_ref, pooled_ref, top_ref = refs
    received = [ref[0] for ref in received]
    top, factors = rescaling(peak_ref[:, :1], received, keep_ref.shape[2])
    pooled = total_of(keep_ref[0], received, factors)
    pooled_ref[...] = pooled
    top_ref[...] = jnp.broadcast_to(top, top_ref.shape)
    scaled_b = (pooled * gain_ref[...]).astype(BF16)
    product = jnp.dot(scaled_b, weight_ref[...], preferred_element_type=F32)
    mask = head_mask(product.shape, product.shape[1] // product.shape[0])
    squares = jnp.sum(pooled * pooled, axis=1, keepdims=True)
    product_flat = jnp.sum(jnp.where(mask, product, 0.0), axis=0, keepdims=True)
    squares_flat = jnp.sum(jnp.where(mask, squares, 0.0), axis=0, keepdims=True)
    sums_ref[0:1, :] = product_flat
    sums_ref[1:2, :] = squares_flat


def tree_sum(level):
    while len(level) > 1:
        level = [a + b for a, b in zip(level[::2], level[1::2])]
    return level[0]


def tree_sum_kernel(*refs):
    refs[-1][...] = tree_sum([ref[...] for ref in refs[:-1]])


def head_grads_kernel(full_width, count, *refs):
    terms, refs = refs[:count], refs[count:]
    pooled_ref, top_ref, gain_ref, weight_ref, bias_ref, label_ref, *refs = refs
    bias_grad_ref, copy_ref, grad_ref, note_ref, normed_ref = refs
    pooled, gain = pooled_ref[...], gain_ref[...]
    heads, width = pooled.shape
    columns = bias_ref.shape[1]
    sums = tree_sum([ref[...] for ref in terms])
    mask = head_mask((heads, columns), columns // heads)
    inverse_flat = lax.rsqrt(sums[1:2] / full_width + 1e-05)
    inverse_rms = jnp.max(jnp.where(mask, inverse_flat, 0.0), axis=1, keepdims=True)
    product = inverse_flat * sums[0:1]
    logits = product + bias_ref[...]
    target = label_ref[...].astype(F32)
    losses = jnp.maximum(logits, 0.0) + jnp.log1p(jnp.exp(-jnp.abs(logits))) - target * logits
    loss = jnp.sum(losses, axis=1, keepdims=True)
    bias_grad = jax.nn.sigmoid(logits) - target
    bias_grad_ref[...] = bias_grad
    copy_ref[...] = bias_grad
    by_head = jnp.where(mask, bias_grad, 0.0)
    high = by_head.astype(BF16)
    low = (by_head - high.astype(F32)).astype(BF16)
    both = jnp.concatenate([high, low], axis=0)
    back = lax.dot_general(both, weight_ref[...], (((1,), (1,)), ((), ())), preferred_element_type=F32)
    normed_grad = (back[:heads] + back[heads:]) * gain
    inner = jnp.sum(by_head * product, axis=1, keepdims=True) / full_width
    unit = pooled * inverse_rms
    grad_ref[...] = (inverse_rms * (normed_grad - unit * inner)).astype(BF16)
    note_ref[...] = into_lanes([top_ref[:, :1], jnp.broadcast_to(loss, (heads, 1))], heads)
    normed_ref[...] = unit * gain


def head_weight_grad_kernel(attributes, normed_ref, bias_grad_ref, out_ref):
    heads = normed_ref.shape[0]
    columns = out_ref.shape[1]
    parts = jnp.concatenate(pieces(normed_ref[...]), axis=0)
    row = lax.broadcasted_iota(jnp.int32, (3 * heads, columns), 0) % heads
    column = pl.program_id(0) * columns + lax.broadcasted_iota(jnp.int32, (3 * heads, columns), 1)
    ones = jnp.where(column // attributes == row, 1.0, 0.0).astype(BF16)
    normed = lax.dot_general(parts, ones, (((0,), (0,)), ((), ())), preferred_element_type=F32)
    out_ref[...] = normed * bias_grad_ref[...]


def head_weight_grad(normed, bias_grad):
    rows, width = normed.shape
    columns = bias_grad.shape[1]
    block = columns // 4
    return pl.pallas_call(
        functools.partial(head_weight_grad_kernel, columns // rows),
        out_shape=jax.ShapeDtypeStruct((width, columns), F32),
        grid=(columns // block,),
        in_specs=[
            pl.BlockSpec((rows, width), lambda i: (0, 0)),
            pl.BlockSpec((1, block), lambda i: (0, i)),
        ],
        out_specs=pl.BlockSpec((width, block), lambda i: (0, i)),
        compiler_params=pltpu.CompilerParams(vmem_limit_bytes=16 * MIB),
        name="head_weight_grad",
    )(normed, bias_grad)


def shards(tokens, doc_length, queries, norm_gain, head_weight, head_bias, labels):
    contexts, classes = lax.axis_size("ctx"), lax.axis_size("cls")
    token_count = tokens.shape[0]
    rows, width = queries.shape
    full_width = width * contexts
    heads = rows * classes
    half = heads // 2
    columns = labels.shape[0]
    blocks = contexts // 2
    pair = [((blocks, half, width), F32), ((blocks, half, width + LANES), BF16)]
    product = ((heads, token_count), F32)
    cost = pl.CostEstimate(flops=256 * token_count * full_width, bytes_accessed=0, transcendentals=0)

    def project_half(parts):
        return call(functools.partial(project_kernel, len(parts)), [product], "project", [*parts, held_a], cost=cost)[0]

    held_a, held_b, queries_here, gain = load(width, tokens, queries, norm_gain[None, :])
    first, second = gather(queries, queries_here)
    part = project_half(first)
    keep_b, send_b, own_peak, weights, left = call(
        functools.partial(pool_kernel, classes),
        [*pair, ((heads, LANES), F32), product, ((heads, token_count), BF16)],
        "pool",
        [doc_length, *second, part, held_b],
        smem_args=(0,),
        cost=cost,
    )
    half_a = call(pool_rest_kernel, pair, "pool_rest", [left, own_peak, held_a], cost=cost)
    parts = scatter_sum([half_a, (keep_b, send_b)], own_peak)
    sums, pooled, top = call(
        head_sums_kernel,
        [((2, columns), F32), ((rows, width), F32), ((rows, LANES), F32)],
        "head_sums",
        [*parts, gain, head_weight],
    )
    group = min(4, contexts)
    terms = [sums] + [swap(sums, bits, 0) for bits in range(1, group)]
    while group < contexts:
        (sums,) = call(tree_sum_kernel, [((2, columns), F32)], "tree_sum", terms)
        terms = [sums, swap(sums, group, 0)]
        group *= 2
    bias_grad, bias_grad_here, pooled_grad, note, normed = call(
        functools.partial(head_grads_kernel, full_width, len(terms)),
        [((1, columns), F32)] * 2 + [((rows, width), BF16), ((rows, LANES), BF16), ((rows, width), F32)],
        "head_grads",
        [*terms, pooled, top, gain, head_weight, head_bias[None, :], labels[None, :]],
    )
    head_grad = head_weight_grad(normed, bias_grad_here)
    first, second = gather(pooled_grad)
    part = project_half(first)
    notes = [note] + [swap(note, 0, bits) for bits in range(2, classes, 2)]
    notes = notes + [swap(note, 0, 1) for note in notes]
    pair = [((blocks, half, width), F32), ((blocks, half, width), BF16)]
    keep_b, send_b, left, loss = call(
        functools.partial(grad_kernel, 1.0 / (columns * classes), classes),
        [*pair, ((heads, token_count), BF16), ((1, 1), F32)],
        "grad",
        [*second, *notes, part, held_b, weights, own_peak],
        cost=cost,
    )
    half_a = call(grad_rest_kernel, pair, "grad_rest", [left, held_a], cost=cost)
    parts = scatter_sum([half_a, (keep_b, send_b)], None)
    (query_grad,) = call(far_sum_kernel, [((rows, width), F32)], "far_sum", parts)
    return (loss.reshape(()), query_grad, head_grad, bias_grad.reshape(-1))


def solution(mesh):
    return jax.shard_map(
        shards,
        mesh=mesh,
        in_specs=(
            P(("ctx", "cls"), None),
            P(),
            P("cls", "ctx"),
            P("ctx"),
            P("ctx", "cls"),
            P("cls"),
            P("cls"),
        ),
        out_specs=(P(), P("cls", "ctx"), P("ctx", "cls"), P("cls")),
        check_vma=False,
    )
```

```python
import functools

import jax
import jax.numpy as jnp
from jax import lax
from jax.experimental import pallas as pl
from jax.experimental.pallas import tpu as pltpu
from jax.sharding import PartitionSpec as P

F32 = jnp.float32
BF16 = jnp.bfloat16
LANES = 128
MASKED = -1e30
MIB = 1024 * 1024


def swap(x, ctx_bits, cls_bits):
    contexts, classes = lax.axis_size("ctx"), lax.axis_size("cls")
    pairs = [
        (c * classes + k, (c ^ ctx_bits) * classes + (k ^ cls_bits)) for c in range(contexts) for k in range(classes)
    ]
    return lax.ppermute(x, ("ctx", "cls"), pairs)


def far_steps():
    return [(2 * j, 0) for j in reversed(range(1, lax.axis_size("ctx") // 2))]


def near_steps():
    steps = [(i, 2 * k) for i in range(2) for k in range(lax.axis_size("cls") // 2) if i or k]
    return sorted(steps, key=lambda step: (not (step[0] and step[1]), not step[0]))


def call(kernel, outs, name, args, smem_args=(), aliases=None, limit=16, cost=None):
    def spec(i):
        if i in smem_args:
            return pl.BlockSpec(memory_space=pltpu.SMEM)
        return pl.BlockSpec(memory_space=pltpu.VMEM)

    run = pl.pallas_call(
        kernel,
        out_shape=[jax.ShapeDtypeStruct(s, d) for s, d in outs],
        in_specs=[spec(i) for i in range(len(args))],
        out_specs=[pl.BlockSpec(memory_space=pltpu.VMEM)] * len(outs),
        input_output_aliases=aliases or {},
        compiler_params=pltpu.CompilerParams(vmem_limit_bytes=limit * MIB),
        cost_estimate=cost,
        name=name,
    )
    return list(run(*args))


def stack_kernel(*refs):
    out_ref = refs[-1]
    for at, ref in enumerate(refs[:-1]):
        out_ref[at] = ref[...].reshape(out_ref.shape[1:])


def gather(block, local=None):
    far = [swap(block, *step) for step in far_steps()[::-1]]
    rows, width = block.shape
    (held,) = call(
        stack_kernel, [((len(far) + 1, rows, width), block.dtype)], "stack", [block if local is None else local, *far]
    )
    parts = {step: swap(held, *step) for step in near_steps()[::-1]}
    parts[0, 0] = held
    other = {step: swap(part, 0, 1) for step, part in parts.items()}
    steps = sorted(parts)
    return [[group[step] for group in (parts, other) for step in steps if step[0] == i] for i in range(2)]


def pieces(x):
    high = x.astype(BF16)
    rest = x - high.astype(F32)
    middle = rest.astype(BF16)
    return high, middle, (rest - middle.astype(F32)).astype(BF16)


def into_lanes(columns, rows):
    lane = lax.broadcasted_iota(jnp.int32, (rows, LANES), 1)
    out = jnp.zeros((rows, LANES), F32)
    for i, column in enumerate(columns):
        for j, piece in enumerate(pieces(column)):
            out = jnp.where(lane == 3 * i + j, piece.astype(F32), out)
    return out.astype(BF16)


def from_lanes(block, width, i):
    at = width + 3 * i
    block = block.astype(F32)
    return block[:, at : at + 1] + (block[:, at + 1 : at + 2] + block[:, at + 2 : at + 3])


def load_kernel(tokens_ref, *refs):
    count = (len(refs) - 3) // 2
    others, halves, copies_of, sems = refs[:count], refs[count : count + 2], refs[count + 2 : -1], refs[-1]
    blocks, _, width = halves[0].shape
    copies = [pltpu.make_async_copy(src, dst, sems.at[i]) for i, (src, dst) in enumerate(zip(others, copies_of))]
    for i in range(2):
        for j in range(blocks):
            start = pl.multiple_of((lax.axis_index("ctx") ^ i ^ (2 * j)) * width, LANES)
            sem = sems.at[count + i * blocks + j]
            copies.append(pltpu.make_async_copy(tokens_ref.at[:, pl.ds(start, width)], halves[i].at[j], sem))
    for copy in copies:
        copy.start()
    for copy in copies:
        copy.wait()


def load(width, tokens, *others):
    rows, full_width = tokens.shape
    blocks = full_width // width // 2
    outs = [pltpu.VMEM((blocks, rows, width), tokens.dtype)] * 2 + [pltpu.VMEM(x.shape, x.dtype) for x in others]
    run = pl.pallas_call(
        load_kernel,
        out_shape=outs,
        in_specs=[pl.BlockSpec(memory_space=pltpu.HBM)] * (1 + len(others)),
        out_specs=[pl.BlockSpec(memory_space=pltpu.VMEM)] * len(outs),
        scratch_shapes=[pltpu.SemaphoreType.DMA((2 * blocks + len(others),))],
        compiler_params=pltpu.CompilerParams(vmem_limit_bytes=16 * MIB),
        name="load",
    )
    return run(*[pltpu.with_memory_space_constraint(x, pltpu.HBM) for x in (tokens, *others)])


def project(parts, held_ref, tile=256):
    blocks, token_count, width = held_ref.shape
    tiles = []
    for at in range(0, token_count, tile):
        total = None
        for j in range(blocks):
            left = jnp.concatenate([ref[j] for ref in parts], axis=0)[:, :width]
            block = held_ref[j, at : at + tile, :]
            part = lax.dot_general(left, block, (((1,), (1,)), ((), ())), preferred_element_type=F32)
            total = part if total is None else total + part
        tiles.append(total)
    return jnp.concatenate(tiles, axis=1)


def spread(left, held_ref, keep_ref, send_ref, extra, tile=256):
    blocks, half, width = keep_ref.shape
    for j in range(blocks):
        for at in range(0, width, tile):
            part = jnp.dot(left, held_ref[j, :, at : at + tile], preferred_element_type=F32)
            keep_ref[j, :, at : at + tile] = part[:half]
            send_ref[j, :, at : at + tile] = part[half:].astype(BF16)
        if extra is not None:
            send_ref[j, :, width:] = extra


def project_kernel(count, *refs):
    refs[-1][...] = project(refs[:count], refs[count])


def peak_lanes(peak, half):
    return into_lanes([peak[half:, :1]], half)


def pool_kernel(count, length_ref, *refs):
    parts, refs = refs[:count], refs[count:]
    part_ref, held_ref, spread_ref, keep_ref, send_ref, peak_ref, w_ref, left_ref = refs
    scores = part_ref[...] + project(parts, held_ref)
    shard = lax.axis_index("ctx") * lax.axis_size("cls") + lax.axis_index("cls")
    valid = lax.broadcasted_iota(jnp.int32, scores.shape, 1) < length_ref[0] - shard * scores.shape[1]
    peak = jnp.max(jnp.where(valid, scores, MASKED), axis=1, keepdims=True)
    weights = jnp.where(valid, jnp.exp(scores - peak), 0.0)
    left = weights.astype(BF16)
    w_ref[...] = weights
    left_ref[...] = left
    peak_ref[...] = jnp.broadcast_to(peak, peak_ref.shape)
    spread(left, spread_ref, keep_ref, send_ref, peak_lanes(peak, keep_ref.shape[1]))


def pool_rest_kernel(left_ref, peak_ref, held_ref, keep_ref, send_ref):
    spread(left_ref[...], held_ref, keep_ref, send_ref, peak_lanes(peak_ref[...], keep_ref.shape[1]))


def grad_kernel(scale, count, *refs):
    parts, refs = refs[:count], refs[count:]
    part_ref, held_ref, spread_ref, w_ref, peak_ref, keep_ref, send_ref, left_ref, loss_ref = refs
    width = held_ref.shape[2]
    projected = part_ref[...] + project(parts, held_ref)
    blocks = [ref[0] for ref in parts]
    top = jnp.concatenate([from_lanes(block, width, 0) for block in blocks], axis=0)
    weights = w_ref[...] * jnp.exp(peak_ref[:, :1] - top)
    left = (weights * projected).astype(BF16)
    left_ref[...] = left
    spread(left, spread_ref, keep_ref, send_ref, None)
    loss_ref[...] = tree_sum([from_lanes(block, width, 1)[:1] for block in blocks]) * scale


def grad_rest_kernel(left_ref, held_ref, keep_ref, send_ref):
    spread(left_ref[...], held_ref, keep_ref, send_ref, None)


def rescaling(peak, received, width):
    if peak is None:
        return None, None
    others = [from_lanes(block, width, 0) for block in received]
    top = peak
    for other in others:
        top = jnp.maximum(top, other)
    return top, [jnp.exp(p - top) for p in [peak, *others]]


def total_of(keep, received, factors):
    total = keep if factors is None else keep * factors[0]
    for i, block in enumerate(received):
        block = block[:, : keep.shape[1]].astype(F32)
        total = total + (block if factors is None else block * factors[i + 1])
    return total


def put(ref, j, total, lanes):
    width = total.shape[1]
    ref[j, :, :width] = total.astype(BF16)
    if lanes is not None:
        ref[j, :, width:] = lanes


def core_kernel(peaks, first, *refs):
    keep_ref, recv_ref, *refs = refs
    peak = refs.pop(0)[: keep_ref.shape[1], :1] if peaks else None
    refs = refs if first else refs[1:-1]
    top_ref = refs.pop() if peaks and first else None
    width = keep_ref.shape[2]
    rows = refs[0].shape[1]
    top, factors = rescaling(peak, [recv_ref[0]], width)
    lanes = into_lanes([top], top.shape[0]) if peaks else None
    for j in range(keep_ref.shape[0]):
        total = total_of(keep_ref[j], [recv_ref[j]], factors)
        for k, ref in enumerate(refs):
            at = slice(k * rows, (k + 1) * rows)
            if first and k == 0:
                ref[j] = total[at]
            else:
                put(ref, j, total[at], lanes[at] if peaks else None)
    if peaks and first:
        top_ref[...] = jnp.broadcast_to(top[:rows], top_ref.shape)


def near_sum_kernel(peaks, count, steps, *refs):
    keep_ref, *refs = refs
    received, refs = refs[:count], refs[count:]
    peak = refs.pop(0)[:, :1] if peaks else None
    top_ref = refs.pop() if peaks else None
    top, factors = rescaling(peak, [ref[0] for ref in received], keep_ref.shape[2])
    lanes = into_lanes([top], top.shape[0]) if peaks else None
    for p in range(keep_ref.shape[0]):
        total = total_of(keep_ref[p], [ref[p] for ref in received], factors)
        if p == 0:
            refs[0][0] = total
        else:
            put(refs[steps.index((2 * p, 0)) + 1], 0, total, lanes)
    if peaks:
        top_ref[...] = jnp.broadcast_to(top, top_ref.shape)


def scatter_sum(halves, peak):
    peaks = peak is not None
    near, far = near_steps(), far_steps()
    across = (len(near) + 1) // 2
    blocks, half, width = halves[0][0].shape
    lanes = halves[0][1].shape[2]
    rows = half // across
    top_out = [((rows, LANES), F32)] if peaks else []
    part = ((blocks, rows, lanes), BF16)
    (keep_a, send_a), (keep_b, send_b) = halves
    args = [keep_b, swap(send_b, 0, 1)] + ([peak] if peaks else []) + [send_a]
    outs = [part] * across + [((blocks, half, lanes), BF16)]
    *parts_b, send_a = call(
        functools.partial(core_kernel, peaks, False), outs, "core_sum", args, aliases={len(args) - 1: across}
    )
    args = [keep_a, swap(send_a, 0, 1)] + ([peak] if peaks else [])
    outs = [((blocks, rows, width), F32)] + [part] * (across - 1) + top_out
    out = call(functools.partial(core_kernel, peaks, True), outs, "core_sum", args)
    parts = {(i, 2 * k): x for i, group in enumerate((out, parts_b)) for k, x in enumerate(group[:across])}
    received = [swap(parts[step], *step) for step in near]
    outs = [((1, rows, width), F32)] + [((1, rows, lanes), BF16)] * len(far) + top_out
    args = [parts[0, 0], *received] + (out[-1:] if peaks else [])
    out = call(functools.partial(near_sum_kernel, peaks, len(received), far), outs, "near_sum", args)
    received = [swap(x, *step) for x, step in zip(out[1:], far)]
    return [out[0], *received] + (out[-1:] if peaks else [])


def far_sum_kernel(*refs):
    keep_ref, *received, out_ref = refs
    out_ref[...] = total_of(keep_ref[0], [ref[0] for ref in received], None)


def head_mask(shape, attributes):
    row = lax.broadcasted_iota(jnp.int32, shape, 0)
    column = lax.broadcasted_iota(jnp.int32, shape, 1)
    return column // attributes == row


def head_sums_kernel(*refs):
    keep_ref, *received, peak_ref, gain_ref, weight_ref, sums_ref, pooled_ref, top_ref = refs
    received = [ref[0] for ref in received]
    top, factors = rescaling(peak_ref[:, :1], received, keep_ref.shape[2])
    pooled = total_of(keep_ref[0], received, factors)
    pooled_ref[...] = pooled
    top_ref[...] = jnp.broadcast_to(top, top_ref.shape)
    scaled_b = (pooled * gain_ref[...]).astype(BF16)
    product = jnp.dot(scaled_b, weight_ref[...], preferred_element_type=F32)
    mask = head_mask(product.shape, product.shape[1] // product.shape[0])
    squares = jnp.sum(pooled * pooled, axis=1, keepdims=True)
    product_flat = jnp.sum(jnp.where(mask, product, 0.0), axis=0, keepdims=True)
    squares_flat = jnp.sum(jnp.where(mask, squares, 0.0), axis=0, keepdims=True)
    sums_ref[0:1, :] = product_flat
    sums_ref[1:2, :] = squares_flat


def tree_sum(level):
    while len(level) > 1:
        level = [a + b for a, b in zip(level[::2], level[1::2])]
    return level[0]


def tree_sum_kernel(*refs):
    refs[-1][...] = tree_sum([ref[...] for ref in refs[:-1]])


def head_grads_kernel(full_width, sums_ref, other_sums_ref, *refs):
    pooled_ref, top_ref, gain_ref, weight_ref, bias_ref, label_ref, *refs = refs
    bias_grad_ref, copy_ref, grad_ref, normed_ref = refs
    pooled, gain = pooled_ref[...], gain_ref[...]
    heads, width = pooled.shape
    columns = bias_ref.shape[1]
    sums = sums_ref[...] + other_sums_ref[...]
    mask = head_mask((heads, columns), columns // heads)
    inverse_flat = lax.rsqrt(sums[1:2] / full_width + 1e-05)
    inverse_rms = jnp.max(jnp.where(mask, inverse_flat, 0.0), axis=1, keepdims=True)
    product = inverse_flat * sums[0:1]
    logits = product + bias_ref[...]
    target = label_ref[...].astype(F32)
    losses = jnp.maximum(logits, 0.0) + jnp.log1p(jnp.exp(-jnp.abs(logits))) - target * logits
    loss = jnp.sum(losses, axis=1, keepdims=True)
    bias_grad = jax.nn.sigmoid(logits) - target
    bias_grad_ref[...] = bias_grad
    copy_ref[...] = bias_grad
    by_head = jnp.where(mask, bias_grad, 0.0)
    high = by_head.astype(BF16)
    low = (by_head - high.astype(F32)).astype(BF16)
    both = jnp.concatenate([high, low], axis=0)
    back = lax.dot_general(both, weight_ref[...], (((1,), (1,)), ((), ())), preferred_element_type=F32)
    normed_grad = (back[:heads] + back[heads:]) * gain
    inner = jnp.sum(by_head * product, axis=1, keepdims=True) / full_width
    unit = pooled * inverse_rms
    grad_ref[:, :width] = (inverse_rms * (normed_grad - unit * inner)).astype(BF16)
    grad_ref[:, width:] = into_lanes([top_ref[:, :1], jnp.broadcast_to(loss, (heads, 1))], heads)
    normed_ref[...] = unit * gain


def head_weight_grad_kernel(attributes, normed_ref, bias_grad_ref, out_ref):
    heads = normed_ref.shape[0]
    columns = out_ref.shape[1]
    parts = jnp.concatenate(pieces(normed_ref[...]), axis=0)
    row = lax.broadcasted_iota(jnp.int32, (3 * heads, columns), 0) % heads
    column = pl.program_id(0) * columns + lax.broadcasted_iota(jnp.int32, (3 * heads, columns), 1)
    ones = jnp.where(column // attributes == row, 1.0, 0.0).astype(BF16)
    normed = lax.dot_general(parts, ones, (((0,), (0,)), ((), ())), preferred_element_type=F32)
    out_ref[...] = normed * bias_grad_ref[...]


def head_weight_grad(normed, bias_grad):
    rows, width = normed.shape
    columns = bias_grad.shape[1]
    block = columns // 4
    return pl.pallas_call(
        functools.partial(head_weight_grad_kernel, columns // rows),
        out_shape=jax.ShapeDtypeStruct((width, columns), F32),
        grid=(columns // block,),
        in_specs=[
            pl.BlockSpec((rows, width), lambda i: (0, 0)),
            pl.BlockSpec((1, block), lambda i: (0, i)),
        ],
        out_specs=pl.BlockSpec((width, block), lambda i: (0, i)),
        compiler_params=pltpu.CompilerParams(vmem_limit_bytes=16 * MIB),
        name="head_weight_grad",
    )(normed, bias_grad)


def shards(tokens, doc_length, queries, norm_gain, head_weight, head_bias, labels):
    contexts, classes = lax.axis_size("ctx"), lax.axis_size("cls")
    token_count = tokens.shape[0]
    rows, width = queries.shape
    full_width = width * contexts
    heads = rows * classes
    half = heads // 2
    columns = labels.shape[0]
    blocks = contexts // 2
    pair = [((blocks, half, width), F32), ((blocks, half, width + LANES), BF16)]
    product = ((heads, token_count), F32)
    cost = pl.CostEstimate(flops=256 * token_count * full_width, bytes_accessed=0, transcendentals=0)

    def project_half(parts):
        return call(functools.partial(project_kernel, len(parts)), [product], "project", [*parts, held_b], cost=cost)[0]

    held_a, held_b, queries_here, gain = load(width, tokens, queries, norm_gain[None, :])
    first, second = gather(queries, queries_here)
    part = project_half(second)
    keep_b, send_b, own_peak, weights, left = call(
        functools.partial(pool_kernel, classes),
        [*pair, ((heads, LANES), F32), product, ((heads, token_count), BF16)],
        "pool",
        [doc_length, *first, part, held_a, held_b],
        smem_args=(0,),
        cost=cost,
    )
    half_a = call(pool_rest_kernel, pair, "pool_rest", [left, own_peak, held_a], cost=cost)
    parts = scatter_sum([half_a, (keep_b, send_b)], own_peak)
    sums, pooled, top = call(
        head_sums_kernel,
        [((2, columns), F32), ((rows, width), F32), ((rows, LANES), F32)],
        "head_sums",
        [*parts, gain, head_weight],
    )
    far_sums = [swap(sums, *step) for step in far_steps()[::-1]]
    (sums,) = call(tree_sum_kernel, [((2, columns), F32)], "tree_sum", [sums, *far_sums])
    bias_grad, bias_grad_here, pooled_grad, normed = call(
        functools.partial(head_grads_kernel, full_width),
        [((1, columns), F32), ((1, columns), F32), ((rows, width + LANES), BF16), ((rows, width), F32)],
        "head_grads",
        [sums, swap(sums, 1, 0), pooled, top, gain, head_weight, head_bias[None, :], labels[None, :]],
    )
    head_grad = head_weight_grad(normed, bias_grad_here)
    first, second = gather(pooled_grad)
    part = project_half(second)
    pair = [((blocks, half, width), F32), ((blocks, half, width), BF16)]
    keep_b, send_b, left, loss = call(
        functools.partial(grad_kernel, 1.0 / (columns * classes), classes),
        [*pair, ((heads, token_count), BF16), ((1, 1), F32)],
        "grad",
        [*first, part, held_a, held_b, weights, own_peak],
        cost=cost,
    )
    half_a = call(grad_rest_kernel, pair, "grad_rest", [left, held_a], cost=cost)
    parts = scatter_sum([half_a, (keep_b, send_b)], None)
    (query_grad,) = call(far_sum_kernel, [((rows, width), F32)], "far_sum", parts)
    return (loss.reshape(()), query_grad, head_grad, bias_grad.reshape(-1))


def solution(mesh):
    return jax.shard_map(
        shards,
        mesh=mesh,
        in_specs=(
            P(("ctx", "cls"), None),
            P(),
            P("cls", "ctx"),
            P("ctx"),
            P("ctx", "cls"),
            P("cls"),
            P("cls"),
        ),
        out_specs=(P(), P("cls", "ctx"), P("ctx", "cls"), P("cls")),
        check_vma=False,
    )
```

```python
import functools

import jax
import jax.numpy as jnp
from jax import lax
from jax.experimental import pallas as pl
from jax.experimental.pallas import tpu as pltpu
from jax.sharding import PartitionSpec as P

F32 = jnp.float32
BF16 = jnp.bfloat16
LANES = 128
MASKED = -1e30
MIB = 1024 * 1024


def swap(x, ctx_bits, cls_bits):
    contexts, classes = lax.axis_size("ctx"), lax.axis_size("cls")
    pairs = [
        (c * classes + k, (c ^ ctx_bits) * classes + (k ^ cls_bits)) for c in range(contexts) for k in range(classes)
    ]
    return lax.ppermute(x, ("ctx", "cls"), pairs)


def far_steps():
    return [(2 * j, 0) for j in reversed(range(1, lax.axis_size("ctx") // 2))]


def near_steps():
    steps = [(i, 2 * k) for i in range(2) for k in range(lax.axis_size("cls") // 2) if i or k]
    return sorted(steps, key=lambda step: (not (step[0] and step[1]), not step[0]))


def call(kernel, outs, name, args, smem_args=(), aliases=None, limit=16, cost=None):
    def spec(i):
        if i in smem_args:
            return pl.BlockSpec(memory_space=pltpu.SMEM)
        return pl.BlockSpec(memory_space=pltpu.VMEM)

    run = pl.pallas_call(
        kernel,
        out_shape=[jax.ShapeDtypeStruct(s, d) for s, d in outs],
        in_specs=[spec(i) for i in range(len(args))],
        out_specs=[pl.BlockSpec(memory_space=pltpu.VMEM)] * len(outs),
        input_output_aliases=aliases or {},
        compiler_params=pltpu.CompilerParams(vmem_limit_bytes=limit * MIB),
        cost_estimate=cost,
        name=name,
    )
    return list(run(*args))


def stack_kernel(*refs):
    out_ref = refs[-1]
    for at, ref in enumerate(refs[:-1]):
        out_ref[at] = ref[...].reshape(out_ref.shape[1:])


def gather(block, local=None):
    far = [swap(block, *step) for step in far_steps()[::-1]]
    rows, width = block.shape
    (held,) = call(
        stack_kernel, [((len(far) + 1, rows, width), block.dtype)], "stack", [block if local is None else local, *far]
    )
    parts = {step: swap(held, *step) for step in near_steps()[::-1]}
    parts[0, 0] = held
    other = {step: swap(part, 0, 1) for step, part in parts.items()}
    steps = sorted(parts)
    return [[group[step] for group in (parts, other) for step in steps if step[0] == i] for i in range(2)]


def pieces(x):
    high = x.astype(BF16)
    rest = x - high.astype(F32)
    middle = rest.astype(BF16)
    return high, middle, (rest - middle.astype(F32)).astype(BF16)


def into_lanes(columns, rows):
    lane = lax.broadcasted_iota(jnp.int32, (rows, LANES), 1)
    out = jnp.zeros((rows, LANES), F32)
    for i, column in enumerate(columns):
        for j, piece in enumerate(pieces(column)):
            out = jnp.where(lane == 3 * i + j, piece.astype(F32), out)
    return out.astype(BF16)


def from_lanes(block, width, i):
    at = width + 3 * i
    block = block.astype(F32)
    return block[:, at : at + 1] + (block[:, at + 1 : at + 2] + block[:, at + 2 : at + 3])


def token_copies(tokens_ref, held_ref, sems, half, first):
    blocks, _, width = held_ref.shape
    copies = []
    for j in range(blocks):
        start = pl.multiple_of((lax.axis_index("ctx") ^ half ^ (2 * (first + j))) * width, LANES)
        copies.append(pltpu.make_async_copy(tokens_ref.at[:, pl.ds(start, width)], held_ref.at[j], sems.at[j]))
    return copies


def load_kernel(*refs):
    tokens_ref, queries_ref, gain_ref, length_ref, a_ref, b_ref, here_ref, gain_here_ref, length_out_ref = refs[:9]
    sems_a, sems_b, sems = refs[9:]
    copies = [
        pltpu.make_async_copy(queries_ref, here_ref, sems.at[0]),
        pltpu.make_async_copy(gain_ref, gain_here_ref, sems.at[1]),
        *token_copies(tokens_ref, a_ref, sems_a, 0, 0),
        *token_copies(tokens_ref, b_ref, sems_b, 1, 0),
    ]
    for copy in copies:
        copy.start()
    length_out_ref[...] = jnp.full(length_out_ref.shape, length_ref[0], jnp.int32)
    for copy in copies:
        copy.wait()


def in_vmem(kernel, outs, name, hbm_args, other_args, other_space, scratch):
    specs = [pl.BlockSpec(memory_space=pltpu.HBM)] * len(hbm_args)
    run = pl.pallas_call(
        kernel,
        out_shape=[pltpu.VMEM(*out) for out in outs],
        in_specs=specs + [pl.BlockSpec(memory_space=other_space)] * len(other_args),
        out_specs=[pl.BlockSpec(memory_space=pltpu.VMEM)] * len(outs),
        scratch_shapes=scratch,
        compiler_params=pltpu.CompilerParams(vmem_limit_bytes=16 * MIB),
        name=name,
    )
    return run(*[pltpu.with_memory_space_constraint(x, pltpu.HBM) for x in hbm_args], *other_args)


def load(width, tokens, queries, gain, length):
    rows, full_width = tokens.shape
    blocks = full_width // width // 2
    now = blocks - blocks // 2
    outs = [((blocks, rows, width), BF16), ((now, rows, width), BF16), (queries.shape, BF16), (gain.shape, F32)]
    dma = pltpu.SemaphoreType.DMA
    scratch = [dma((blocks,)), dma((now,)), dma((2,))]
    outs.append(((1, LANES), jnp.int32))
    return in_vmem(load_kernel, outs, "load", [tokens, queries, gain], [length], pltpu.SMEM, scratch)


def project_load_kernel(first, count, tokens_ref, *refs):
    parts, (held_ref, out_ref, rest_ref, sems) = refs[:count], refs[count:]
    copies = token_copies(tokens_ref, rest_ref, sems, 1, first)
    for copy in copies:
        copy.start()
    out_ref[...] = project(parts, [held_ref])
    for copy in copies:
        copy.wait()


def project(parts, held, tile=256):
    blocks = [(ref, j) for ref in held for j in range(ref.shape[0])]
    _, token_count, width = held[0].shape
    tiles = []
    for at in range(0, token_count, tile):
        total = None
        for j, (ref, own) in enumerate(blocks):
            left = jnp.concatenate([part[j] for part in parts], axis=0)[:, :width]
            block = ref[own, at : at + tile, :]
            part = lax.dot_general(left, block, (((1,), (1,)), ((), ())), preferred_element_type=F32)
            total = part if total is None else total + part
        tiles.append(total)
    return jnp.concatenate(tiles, axis=1)


def spread(left, held, keep_ref, send_ref, extra, tile=256):
    blocks = [(ref, j) for ref in held for j in range(ref.shape[0])]
    _, half, width = keep_ref.shape
    for j, (ref, own) in enumerate(blocks):
        for at in range(0, width, tile):
            part = jnp.dot(left, ref[own, :, at : at + tile], preferred_element_type=F32)
            keep_ref[j, :, at : at + tile] = part[:half]
            send_ref[j, :, at : at + tile] = part[half:].astype(BF16)
        if extra is not None:
            send_ref[j, :, width:] = extra


def project_kernel(count, *refs):
    refs[-1][...] = project(refs[:count], [refs[count]])


def peak_lanes(peak, half):
    return into_lanes([peak[half:, :1]], half)


def pool_kernel(count, length_ref, *refs):
    parts, held, refs = refs[:count], refs[count : count + 2], refs[count + 2 :]
    part_ref, keep_ref, send_ref, peak_ref, w_ref, left_ref = refs
    scores = part_ref[...] + project(parts, held)
    shard = lax.axis_index("ctx") * lax.axis_size("cls") + lax.axis_index("cls")
    valid = lax.broadcasted_iota(jnp.int32, scores.shape, 1) < length_ref[:, :1] - shard * scores.shape[1]
    peak = jnp.max(jnp.where(valid, scores, MASKED), axis=1, keepdims=True)
    weights = jnp.where(valid, jnp.exp(scores - peak), 0.0)
    left = weights.astype(BF16)
    w_ref[...] = weights
    left_ref[...] = left
    peak_ref[...] = jnp.broadcast_to(peak, peak_ref.shape)
    spread(left, held, keep_ref, send_ref, peak_lanes(peak, keep_ref.shape[1]))


def pool_rest_kernel(left_ref, peak_ref, held_ref, keep_ref, send_ref):
    spread(left_ref[...], [held_ref], keep_ref, send_ref, peak_lanes(peak_ref[...], keep_ref.shape[1]))


def grad_kernel(scale, count, *refs):
    parts, held, refs = refs[:count], refs[count : count + 2], refs[count + 2 :]
    part_ref, w_ref, peak_ref, keep_ref, send_ref, left_ref, loss_ref = refs
    width = held[0].shape[2]
    projected = part_ref[...] + project(parts, held)
    blocks = [ref[0] for ref in parts]
    top = jnp.concatenate([from_lanes(block, width, 0) for block in blocks], axis=0)
    weights = w_ref[...] * jnp.exp(peak_ref[:, :1] - top)
    left = (weights * projected).astype(BF16)
    left_ref[...] = left
    spread(left, held, keep_ref, send_ref, None)
    loss_ref[...] = tree_sum([from_lanes(block, width, 1)[:1] for block in blocks]) * scale


def grad_rest_kernel(left_ref, held_ref, keep_ref, send_ref):
    spread(left_ref[...], [held_ref], keep_ref, send_ref, None)


def rescaling(peak, received, width):
    if peak is None:
        return None, None
    others = [from_lanes(block, width, 0) for block in received]
    top = peak
    for other in others:
        top = jnp.maximum(top, other)
    return top, [jnp.exp(p - top) for p in [peak, *others]]


def total_of(keep, received, factors):
    total = keep if factors is None else keep * factors[0]
    for i, block in enumerate(received):
        block = block[:, : keep.shape[1]].astype(F32)
        total = total + (block if factors is None else block * factors[i + 1])
    return total


def put(ref, j, total, lanes):
    width = total.shape[1]
    ref[j, :, :width] = total.astype(BF16)
    if lanes is not None:
        ref[j, :, width:] = lanes


def core_kernel(peaks, first, *refs):
    keep_ref, recv_ref, *refs = refs
    peak = refs.pop(0)[: keep_ref.shape[1], :1] if peaks else None
    refs = refs if first else refs[1:-1]
    top_ref = refs.pop() if peaks and first else None
    width = keep_ref.shape[2]
    rows = refs[0].shape[1]
    top, factors = rescaling(peak, [recv_ref[0]], width)
    lanes = into_lanes([top], top.shape[0]) if peaks else None
    for j in range(keep_ref.shape[0]):
        total = total_of(keep_ref[j], [recv_ref[j]], factors)
        for k, ref in enumerate(refs):
            at = slice(k * rows, (k + 1) * rows)
            if first and k == 0:
                ref[j] = total[at]
            else:
                put(ref, j, total[at], lanes[at] if peaks else None)
    if peaks and first:
        top_ref[...] = jnp.broadcast_to(top[:rows], top_ref.shape)


def near_sum_kernel(peaks, count, steps, *refs):
    keep_ref, *refs = refs
    received, refs = refs[:count], refs[count:]
    peak = refs.pop(0)[:, :1] if peaks else None
    top_ref = refs.pop() if peaks else None
    top, factors = rescaling(peak, [ref[0] for ref in received], keep_ref.shape[2])
    lanes = into_lanes([top], top.shape[0]) if peaks else None
    for p in range(keep_ref.shape[0]):
        total = total_of(keep_ref[p], [ref[p] for ref in received], factors)
        if p == 0:
            refs[0][0] = total
        else:
            put(refs[steps.index((2 * p, 0)) + 1], 0, total, lanes)
    if peaks:
        top_ref[...] = jnp.broadcast_to(top, top_ref.shape)


def scatter_sum(halves, peak):
    peaks = peak is not None
    near, far = near_steps(), far_steps()
    across = (len(near) + 1) // 2
    blocks, half, width = halves[0][0].shape
    lanes = halves[0][1].shape[2]
    rows = half // across
    top_out = [((rows, LANES), F32)] if peaks else []
    part = ((blocks, rows, lanes), BF16)
    (keep_a, send_a), (keep_b, send_b) = halves
    args = [keep_b, swap(send_b, 0, 1)] + ([peak] if peaks else []) + [send_a]
    outs = [part] * across + [((blocks, half, lanes), BF16)]
    *parts_b, send_a = call(
        functools.partial(core_kernel, peaks, False), outs, "core_sum", args, aliases={len(args) - 1: across}
    )
    args = [keep_a, swap(send_a, 0, 1)] + ([peak] if peaks else [])
    outs = [((blocks, rows, width), F32)] + [part] * (across - 1) + top_out
    out = call(functools.partial(core_kernel, peaks, True), outs, "core_sum", args)
    parts = {(i, 2 * k): x for i, group in enumerate((out, parts_b)) for k, x in enumerate(group[:across])}
    received = [swap(parts[step], *step) for step in near]
    outs = [((1, rows, width), F32)] + [((1, rows, lanes), BF16)] * len(far) + top_out
    args = [parts[0, 0], *received] + (out[-1:] if peaks else [])
    out = call(functools.partial(near_sum_kernel, peaks, len(received), far), outs, "near_sum", args)
    received = [swap(x, *step) for x, step in zip(out[1:], far)]
    return [out[0], *received] + (out[-1:] if peaks else [])


def far_sum_kernel(*refs):
    keep_ref, *received, out_ref = refs
    out_ref[...] = total_of(keep_ref[0], [ref[0] for ref in received], None)


def head_mask(shape, attributes):
    row = lax.broadcasted_iota(jnp.int32, shape, 0)
    column = lax.broadcasted_iota(jnp.int32, shape, 1)
    return column // attributes == row


def head_sums_kernel(*refs):
    keep_ref, *received, peak_ref, gain_ref, weight_ref, sums_ref, pooled_ref, top_ref = refs
    received = [ref[0] for ref in received]
    top, factors = rescaling(peak_ref[:, :1], received, keep_ref.shape[2])
    pooled = total_of(keep_ref[0], received, factors)
    pooled_ref[...] = pooled
    top_ref[...] = jnp.broadcast_to(top, top_ref.shape)
    scaled_b = (pooled * gain_ref[...]).astype(BF16)
    product = jnp.dot(scaled_b, weight_ref[...], preferred_element_type=F32)
    mask = head_mask(product.shape, product.shape[1] // product.shape[0])
    squares = jnp.sum(pooled * pooled, axis=1, keepdims=True)
    product_flat = jnp.sum(jnp.where(mask, product, 0.0), axis=0, keepdims=True)
    squares_flat = jnp.sum(jnp.where(mask, squares, 0.0), axis=0, keepdims=True)
    sums_ref[0:1, :] = product_flat
    sums_ref[1:2, :] = squares_flat


def tree_sum(level):
    while len(level) > 1:
        level = [a + b for a, b in zip(level[::2], level[1::2])]
    return level[0]


def tree_sum_kernel(*refs):
    refs[-1][...] = tree_sum([ref[...] for ref in refs[:-1]])


def head_grads_kernel(full_width, sums_ref, other_sums_ref, *refs):
    pooled_ref, top_ref, gain_ref, weight_ref, bias_ref, label_ref, *refs = refs
    bias_grad_ref, copy_ref, grad_ref, normed_ref = refs
    pooled, gain = pooled_ref[...], gain_ref[...]
    heads, width = pooled.shape
    columns = bias_ref.shape[1]
    sums = sums_ref[...] + other_sums_ref[...]
    mask = head_mask((heads, columns), columns // heads)
    inverse_flat = lax.rsqrt(sums[1:2] / full_width + 1e-05)
    inverse_rms = jnp.max(jnp.where(mask, inverse_flat, 0.0), axis=1, keepdims=True)
    product = inverse_flat * sums[0:1]
    logits = product + bias_ref[...]
    target = label_ref[...].astype(F32)
    losses = jnp.maximum(logits, 0.0) + jnp.log1p(jnp.exp(-jnp.abs(logits))) - target * logits
    loss = jnp.sum(losses, axis=1, keepdims=True)
    bias_grad = jax.nn.sigmoid(logits) - target
    bias_grad_ref[...] = bias_grad
    copy_ref[...] = bias_grad
    by_head = jnp.where(mask, bias_grad, 0.0)
    high = by_head.astype(BF16)
    low = (by_head - high.astype(F32)).astype(BF16)
    both = jnp.concatenate([high, low], axis=0)
    back = lax.dot_general(both, weight_ref[...], (((1,), (1,)), ((), ())), preferred_element_type=F32)
    normed_grad = (back[:heads] + back[heads:]) * gain
    inner = jnp.sum(by_head * product, axis=1, keepdims=True) / full_width
    unit = pooled * inverse_rms
    grad_ref[:, :width] = (inverse_rms * (normed_grad - unit * inner)).astype(BF16)
    grad_ref[:, width:] = into_lanes([top_ref[:, :1], jnp.broadcast_to(loss, (heads, 1))], heads)
    normed_ref[...] = unit * gain


def head_weight_grad_kernel(attributes, normed_ref, bias_grad_ref, out_ref):
    heads = normed_ref.shape[0]
    columns = out_ref.shape[1]
    parts = jnp.concatenate(pieces(normed_ref[...]), axis=0)
    row = lax.broadcasted_iota(jnp.int32, (3 * heads, columns), 0) % heads
    column = pl.program_id(0) * columns + lax.broadcasted_iota(jnp.int32, (3 * heads, columns), 1)
    ones = jnp.where(column // attributes == row, 1.0, 0.0).astype(BF16)
    normed = lax.dot_general(parts, ones, (((0,), (0,)), ((), ())), preferred_element_type=F32)
    out_ref[...] = normed * bias_grad_ref[...]


def head_weight_grad(normed, bias_grad):
    rows, width = normed.shape
    columns = bias_grad.shape[1]
    block = columns // 4
    return pl.pallas_call(
        functools.partial(head_weight_grad_kernel, columns // rows),
        out_shape=jax.ShapeDtypeStruct((width, columns), F32),
        grid=(columns // block,),
        in_specs=[
            pl.BlockSpec((rows, width), lambda i: (0, 0)),
            pl.BlockSpec((1, block), lambda i: (0, i)),
        ],
        out_specs=pl.BlockSpec((width, block), lambda i: (0, i)),
        compiler_params=pltpu.CompilerParams(vmem_limit_bytes=16 * MIB),
        name="head_weight_grad",
    )(normed, bias_grad)


def shards(tokens, doc_length, queries, norm_gain, head_weight, head_bias, labels):
    contexts, classes = lax.axis_size("ctx"), lax.axis_size("cls")
    token_count = tokens.shape[0]
    rows, width = queries.shape
    full_width = width * contexts
    heads = rows * classes
    half = heads // 2
    columns = labels.shape[0]
    blocks = contexts // 2
    pair = [((blocks, half, width), F32), ((blocks, half, width + LANES), BF16)]
    product = ((heads, token_count), F32)
    cost = pl.CostEstimate(flops=256 * token_count * full_width, bytes_accessed=0, transcendentals=0)

    held_a, held_b, queries_here, gain, length = load(width, tokens, queries, norm_gain[None, :], doc_length)
    first, second = gather(queries, queries_here)
    now = held_b.shape[0]
    rest = (blocks - now, token_count, width)
    part, held_c = in_vmem(
        functools.partial(project_load_kernel, now, classes),
        [product, (rest, BF16)],
        "project_load",
        [tokens],
        [*first, held_a],
        pltpu.VMEM,
        [pltpu.SemaphoreType.DMA((blocks - now,))],
    )
    keep_b, send_b, own_peak, weights, left = call(
        functools.partial(pool_kernel, classes),
        [*pair, ((heads, LANES), F32), product, ((heads, token_count), BF16)],
        "pool",
        [length, *second, held_b, held_c, part],
        cost=cost,
    )
    half_a = call(pool_rest_kernel, pair, "pool_rest", [left, own_peak, held_a], cost=cost)
    parts = scatter_sum([half_a, (keep_b, send_b)], own_peak)
    sums, pooled, top = call(
        head_sums_kernel,
        [((2, columns), F32), ((rows, width), F32), ((rows, LANES), F32)],
        "head_sums",
        [*parts, gain, head_weight],
    )
    far_sums = [swap(sums, *step) for step in far_steps()[::-1]]
    (sums,) = call(tree_sum_kernel, [((2, columns), F32)], "tree_sum", [sums, *far_sums])
    bias_grad, bias_grad_here, pooled_grad, normed = call(
        functools.partial(head_grads_kernel, full_width),
        [((1, columns), F32), ((1, columns), F32), ((rows, width + LANES), BF16), ((rows, width), F32)],
        "head_grads",
        [sums, swap(sums, 1, 0), pooled, top, gain, head_weight, head_bias[None, :], labels[None, :]],
    )
    head_grad = head_weight_grad(normed, bias_grad_here)
    first, second = gather(pooled_grad)
    (part,) = call(
        functools.partial(project_kernel, classes), [product], "project", [*first, held_a], cost=cost
    )
    pair = [((blocks, half, width), F32), ((blocks, half, width), BF16)]
    keep_b, send_b, left, loss = call(
        functools.partial(grad_kernel, 1.0 / (columns * classes), classes),
        [*pair, ((heads, token_count), BF16), ((1, 1), F32)],
        "grad",
        [*second, held_b, held_c, part, weights, own_peak],
        cost=cost,
    )
    half_a = call(grad_rest_kernel, pair, "grad_rest", [left, held_a], cost=cost)
    parts = scatter_sum([half_a, (keep_b, send_b)], None)
    (query_grad,) = call(far_sum_kernel, [((rows, width), F32)], "far_sum", parts)
    return (loss.reshape(()), query_grad, head_grad, bias_grad.reshape(-1))


def solution(mesh):
    return jax.shard_map(
        shards,
        mesh=mesh,
        in_specs=(
            P(("ctx", "cls"), None),
            P(),
            P("cls", "ctx"),
            P("ctx"),
            P("ctx", "cls"),
            P("cls"),
            P("cls"),
        ),
        out_specs=(P(), P("cls", "ctx"), P("ctx", "cls"), P("cls")),
        check_vma=False,
    )
```

```python
import functools

import jax
import jax.numpy as jnp
from jax import lax
from jax.experimental import pallas as pl
from jax.experimental.pallas import tpu as pltpu
from jax.sharding import PartitionSpec as P

F32 = jnp.float32
BF16 = jnp.bfloat16
LANES = 128
MASKED = -1e30
MIB = 1024 * 1024


def swap(x, ctx_bits, cls_bits):
    contexts, classes = lax.axis_size("ctx"), lax.axis_size("cls")
    pairs = [
        (c * classes + k, (c ^ ctx_bits) * classes + (k ^ cls_bits)) for c in range(contexts) for k in range(classes)
    ]
    return lax.ppermute(x, ("ctx", "cls"), pairs)


def far_steps():
    return [(2 * j, 0) for j in reversed(range(1, lax.axis_size("ctx") // 2))]


def near_steps():
    steps = [(i, 2 * k) for i in range(2) for k in range(lax.axis_size("cls") // 2) if i or k]
    return sorted(steps, key=lambda step: (not (step[0] and step[1]), not step[0]))


def call(kernel, outs, name, args, smem_args=(), aliases=None, limit=16, cost=None):
    def spec(i):
        if i in smem_args:
            return pl.BlockSpec(memory_space=pltpu.SMEM)
        return pl.BlockSpec(memory_space=pltpu.VMEM)

    run = pl.pallas_call(
        kernel,
        out_shape=[jax.ShapeDtypeStruct(s, d) for s, d in outs],
        in_specs=[spec(i) for i in range(len(args))],
        out_specs=[pl.BlockSpec(memory_space=pltpu.VMEM)] * len(outs),
        input_output_aliases=aliases or {},
        compiler_params=pltpu.CompilerParams(vmem_limit_bytes=limit * MIB),
        cost_estimate=cost,
        name=name,
    )
    return list(run(*args))


def stack_kernel(*refs):
    out_ref = refs[-1]
    for at, ref in enumerate(refs[:-1]):
        out_ref[at] = ref[...].reshape(out_ref.shape[1:])


def gather(block, local=None):
    far = [swap(block, *step) for step in far_steps()[::-1]]
    rows, width = block.shape
    (held,) = call(
        stack_kernel, [((len(far) + 1, rows, width), block.dtype)], "stack", [block if local is None else local, *far]
    )
    parts = {step: swap(held, *step) for step in near_steps()[::-1]}
    parts[0, 0] = held
    other = {step: swap(part, 0, 1) for step, part in parts.items()}
    steps = sorted(parts)
    return [[group[step] for group in (parts, other) for step in steps if step[0] == i] for i in range(2)]


def pieces(x):
    high = x.astype(BF16)
    rest = x - high.astype(F32)
    middle = rest.astype(BF16)
    return high, middle, (rest - middle.astype(F32)).astype(BF16)


def into_lanes(columns, rows):
    lane = lax.broadcasted_iota(jnp.int32, (rows, LANES), 1)
    out = jnp.zeros((rows, LANES), F32)
    for i, column in enumerate(columns):
        for j, piece in enumerate(pieces(column)):
            out = jnp.where(lane == 3 * i + j, piece.astype(F32), out)
    return out.astype(BF16)


def from_lanes(block, width, i):
    at = width + 3 * i
    block = block.astype(F32)
    return block[:, at : at + 1] + (block[:, at + 1 : at + 2] + block[:, at + 2 : at + 3])


def load_kernel(tokens_ref, *refs):
    count = (len(refs) - 3) // 2
    others, halves, copies_of, sems = refs[:count], refs[count : count + 2], refs[count + 2 : -1], refs[-1]
    blocks, _, width = halves[0].shape
    copies = [pltpu.make_async_copy(src, dst, sems.at[i]) for i, (src, dst) in enumerate(zip(others, copies_of))]
    for i in range(2):
        for j in range(blocks):
            start = pl.multiple_of((lax.axis_index("ctx") ^ i ^ (2 * j)) * width, LANES)
            sem = sems.at[count + i * blocks + j]
            copies.append(pltpu.make_async_copy(tokens_ref.at[:, pl.ds(start, width)], halves[i].at[j], sem))
    for copy in copies:
        copy.start()
    for copy in copies:
        copy.wait()


def load(width, tokens, *others):
    rows, full_width = tokens.shape
    blocks = full_width // width // 2
    outs = [pltpu.VMEM((blocks, rows, width), tokens.dtype)] * 2 + [pltpu.VMEM(x.shape, x.dtype) for x in others]
    run = pl.pallas_call(
        load_kernel,
        out_shape=outs,
        in_specs=[pl.BlockSpec(memory_space=pltpu.HBM)] * (1 + len(others)),
        out_specs=[pl.BlockSpec(memory_space=pltpu.VMEM)] * len(outs),
        scratch_shapes=[pltpu.SemaphoreType.DMA((2 * blocks + len(others),))],
        compiler_params=pltpu.CompilerParams(vmem_limit_bytes=16 * MIB),
        name="load",
    )
    return run(*[pltpu.with_memory_space_constraint(x, pltpu.HBM) for x in (tokens, *others)])


def project(parts, held_ref):
    blocks, _, width = held_ref.shape
    total = None
    for j in range(blocks):
        left = jnp.concatenate([ref[j] for ref in parts], axis=0)[:, :width]
        part = lax.dot_general(left, held_ref[j], (((1,), (1,)), ((), ())), preferred_element_type=F32)
        total = part if total is None else total + part
    return total


def spread(left, held_ref, keep_ref, send_ref, extra):
    blocks, half, width = keep_ref.shape
    for j in range(blocks):
        part = jnp.dot(left, held_ref[j], preferred_element_type=F32)
        keep_ref[j] = part[:half]
        send_ref[j, :, :width] = part[half:].astype(BF16)
        if extra is not None:
            send_ref[j, :, width:] = extra


def project_kernel(count, *refs):
    refs[-1][...] = project(refs[:count], refs[count])


def peak_lanes(peak, half):
    return into_lanes([peak[half:, :1]], half)


def pool_kernel(count, length_ref, *refs):
    parts, refs = refs[:count], refs[count:]
    part_ref, held_ref, keep_ref, send_ref, peak_ref, w_ref, left_ref = refs
    scores = part_ref[...] + project(parts, held_ref)
    shard = lax.axis_index("ctx") * lax.axis_size("cls") + lax.axis_index("cls")
    valid = lax.broadcasted_iota(jnp.int32, scores.shape, 1) < length_ref[0] - shard * scores.shape[1]
    peak = jnp.max(jnp.where(valid, scores, MASKED), axis=1, keepdims=True)
    weights = jnp.where(valid, jnp.exp(scores - peak), 0.0)
    left = weights.astype(BF16)
    w_ref[...] = weights
    left_ref[...] = left
    peak_ref[...] = jnp.broadcast_to(peak, peak_ref.shape)
    spread(left, held_ref, keep_ref, send_ref, peak_lanes(peak, keep_ref.shape[1]))


def pool_rest_kernel(left_ref, peak_ref, held_ref, keep_ref, send_ref):
    spread(left_ref[...], held_ref, keep_ref, send_ref, peak_lanes(peak_ref[...], keep_ref.shape[1]))


def grad_kernel(scale, count, *refs):
    parts, refs = refs[:count], refs[count:]
    part_ref, held_ref, w_ref, peak_ref, keep_ref, send_ref, left_ref, loss_ref = refs
    width = held_ref.shape[2]
    projected = part_ref[...] + project(parts, held_ref)
    blocks = [ref[0] for ref in parts]
    top = jnp.concatenate([from_lanes(block, width, 0) for block in blocks], axis=0)
    weights = w_ref[...] * jnp.exp(peak_ref[:, :1] - top)
    left = (weights * projected).astype(BF16)
    left_ref[...] = left
    spread(left, held_ref, keep_ref, send_ref, None)
    loss_ref[...] = tree_sum([from_lanes(block, width, 1)[:1] for block in blocks]) * scale


def grad_rest_kernel(left_ref, held_ref, keep_ref, send_ref):
    spread(left_ref[...], held_ref, keep_ref, send_ref, None)


def rescaling(peak, received, width):
    if peak is None:
        return None, None
    others = [from_lanes(block, width, 0) for block in received]
    top = peak
    for other in others:
        top = jnp.maximum(top, other)
    return top, [jnp.exp(p - top) for p in [peak, *others]]


def total_of(keep, received, factors):
    total = keep if factors is None else keep * factors[0]
    for i, block in enumerate(received):
        block = block[:, : keep.shape[1]].astype(F32)
        total = total + (block if factors is None else block * factors[i + 1])
    return total


def put(ref, j, total, lanes):
    width = total.shape[1]
    ref[j, :, :width] = total.astype(BF16)
    if lanes is not None:
        ref[j, :, width:] = lanes


def core_kernel(peaks, first, *refs):
    keep_ref, recv_ref, *refs = refs
    peak = refs.pop(0)[: keep_ref.shape[1], :1] if peaks else None
    refs = refs if first else refs[1:-1]
    top_ref = refs.pop() if peaks and first else None
    width = keep_ref.shape[2]
    rows = refs[0].shape[1]
    top, factors = rescaling(peak, [recv_ref[0]], width)
    lanes = into_lanes([top], top.shape[0]) if peaks else None
    for j in range(keep_ref.shape[0]):
        total = total_of(keep_ref[j], [recv_ref[j]], factors)
        for k, ref in enumerate(refs):
            at = slice(k * rows, (k + 1) * rows)
            if first and k == 0:
                ref[j] = total[at]
            else:
                put(ref, j, total[at], lanes[at] if peaks else None)
    if peaks and first:
        top_ref[...] = jnp.broadcast_to(top[:rows], top_ref.shape)


def near_sum_kernel(peaks, count, steps, *refs):
    keep_ref, *refs = refs
    received, refs = refs[:count], refs[count:]
    peak = refs.pop(0)[:, :1] if peaks else None
    top_ref = refs.pop() if peaks else None
    top, factors = rescaling(peak, [ref[0] for ref in received], keep_ref.shape[2])
    lanes = into_lanes([top], top.shape[0]) if peaks else None
    for p in range(keep_ref.shape[0]):
        total = total_of(keep_ref[p], [ref[p] for ref in received], factors)
        if p == 0:
            refs[0][0] = total
        else:
            put(refs[steps.index((2 * p, 0)) + 1], 0, total, lanes)
    if peaks:
        top_ref[...] = jnp.broadcast_to(top, top_ref.shape)


def scatter_sum(halves, peak):
    peaks = peak is not None
    near, far = near_steps(), far_steps()
    across = (len(near) + 1) // 2
    blocks, half, width = halves[0][0].shape
    lanes = halves[0][1].shape[2]
    rows = half // across
    top_out = [((rows, LANES), F32)] if peaks else []
    part = ((blocks, rows, lanes), BF16)
    (keep_a, send_a), (keep_b, send_b) = halves
    args = [keep_b, swap(send_b, 0, 1)] + ([peak] if peaks else []) + [send_a]
    outs = [part] * across + [((blocks, half, lanes), BF16)]
    *parts_b, send_a = call(
        functools.partial(core_kernel, peaks, False), outs, "core_sum", args, aliases={len(args) - 1: across}
    )
    args = [keep_a, swap(send_a, 0, 1)] + ([peak] if peaks else [])
    outs = [((blocks, rows, width), F32)] + [part] * (across - 1) + top_out
    out = call(functools.partial(core_kernel, peaks, True), outs, "core_sum", args)
    parts = {(i, 2 * k): x for i, group in enumerate((out, parts_b)) for k, x in enumerate(group[:across])}
    received = [swap(parts[step], *step) for step in near]
    outs = [((1, rows, width), F32)] + [((1, rows, lanes), BF16)] * len(far) + top_out
    args = [parts[0, 0], *received] + (out[-1:] if peaks else [])
    out = call(functools.partial(near_sum_kernel, peaks, len(received), far), outs, "near_sum", args)
    received = [swap(x, *step) for x, step in zip(out[1:], far)]
    return [out[0], *received] + (out[-1:] if peaks else [])


def far_sum_kernel(*refs):
    keep_ref, *received, out_ref = refs
    out_ref[...] = total_of(keep_ref[0], [ref[0] for ref in received], None)


def head_mask(shape, attributes):
    row = lax.broadcasted_iota(jnp.int32, shape, 0)
    column = lax.broadcasted_iota(jnp.int32, shape, 1)
    return column // attributes == row


def head_sums_kernel(*refs):
    keep_ref, *received, peak_ref, gain_ref, weight_ref, sums_ref, pooled_ref, top_ref = refs
    received = [ref[0] for ref in received]
    top, factors = rescaling(peak_ref[:, :1], received, keep_ref.shape[2])
    pooled = total_of(keep_ref[0], received, factors)
    pooled_ref[...] = pooled
    top_ref[...] = jnp.broadcast_to(top, top_ref.shape)
    scaled_b = (pooled * gain_ref[...]).astype(BF16)
    product = jnp.dot(scaled_b, weight_ref[...], preferred_element_type=F32)
    mask = head_mask(product.shape, product.shape[1] // product.shape[0])
    squares = jnp.sum(pooled * pooled, axis=1, keepdims=True)
    product_flat = jnp.sum(jnp.where(mask, product, 0.0), axis=0, keepdims=True)
    squares_flat = jnp.sum(jnp.where(mask, squares, 0.0), axis=0, keepdims=True)
    sums_ref[0:1, :] = product_flat
    sums_ref[1:2, :] = squares_flat


def tree_sum(level):
    while len(level) > 1:
        level = [a + b for a, b in zip(level[::2], level[1::2])]
    return level[0]


def tree_sum_kernel(*refs):
    refs[-1][...] = tree_sum([ref[...] for ref in refs[:-1]])


def head_grads_kernel(full_width, sums_ref, other_sums_ref, *refs):
    pooled_ref, top_ref, gain_ref, weight_ref, bias_ref, label_ref, *refs = refs
    bias_grad_ref, copy_ref, grad_ref, normed_ref = refs
    pooled, gain = pooled_ref[...], gain_ref[...]
    heads, width = pooled.shape
    columns = bias_ref.shape[1]
    sums = sums_ref[...] + other_sums_ref[...]
    mask = head_mask((heads, columns), columns // heads)
    inverse_flat = lax.rsqrt(sums[1:2] / full_width + 1e-05)
    inverse_rms = jnp.max(jnp.where(mask, inverse_flat, 0.0), axis=1, keepdims=True)
    product = inverse_flat * sums[0:1]
    logits = product + bias_ref[...]
    target = label_ref[...].astype(F32)
    losses = jnp.maximum(logits, 0.0) + jnp.log1p(jnp.exp(-jnp.abs(logits))) - target * logits
    loss = jnp.sum(losses, axis=1, keepdims=True)
    bias_grad = jax.nn.sigmoid(logits) - target
    bias_grad_ref[...] = bias_grad
    copy_ref[...] = bias_grad
    by_head = jnp.where(mask, bias_grad, 0.0)
    high = by_head.astype(BF16)
    low = (by_head - high.astype(F32)).astype(BF16)
    both = jnp.concatenate([high, low], axis=0)
    back = lax.dot_general(both, weight_ref[...], (((1,), (1,)), ((), ())), preferred_element_type=F32)
    normed_grad = (back[:heads] + back[heads:]) * gain
    inner = jnp.sum(by_head * product, axis=1, keepdims=True) / full_width
    unit = pooled * inverse_rms
    grad_ref[:, :width] = (inverse_rms * (normed_grad - unit * inner)).astype(BF16)
    grad_ref[:, width:] = into_lanes([top_ref[:, :1], jnp.broadcast_to(loss, (heads, 1))], heads)
    normed_ref[...] = unit * gain


def head_weight_grad_kernel(attributes, normed_ref, bias_grad_ref, out_ref):
    heads = normed_ref.shape[0]
    columns = out_ref.shape[1]
    parts = jnp.concatenate(pieces(normed_ref[...]), axis=0)
    row = lax.broadcasted_iota(jnp.int32, (3 * heads, columns), 0) % heads
    column = pl.program_id(0) * columns + lax.broadcasted_iota(jnp.int32, (3 * heads, columns), 1)
    ones = jnp.where(column // attributes == row, 1.0, 0.0).astype(BF16)
    normed = lax.dot_general(parts, ones, (((0,), (0,)), ((), ())), preferred_element_type=F32)
    out_ref[...] = normed * bias_grad_ref[...]


def head_weight_grad(normed, bias_grad):
    rows, width = normed.shape
    columns = bias_grad.shape[1]
    block = columns // 4
    return pl.pallas_call(
        functools.partial(head_weight_grad_kernel, columns // rows),
        out_shape=jax.ShapeDtypeStruct((width, columns), F32),
        grid=(columns // block,),
        in_specs=[
            pl.BlockSpec((rows, width), lambda i: (0, 0)),
            pl.BlockSpec((1, block), lambda i: (0, i)),
        ],
        out_specs=pl.BlockSpec((width, block), lambda i: (0, i)),
        compiler_params=pltpu.CompilerParams(vmem_limit_bytes=16 * MIB),
        name="head_weight_grad",
    )(normed, bias_grad)


def shards(tokens, doc_length, queries, norm_gain, head_weight, head_bias, labels):
    contexts, classes = lax.axis_size("ctx"), lax.axis_size("cls")
    token_count = tokens.shape[0]
    rows, width = queries.shape
    full_width = width * contexts
    heads = rows * classes
    half = heads // 2
    columns = labels.shape[0]
    blocks = contexts // 2
    pair = [((blocks, half, width), F32), ((blocks, half, width + LANES), BF16)]
    product = ((heads, token_count), F32)
    cost = pl.CostEstimate(flops=256 * token_count * full_width, bytes_accessed=0, transcendentals=0)

    def project_half(parts):
        return call(functools.partial(project_kernel, len(parts)), [product], "project", [*parts, held_a], cost=cost)[0]

    held_a, held_b, queries_here, gain = load(width, tokens, queries, norm_gain[None, :])
    first, second = gather(queries, queries_here)
    part = project_half(first)
    keep_b, send_b, own_peak, weights, left = call(
        functools.partial(pool_kernel, classes),
        [*pair, ((heads, LANES), F32), product, ((heads, token_count), BF16)],
        "pool",
        [doc_length, *second, part, held_b],
        smem_args=(0,),
        cost=cost,
    )
    half_a = call(pool_rest_kernel, pair, "pool_rest", [left, own_peak, held_a], cost=cost)
    parts = scatter_sum([half_a, (keep_b, send_b)], own_peak)
    sums, pooled, top = call(
        head_sums_kernel,
        [((2, columns), F32), ((rows, width), F32), ((rows, LANES), F32)],
        "head_sums",
        [*parts, gain, head_weight],
    )
    far_sums = [swap(sums, *step) for step in far_steps()[::-1]]
    (sums,) = call(tree_sum_kernel, [((2, columns), F32)], "tree_sum", [sums, *far_sums])
    bias_grad, bias_grad_here, pooled_grad, normed = call(
        functools.partial(head_grads_kernel, full_width),
        [((1, columns), F32), ((1, columns), F32), ((rows, width + LANES), BF16), ((rows, width), F32)],
        "head_grads",
        [sums, swap(sums, 1, 0), pooled, top, gain, head_weight, head_bias[None, :], labels[None, :]],
    )
    head_grad = head_weight_grad(normed, bias_grad_here)
    first, second = gather(pooled_grad)
    part = project_half(first)
    pair = [((blocks, half, width), F32), ((blocks, half, width), BF16)]
    keep_b, send_b, left, loss = call(
        functools.partial(grad_kernel, 1.0 / (columns * classes), classes),
        [*pair, ((heads, token_count), BF16), ((1, 1), F32)],
        "grad",
        [*second, part, held_b, weights, own_peak],
        cost=cost,
    )
    half_a = call(grad_rest_kernel, pair, "grad_rest", [left, held_a], cost=cost)
    parts = scatter_sum([half_a, (keep_b, send_b)], None)
    (query_grad,) = call(far_sum_kernel, [((rows, width), F32)], "far_sum", parts)
    return (loss.reshape(()), query_grad, head_grad, bias_grad.reshape(-1))


def solution(mesh):
    return jax.shard_map(
        shards,
        mesh=mesh,
        in_specs=(
            P(("ctx", "cls"), None),
            P(),
            P("cls", "ctx"),
            P("ctx"),
            P("ctx", "cls"),
            P("cls"),
            P("cls"),
        ),
        out_specs=(P(), P("cls", "ctx"), P("ctx", "cls"), P("cls")),
        check_vma=False,
    )
```

```python
import functools

import jax
import jax.numpy as jnp
from jax import lax
from jax.experimental import pallas as pl
from jax.experimental.pallas import tpu as pltpu
from jax.sharding import PartitionSpec as P

F32 = jnp.float32
BF16 = jnp.bfloat16
LANES = 128
MASKED = -1e30
MIB = 1024 * 1024


def swap(x, ctx_bits, cls_bits):
    contexts, classes = lax.axis_size("ctx"), lax.axis_size("cls")
    pairs = [
        (c * classes + k, (c ^ ctx_bits) * classes + (k ^ cls_bits)) for c in range(contexts) for k in range(classes)
    ]
    return lax.ppermute(x, ("ctx", "cls"), pairs)


def far_steps():
    return [(2 * j, 0) for j in reversed(range(1, lax.axis_size("ctx") // 2))]


def near_steps():
    steps = [(i, 2 * k) for i in range(2) for k in range(lax.axis_size("cls") // 2) if i or k]
    return sorted(steps, key=lambda step: (not (step[0] and step[1]), not step[0]))


def call(kernel, outs, name, args, smem_args=(), aliases=None, limit=16, cost=None):
    def spec(i):
        if i in smem_args:
            return pl.BlockSpec(memory_space=pltpu.SMEM)
        return pl.BlockSpec(memory_space=pltpu.VMEM)

    run = pl.pallas_call(
        kernel,
        out_shape=[jax.ShapeDtypeStruct(s, d) for s, d in outs],
        in_specs=[spec(i) for i in range(len(args))],
        out_specs=[pl.BlockSpec(memory_space=pltpu.VMEM)] * len(outs),
        input_output_aliases=aliases or {},
        compiler_params=pltpu.CompilerParams(vmem_limit_bytes=limit * MIB),
        cost_estimate=cost,
        name=name,
    )
    return list(run(*args))


def stack_kernel(*refs):
    out_ref = refs[-1]
    for at, ref in enumerate(refs[:-1]):
        out_ref[at] = ref[...].reshape(out_ref.shape[1:])


def gather(block, local=None):
    far = [swap(block, *step) for step in far_steps()[::-1]]
    rows, width = block.shape
    (held,) = call(
        stack_kernel, [((len(far) + 1, rows, width), block.dtype)], "stack", [block if local is None else local, *far]
    )
    parts = {step: swap(held, *step) for step in near_steps()[::-1]}
    parts[0, 0] = held
    other = {step: swap(part, 0, 1) for step, part in parts.items()}
    steps = sorted(parts)
    return [[group[step] for group in (parts, other) for step in steps if step[0] == i] for i in range(2)]


def pieces(x):
    high = x.astype(BF16)
    rest = x - high.astype(F32)
    middle = rest.astype(BF16)
    return high, middle, (rest - middle.astype(F32)).astype(BF16)


def into_lanes(columns, rows):
    lane = lax.broadcasted_iota(jnp.int32, (rows, LANES), 1)
    out = jnp.zeros((rows, LANES), F32)
    for i, column in enumerate(columns):
        for j, piece in enumerate(pieces(column)):
            out = jnp.where(lane == 3 * i + j, piece.astype(F32), out)
    return out.astype(BF16)


def from_lanes(block, width, i):
    at = width + 3 * i
    block = block.astype(F32)
    return block[:, at : at + 1] + (block[:, at + 1 : at + 2] + block[:, at + 2 : at + 3])


def load_kernel(tokens_ref, *refs):
    count = (len(refs) - 3) // 2
    others, halves, copies_of, sems = refs[:count], refs[count : count + 2], refs[count + 2 : -1], refs[-1]
    blocks, _, width = halves[0].shape
    copies = [pltpu.make_async_copy(src, dst, sems.at[i]) for i, (src, dst) in enumerate(zip(others, copies_of))]
    for i in range(2):
        for j in range(blocks):
            start = pl.multiple_of((lax.axis_index("ctx") ^ i ^ (2 * j)) * width, LANES)
            sem = sems.at[count + i * blocks + j]
            copies.append(pltpu.make_async_copy(tokens_ref.at[:, pl.ds(start, width)], halves[i].at[j], sem))
    for copy in copies:
        copy.start()
    for copy in copies:
        copy.wait()


def load(width, tokens, *others):
    rows, full_width = tokens.shape
    blocks = full_width // width // 2
    outs = [pltpu.VMEM((blocks, rows, width), tokens.dtype)] * 2 + [pltpu.VMEM(x.shape, x.dtype) for x in others]
    run = pl.pallas_call(
        load_kernel,
        out_shape=outs,
        in_specs=[pl.BlockSpec(memory_space=pltpu.HBM)] * (1 + len(others)),
        out_specs=[pl.BlockSpec(memory_space=pltpu.VMEM)] * len(outs),
        scratch_shapes=[pltpu.SemaphoreType.DMA((2 * blocks + len(others),))],
        compiler_params=pltpu.CompilerParams(vmem_limit_bytes=16 * MIB),
        name="load",
    )
    return run(*[pltpu.with_memory_space_constraint(x, pltpu.HBM) for x in (tokens, *others)])


def project(parts, held_ref):
    blocks, _, width = held_ref.shape
    total = None
    for j in range(blocks):
        left = jnp.concatenate([ref[j] for ref in parts], axis=0)[:, :width]
        part = lax.dot_general(left, held_ref[j], (((1,), (1,)), ((), ())), preferred_element_type=F32)
        total = part if total is None else total + part
    return total


def spread(left, held_ref, keep_ref, send_ref, extra):
    blocks, half, width = keep_ref.shape
    for j in range(blocks):
        part = jnp.dot(left, held_ref[j], preferred_element_type=F32)
        keep_ref[j] = part[:half]
        send_ref[j, :, :width] = part[half:].astype(BF16)
        if extra is not None:
            send_ref[j, :, width:] = extra


def project_kernel(count, *refs):
    refs[-1][...] = project(refs[:count], refs[count])


def peak_lanes(peak, half):
    return into_lanes([peak[half:, :1]], half)


def pool_kernel(count, length_ref, *refs):
    parts, refs = refs[:count], refs[count:]
    part_ref, held_ref, keep_ref, send_ref, peak_ref, w_ref, left_ref = refs
    scores = part_ref[...] + project(parts, held_ref)
    shard = lax.axis_index("ctx") * lax.axis_size("cls") + lax.axis_index("cls")
    valid = lax.broadcasted_iota(jnp.int32, scores.shape, 1) < length_ref[0] - shard * scores.shape[1]
    peak = jnp.max(jnp.where(valid, scores, MASKED), axis=1, keepdims=True)
    weights = jnp.where(valid, jnp.exp(scores - peak), 0.0)
    left = weights.astype(BF16)
    w_ref[...] = weights
    left_ref[...] = left
    peak_ref[...] = jnp.broadcast_to(peak, peak_ref.shape)
    spread(left, held_ref, keep_ref, send_ref, peak_lanes(peak, keep_ref.shape[1]))


def pool_rest_kernel(left_ref, peak_ref, held_ref, keep_ref, send_ref):
    spread(left_ref[...], held_ref, keep_ref, send_ref, peak_lanes(peak_ref[...], keep_ref.shape[1]))


def grad_kernel(scale, count, *refs):
    parts, refs = refs[:count], refs[count:]
    part_ref, held_ref, w_ref, peak_ref, keep_ref, send_ref, left_ref, loss_ref = refs
    width = held_ref.shape[2]
    projected = part_ref[...] + project(parts, held_ref)
    blocks = [ref[0] for ref in parts]
    top = jnp.concatenate([from_lanes(block, width, 0) for block in blocks], axis=0)
    weights = w_ref[...] * jnp.exp(peak_ref[:, :1] - top)
    left = (weights * projected).astype(BF16)
    left_ref[...] = left
    spread(left, held_ref, keep_ref, send_ref, None)
    loss_ref[...] = tree_sum([from_lanes(block, width, 1)[:1] for block in blocks]) * scale


def grad_rest_kernel(left_ref, held_ref, keep_ref, send_ref):
    spread(left_ref[...], held_ref, keep_ref, send_ref, None)


def rescaling(peak, received, width):
    if peak is None:
        return None, None
    others = [from_lanes(block, width, 0) for block in received]
    top = peak
    for other in others:
        top = jnp.maximum(top, other)
    return top, [jnp.exp(p - top) for p in [peak, *others]]


def total_of(keep, received, factors):
    total = keep if factors is None else keep * factors[0]
    for i, block in enumerate(received):
        block = block[:, : keep.shape[1]].astype(F32)
        total = total + (block if factors is None else block * factors[i + 1])
    return total


def put(ref, j, total, lanes):
    width = total.shape[1]
    ref[j, :, :width] = total.astype(BF16)
    if lanes is not None:
        ref[j, :, width:] = lanes


def core_kernel(peaks, first, *refs):
    keep_ref, recv_ref, *refs = refs
    peak = refs.pop(0)[: keep_ref.shape[1], :1] if peaks else None
    refs = refs if first else refs[1:-1]
    top_ref = refs.pop() if peaks and first else None
    width = keep_ref.shape[2]
    rows = refs[0].shape[1]
    top, factors = rescaling(peak, [recv_ref[0]], width)
    lanes = into_lanes([top], top.shape[0]) if peaks else None
    for j in range(keep_ref.shape[0]):
        total = total_of(keep_ref[j], [recv_ref[j]], factors)
        for k, ref in enumerate(refs):
            at = slice(k * rows, (k + 1) * rows)
            if first and k == 0:
                ref[j] = total[at]
            else:
                put(ref, j, total[at], lanes[at] if peaks else None)
    if peaks and first:
        top_ref[...] = jnp.broadcast_to(top[:rows], top_ref.shape)


def near_sum_kernel(peaks, count, steps, *refs):
    keep_ref, *refs = refs
    received, refs = refs[:count], refs[count:]
    peak = refs.pop(0)[:, :1] if peaks else None
    top_ref = refs.pop() if peaks else None
    top, factors = rescaling(peak, [ref[0] for ref in received], keep_ref.shape[2])
    lanes = into_lanes([top], top.shape[0]) if peaks else None
    for p in range(keep_ref.shape[0]):
        total = total_of(keep_ref[p], [ref[p] for ref in received], factors)
        if p == 0:
            refs[0][0] = total
        else:
            put(refs[steps.index((2 * p, 0)) + 1], 0, total, lanes)
    if peaks:
        top_ref[...] = jnp.broadcast_to(top, top_ref.shape)


def scatter_sum(halves, peak):
    peaks = peak is not None
    near, far = near_steps(), far_steps()
    across = (len(near) + 1) // 2
    blocks, half, width = halves[0][0].shape
    lanes = halves[0][1].shape[2]
    rows = half // across
    top_out = [((rows, LANES), F32)] if peaks else []
    part = ((blocks, rows, lanes), BF16)
    (keep_a, send_a), (keep_b, send_b) = halves
    args = [keep_b, swap(send_b, 0, 1)] + ([peak] if peaks else []) + [send_a]
    outs = [part] * across + [((blocks, half, lanes), BF16)]
    *parts_b, send_a = call(
        functools.partial(core_kernel, peaks, False), outs, "core_sum", args, aliases={len(args) - 1: across}
    )
    args = [keep_a, swap(send_a, 0, 1)] + ([peak] if peaks else [])
    outs = [((blocks, rows, width), F32)] + [part] * (across - 1) + top_out
    out = call(functools.partial(core_kernel, peaks, True), outs, "core_sum", args)
    parts = {(i, 2 * k): x for i, group in enumerate((out, parts_b)) for k, x in enumerate(group[:across])}
    received = [swap(parts[step], *step) for step in near]
    outs = [((1, rows, width), F32)] + [((1, rows, lanes), BF16)] * len(far) + top_out
    args = [parts[0, 0], *received] + (out[-1:] if peaks else [])
    out = call(functools.partial(near_sum_kernel, peaks, len(received), far), outs, "near_sum", args)
    received = [swap(x, *step) for x, step in zip(out[1:], far)]
    return [out[0], *received] + (out[-1:] if peaks else [])


def far_sum_kernel(*refs):
    keep_ref, *received, out_ref = refs
    out_ref[...] = total_of(keep_ref[0], [ref[0] for ref in received], None)


def head_mask(shape, attributes):
    row = lax.broadcasted_iota(jnp.int32, shape, 0)
    column = lax.broadcasted_iota(jnp.int32, shape, 1)
    return column // attributes == row


def head_sums_kernel(*refs):
    keep_ref, *received, peak_ref, gain_ref, weight_ref, sums_ref, pooled_ref, top_ref = refs
    received = [ref[0] for ref in received]
    top, factors = rescaling(peak_ref[:, :1], received, keep_ref.shape[2])
    pooled = total_of(keep_ref[0], received, factors)
    pooled_ref[...] = pooled
    top_ref[...] = jnp.broadcast_to(top, top_ref.shape)
    scaled_b = (pooled * gain_ref[...]).astype(BF16)
    product = jnp.dot(scaled_b, weight_ref[...], preferred_element_type=F32)
    mask = head_mask(product.shape, product.shape[1] // product.shape[0])
    squares = jnp.sum(pooled * pooled, axis=1, keepdims=True)
    product_flat = jnp.sum(jnp.where(mask, product, 0.0), axis=0, keepdims=True)
    squares_flat = jnp.sum(jnp.where(mask, squares, 0.0), axis=0, keepdims=True)
    sums_ref[0:1, :] = product_flat
    sums_ref[1:2, :] = squares_flat


def tree_sum(level):
    while len(level) > 1:
        level = [a + b for a, b in zip(level[::2], level[1::2])]
    return level[0]


def tree_sum_kernel(*refs):
    refs[-1][...] = tree_sum([ref[...] for ref in refs[:-1]])


def head_grads_kernel(full_width, sums_ref, other_sums_ref, *refs):
    pooled_ref, top_ref, gain_ref, weight_ref, bias_ref, label_ref, *refs = refs
    bias_grad_ref, copy_ref, grad_ref, normed_ref = refs
    pooled, gain = pooled_ref[...], gain_ref[...]
    heads, width = pooled.shape
    columns = bias_ref.shape[1]
    sums = sums_ref[...] + other_sums_ref[...]
    mask = head_mask((heads, columns), columns // heads)
    inverse_flat = lax.rsqrt(sums[1:2] / full_width + 1e-05)
    inverse_rms = jnp.max(jnp.where(mask, inverse_flat, 0.0), axis=1, keepdims=True)
    product = inverse_flat * sums[0:1]
    logits = product + bias_ref[...]
    target = label_ref[...].astype(F32)
    losses = jnp.maximum(logits, 0.0) + jnp.log1p(jnp.exp(-jnp.abs(logits))) - target * logits
    loss = jnp.sum(losses, axis=1, keepdims=True)
    bias_grad = jax.nn.sigmoid(logits) - target
    bias_grad_ref[...] = bias_grad
    copy_ref[...] = bias_grad
    by_head = jnp.where(mask, bias_grad, 0.0)
    high = by_head.astype(BF16)
    low = (by_head - high.astype(F32)).astype(BF16)
    both = jnp.concatenate([high, low], axis=0)
    back = lax.dot_general(both, weight_ref[...], (((1,), (1,)), ((), ())), preferred_element_type=F32)
    normed_grad = (back[:heads] + back[heads:]) * gain
    inner = jnp.sum(by_head * product, axis=1, keepdims=True) / full_width
    unit = pooled * inverse_rms
    grad_ref[:, :width] = (inverse_rms * (normed_grad - unit * inner)).astype(BF16)
    grad_ref[:, width:] = into_lanes([top_ref[:, :1], jnp.broadcast_to(loss, (heads, 1))], heads)
    normed_ref[...] = unit * gain


def head_weight_grad_kernel(attributes, normed_ref, bias_grad_ref, out_ref, parts_ref):
    heads = normed_ref.shape[0]
    columns = out_ref.shape[1]

    @pl.when(pl.program_id(0) == 0)
    def _():
        parts_ref[...] = jnp.concatenate([x.astype(F32) for x in pieces(normed_ref[...])], axis=0).T.astype(BF16)

    row = lax.broadcasted_iota(jnp.int32, (3 * heads, columns), 0) % heads
    column = pl.program_id(0) * columns + lax.broadcasted_iota(jnp.int32, (3 * heads, columns), 1)
    ones = jnp.where(column // attributes == row, 1.0, 0.0).astype(BF16)
    normed = jnp.dot(parts_ref[...], ones, preferred_element_type=F32)
    out_ref[...] = normed * bias_grad_ref[...]


def head_weight_grad(normed, bias_grad):
    rows, width = normed.shape
    columns = bias_grad.shape[1]
    block = columns // 4
    return pl.pallas_call(
        functools.partial(head_weight_grad_kernel, columns // rows),
        out_shape=jax.ShapeDtypeStruct((width, columns), F32),
        grid=(columns // block,),
        in_specs=[
            pl.BlockSpec((rows, width), lambda i: (0, 0)),
            pl.BlockSpec((1, block), lambda i: (0, i)),
        ],
        out_specs=pl.BlockSpec((width, block), lambda i: (0, i)),
        scratch_shapes=[pltpu.VMEM((width, 3 * rows), BF16)],
        compiler_params=pltpu.CompilerParams(vmem_limit_bytes=16 * MIB),
        name="head_weight_grad",
    )(normed, bias_grad)


def shards(tokens, doc_length, queries, norm_gain, head_weight, head_bias, labels):
    contexts, classes = lax.axis_size("ctx"), lax.axis_size("cls")
    token_count = tokens.shape[0]
    rows, width = queries.shape
    full_width = width * contexts
    heads = rows * classes
    half = heads // 2
    columns = labels.shape[0]
    blocks = contexts // 2
    pair = [((blocks, half, width), F32), ((blocks, half, width + LANES), BF16)]
    product = ((heads, token_count), F32)
    cost = pl.CostEstimate(flops=256 * token_count * full_width, bytes_accessed=0, transcendentals=0)

    def project_half(parts):
        return call(functools.partial(project_kernel, len(parts)), [product], "project", [*parts, held_a], cost=cost)[0]

    held_a, held_b, queries_here, gain = load(width, tokens, queries, norm_gain[None, :])
    first, second = gather(queries, queries_here)
    part = project_half(first)
    keep_b, send_b, own_peak, weights, left = call(
        functools.partial(pool_kernel, classes),
        [*pair, ((heads, LANES), F32), product, ((heads, token_count), BF16)],
        "pool",
        [doc_length, *second, part, held_b],
        smem_args=(0,),
        cost=cost,
    )
    half_a = call(pool_rest_kernel, pair, "pool_rest", [left, own_peak, held_a], cost=cost)
    parts = scatter_sum([half_a, (keep_b, send_b)], own_peak)
    sums, pooled, top = call(
        head_sums_kernel,
        [((2, columns), F32), ((rows, width), F32), ((rows, LANES), F32)],
        "head_sums",
        [*parts, gain, head_weight],
    )
    far_sums = [swap(sums, *step) for step in far_steps()[::-1]]
    (sums,) = call(tree_sum_kernel, [((2, columns), F32)], "tree_sum", [sums, *far_sums])
    bias_grad, bias_grad_here, pooled_grad, normed = call(
        functools.partial(head_grads_kernel, full_width),
        [((1, columns), F32), ((1, columns), F32), ((rows, width + LANES), BF16), ((rows, width), F32)],
        "head_grads",
        [sums, swap(sums, 1, 0), pooled, top, gain, head_weight, head_bias[None, :], labels[None, :]],
    )
    head_grad = head_weight_grad(normed, bias_grad_here)
    first, second = gather(pooled_grad)
    part = project_half(first)
    pair = [((blocks, half, width), F32), ((blocks, half, width), BF16)]
    keep_b, send_b, left, loss = call(
        functools.partial(grad_kernel, 1.0 / (columns * classes), classes),
        [*pair, ((heads, token_count), BF16), ((1, 1), F32)],
        "grad",
        [*second, part, held_b, weights, own_peak],
        cost=cost,
    )
    half_a = call(grad_rest_kernel, pair, "grad_rest", [left, held_a], cost=cost)
    parts = scatter_sum([half_a, (keep_b, send_b)], None)
    (query_grad,) = call(far_sum_kernel, [((rows, width), F32)], "far_sum", parts)
    return (loss.reshape(()), query_grad, head_grad, bias_grad.reshape(-1))


def solution(mesh):
    return jax.shard_map(
        shards,
        mesh=mesh,
        in_specs=(
            P(("ctx", "cls"), None),
            P(),
            P("cls", "ctx"),
            P("ctx"),
            P("ctx", "cls"),
            P("cls"),
            P("cls"),
        ),
        out_specs=(P(), P("cls", "ctx"), P("ctx", "cls"), P("cls")),
        check_vma=False,
    )
```
